128 devices in a mesh: batch: 4 (over z), seq: 32 (over y, x, core).
Axes of the slice: x: 4, y: 4, z: 4, core: 2. Of those that a mesh axis runs over, the one named last changes fastest.
Arguments:
- tokens: bfloat16 [2, 4, 4096, 576], P(None, 'batch', 'seq'), may hold values from -6 to 6
- doc_lengths: int32 [2, 4, 3], P(None, 'batch'), may hold values from 1 to 4094, as said below
- first_gain: bfloat16 [576], P('seq'), may hold values from 0.5 to 1.5
- query_weight: bfloat16 [576, 576], P('batch', 'seq'), may hold values from -0.25 to 0.25
- key_matrix: bfloat16 [576, 192], P('batch', 'seq'), may hold values from -0.25 to 0.25
- value_matrix: bfloat16 [576, 192], P('batch', 'seq'), may hold values from -0.25 to 0.25
- output_weight: bfloat16 [576, 576], P('batch', 'seq'), may hold values from -4 to 4
- second_gain: bfloat16 [576], P('seq'), may hold values from 0.5 to 1.5
- gate_weight: bfloat16 [576, 1536], P('batch', 'seq'), may hold values from -0.25 to 0.25
- up_weight: bfloat16 [576, 1536], P('batch', 'seq'), may hold values from -0.25 to 0.25
- down_weight: bfloat16 [1536, 576], P('batch', 'seq'), may hold values from -0.15625 to 0.15625
- cotangent: bfloat16 [2, 4, 4096, 576], P(None, 'batch', 'seq'), may hold values from -6 to 6
Outputs:
- mixed: bfloat16 [2, 4, 4096, 576], P(None, 'batch', 'seq')
- tokens_grad: bfloat16 [2, 4, 4096, 576], P(None, 'batch', 'seq')
- first_gain_grad: float32 [576], P('seq')
- query_grad: float32 [576, 576], P('batch', 'seq')
- key_grad: float32 [576, 192], P('batch', 'seq')
- value_grad: float32 [576, 192], P('batch', 'seq')
- output_grad: float32 [576, 576], P('batch', 'seq')
- second_gain_grad: float32 [576], P('seq')
- gate_grad: float32 [576, 1536], P('batch', 'seq')
- up_grad: float32 [576, 1536], P('batch', 'seq')
- down_grad: float32 [1536, 576], P('batch', 'seq')
The draws below stay inside these ranges and needn't reach their ends.
Inputs may be any that keep to these rules, and one draw needn't show every extreme that they name: `doc_lengths`: in each row the 3 lengths sum to 4096; all but one of them, whose place in the row varies, are under 128 // 2. Some row holds the longest document possible.
All inputs are finite; a program needn't handle non-finite values.
Results may differ from the reference program's by a relative error of at most 0.028.
Values may be sent and summed in bfloat16 or wider, within the bound.
A program may use at most 128 MiB of HBM per device.

```python
import math
import jax
import jax.numpy as jnp
from jax import lax

MODEL_WIDTH = 576
QUERY_HEADS = 9
KEY_VALUE_HEADS = 3
HEAD_SIZE = 64
FF = 1536
PIECE = 128
MICRO = 2
NDOC = 3
LEN = 4096
SEQS = 4


def draw_doc_lengths(key, part):
    key = jax.random.fold_in(key, 7)
    short_key, place_key = jax.random.split(key)
    row_count = MICRO * SEQS
    shorts = jax.random.randint(short_key, (row_count, NDOC - 1), 1, PIECE // 2, dtype=jnp.int32)
    row_ids = jnp.arange(row_count, dtype=jnp.int32)[:, None]
    shorts = jnp.where(row_ids == 0, 1, shorts).astype(jnp.int32)
    longest = (LEN - jnp.sum(shorts, axis=1)).astype(jnp.int32)
    place = jax.random.randint(place_key, (row_count, 1), 0, NDOC, dtype=jnp.int32)
    slots = jnp.arange(NDOC, dtype=jnp.int32)[None, :]
    pick = jnp.clip(slots - (slots > place).astype(jnp.int32), 0, NDOC - 2)
    chosen = jnp.take_along_axis(shorts, pick, axis=1)
    result = jnp.where(slots == place, longest[:, None], chosen)
    return result.astype(jnp.int32).reshape(MICRO, SEQS, NDOC)


def block_levels(own_key, shape, pieces, least, largest):
    loudness, own = 1.0, jax.random.fold_in(own_key, 6)
    for position, parts in pieces:
        draws = jnp.exp(jax.random.uniform(jax.random.fold_in(own, position), (parts,), jnp.float32, least / len(pieces), largest / len(pieces)))
        loudness = loudness * jnp.repeat(draws, shape[position] // parts).reshape([-1 if axis == position else 1 for axis in range(len(shape))])
    return loudness


def gaussian(own_key, dims, deviation, reach, shards=(), held_as=jnp.bfloat16):
    array = deviation * jax.random.normal(own_key, dims, jnp.float32)
    if shards:
        array = array * block_levels(own_key, dims, shards, -0.22, 0.18)
    return jnp.clip(array, -reach, reach).astype(held_as)


def setup_inputs(seed: int = 0) -> dict:
    arg_keys = jax.random.split(jax.random.key(seed), 13)
    return {
        "tokens": gaussian(arg_keys[0], (MICRO, SEQS, LEN, MODEL_WIDTH), 1.0, 6.0, ((1, 4), (2, 32))),
        "doc_lengths": draw_doc_lengths(jax.random.fold_in(arg_keys[12], 71), 0),
        "first_gain": jnp.clip(1.0 + 0.1 * jax.random.normal(arg_keys[2], (MODEL_WIDTH,), jnp.float32), 0.5, 1.5).astype(jnp.bfloat16),
        "query_weight": gaussian(arg_keys[3], (MODEL_WIDTH, QUERY_HEADS * HEAD_SIZE), MODEL_WIDTH ** -0.5, 0.25, ((0, 4), (1, 32))),
        "key_matrix": gaussian(arg_keys[4], (MODEL_WIDTH, KEY_VALUE_HEADS * HEAD_SIZE), MODEL_WIDTH ** -0.5, 0.25, ((0, 4), (1, 32))),
        "value_matrix": gaussian(arg_keys[5], (MODEL_WIDTH, KEY_VALUE_HEADS * HEAD_SIZE), MODEL_WIDTH ** -0.5, 0.25, ((0, 4), (1, 32))),
        "output_weight": gaussian(arg_keys[6], (QUERY_HEADS * HEAD_SIZE, MODEL_WIDTH), (max(1, QUERY_HEADS * HEAD_SIZE * 16 // LEN)) ** -0.5, 4.0, ((0, 4), (1, 32))),
        "second_gain": jnp.clip(1.0 + 0.1 * jax.random.normal(arg_keys[7], (MODEL_WIDTH,), jnp.float32), 0.5, 1.5).astype(jnp.bfloat16),
        "gate_weight": gaussian(arg_keys[8], (MODEL_WIDTH, FF), MODEL_WIDTH ** -0.5, 0.25, ((0, 4), (1, 32))),
        "up_weight": gaussian(arg_keys[9], (MODEL_WIDTH, FF), MODEL_WIDTH ** -0.5, 0.25, ((0, 4), (1, 32))),
        "down_weight": gaussian(arg_keys[10], (FF, MODEL_WIDTH), FF ** -0.5, 0.15625, ((0, 4), (1, 32))),
        "cotangent": gaussian(arg_keys[11], (MICRO, SEQS, LEN, MODEL_WIDTH), 1.0, 6.0, ((1, 4), (2, 32))),
    }


EPS = 1e-05
THETA = 100000.0
MASKED = -1e+30

@jax.custom_vjp
def reduced_precision(v):
    return lax.optimization_barrier(v.astype(jnp.bfloat16)).astype(jnp.float32)

@jax.custom_vjp
def reduced_backward(v):
    return v

def low_keep(v):
    return (reduced_precision(v), None)

def low_pass(kept, grad):
    return (grad,)

def back_keep(v):
    return (v, None)

def back_low(kept, grad):
    return (reduced_precision(grad),)
reduced_precision.defvjp(low_keep, low_pass)
reduced_backward.defvjp(back_keep, back_low)

def matrix_product(left, right):
    return jnp.dot(left, right, precision=lax.Precision.HIGHEST)

def norm(values, gain):
    return values * lax.rsqrt(lax.optimization_barrier(jnp.mean(values * values, axis=-1, keepdims=True)) + EPS) * gain

def doc_tables(lengths, total_count):
    ends = jnp.cumsum(lengths, axis=-1).astype(jnp.int32)
    starts = (ends - lengths).astype(jnp.int32)
    places = jnp.arange(total_count, dtype=jnp.int32)
    docs = lax.optimization_barrier(jnp.sum((places[:, None] >= ends[..., None, :]).astype(jnp.int32), axis=-1)).astype(jnp.int32)
    labels = jnp.arange(lengths.shape[-1], dtype=jnp.int32)
    first = lax.optimization_barrier(jnp.sum(jnp.where(docs[..., None] == labels, starts[..., None, :], 0), axis=-1)).astype(jnp.int32)
    return (docs, (places - first).astype(jnp.int32))

def rope_tables(positions, width):
    half = width // 2
    inverse_rates = THETA ** (-2.0 * jnp.arange(half, dtype=jnp.float32) / width)
    angles = positions.astype(jnp.float32)[..., None] * inverse_rates
    angles = jnp.concatenate([angles, angles], axis=-1)
    return (jnp.cos(angles), jnp.sin(angles))

def apply_rotation(values, cosine_table, sine_table):
    half = values.shape[-1] // 2
    turned = jnp.concatenate([-values[..., half:], values[..., :half]], axis=-1)
    return values * cosine_table[..., None, :] + turned * sine_table[..., None, :]

def attend(query_rows_local, keys, values, docs):
    total_count, heads_kv, query_group, width = query_rows_local.shape
    height = min(512, total_count)
    blocks = total_count // height
    scale = 1.0 / math.sqrt(width)
    places = jnp.arange(total_count, dtype=jnp.int32)

    def one_block(item):
        query_rows, offset = item
        query_pos = offset + jnp.arange(height, dtype=jnp.int32)
        query_docs = lax.dynamic_slice_in_dim(docs, offset, height)
        raw = reduced_backward(jnp.einsum('qcgd,kcd->cgqk', query_rows, keys, precision=lax.Precision.HIGHEST) * scale)
        allowed = (places[None, :] <= query_pos[:, None]) & (docs[None, :] == query_docs[:, None])
        scores = jnp.where(allowed, raw, MASKED)
        peak = lax.optimization_barrier(jnp.max(scores, axis=-1, keepdims=True))
        powers = jnp.exp(scores - peak)
        probs = powers / lax.optimization_barrier(jnp.sum(powers, axis=-1, keepdims=True))
        return jnp.einsum('cgqk,kcd->qcgd', reduced_precision(probs), values, precision=lax.Precision.HIGHEST)
    offsets = jnp.arange(blocks, dtype=jnp.int32) * height
    blocked = query_rows_local.reshape(blocks, height, heads_kv, query_group, width)
    result = lax.map(jax.checkpoint(one_block), (blocked, offsets))
    return result.reshape(total_count, heads_kv * query_group * width)

def layer(rows_in, lengths, params):
    first_gain, query_weight, key_matrix, value_matrix, output_weight, second_gain, gate_weight, up_weight, down_weight = params
    total_count = rows_in.shape[0]
    query_group = QUERY_HEADS // KEY_VALUE_HEADS
    docs, positions = doc_tables(lengths, total_count)
    cosine_table, sine_table = rope_tables(positions, HEAD_SIZE)
    hidden_first = reduced_precision(norm(rows_in, first_gain))
    query_projected = reduced_backward(matrix_product(hidden_first, query_weight)).reshape(total_count, QUERY_HEADS, HEAD_SIZE)
    key_projected = reduced_backward(matrix_product(hidden_first, key_matrix)).reshape(total_count, KEY_VALUE_HEADS, HEAD_SIZE)
    value_projected = reduced_backward(matrix_product(hidden_first, value_matrix)).reshape(total_count, KEY_VALUE_HEADS, HEAD_SIZE)
    query_rows_local = reduced_precision(apply_rotation(query_projected, cosine_table, sine_table)).reshape(total_count, KEY_VALUE_HEADS, query_group, HEAD_SIZE)
    keys = reduced_precision(apply_rotation(key_projected, cosine_table, sine_table))
    values = reduced_precision(value_projected)
    attended = reduced_precision(reduced_backward(attend(query_rows_local, keys, values, docs)))
    middle = rows_in + reduced_backward(matrix_product(attended, output_weight))
    second_hidden = reduced_precision(norm(middle, second_gain))
    gate = reduced_backward(matrix_product(second_hidden, gate_weight))
    up_part = reduced_backward(matrix_product(second_hidden, up_weight))
    product = reduced_precision(jax.nn.silu(gate) * up_part)
    return middle + matrix_product(product, down_weight)

def reference(tokens, doc_lengths, first_gain, query_weight, key_matrix, value_matrix, output_weight, second_gain, gate_weight, up_weight, down_weight, cotangent):
    params = (first_gain.astype(jnp.float32), query_weight.astype(jnp.float32), key_matrix.astype(jnp.float32), value_matrix.astype(jnp.float32), output_weight.astype(jnp.float32), second_gain.astype(jnp.float32), gate_weight.astype(jnp.float32), up_weight.astype(jnp.float32), down_weight.astype(jnp.float32))
    flat_rows = tokens.astype(jnp.float32).reshape(MICRO * SEQS, LEN, MODEL_WIDTH)
    flat_lengths = doc_lengths.reshape(MICRO * SEQS, NDOC)
    flat_cot = cotangent.astype(jnp.float32).reshape(MICRO * SEQS, LEN, MODEL_WIDTH)

    def one_row(carry, item):
        rows_in, lengths, cot_rows = item

        def forward(rows_arg, params_arg):
            return layer(rows_arg, lengths, params_arg)
        result, pullback = jax.vjp(forward, rows_in, params)
        grad_rows, grad_params = pullback(cot_rows)
        carry = jax.tree.map(jnp.add, carry, grad_params)
        return (carry, (result.astype(jnp.bfloat16), grad_rows.astype(jnp.bfloat16)))
    zero_filled = jax.tree.map(jnp.zeros_like, params)
    sums, (mixed, grads) = lax.scan(one_row, zero_filled, (flat_rows, flat_lengths, flat_cot))
    mixed = mixed.reshape(MICRO, SEQS, LEN, MODEL_WIDTH)
    grads = grads.reshape(MICRO, SEQS, LEN, MODEL_WIDTH)
    return (mixed, grads, sums[0], sums[1], sums[2], sums[3], sums[4], sums[5], sums[6], sums[7], sums[8])
```

```python
import numpy as np
import ml_dtypes
import jax
import jax.numpy as jnp
from jax import lax
from jax.experimental import pallas as pl
from jax.experimental.pallas import tpu as pltpu
from jax.sharding import PartitionSpec as P

D = 576
HEADS = 9
KV = 3
HD = 64
FF = 1536
PIECE = 128
T = 2 * PIECE
LANES = 3 * T
EPS = 1e-05
THETA = 100000.0
MASKED = -1e30
MESH = pl.DeviceIdType.MESH
F32 = jnp.float32
BF16 = jnp.bfloat16
VLIMIT = 58 * 1024 * 1024


def spread_matrix():
    m = np.zeros((960, 1024), np.float32)
    n = np.arange(576)
    m[n, 32 * (n // 18) + n % 18] = 1
    n = np.arange(192)
    m[576 + n, 32 * (n // 6) + 18 + n % 6] = 1
    m[768 + n, 32 * (n // 6) + 24 + n % 6] = 1
    return m.astype(ml_dtypes.bfloat16)


def gain_matrix():
    n = np.arange(576)
    fold = np.zeros((576, 576), np.float32)
    for b in range(4):
        fold[n, 144 * b + n % 18] = 1
    owner = (n[None, :] // 18 == np.arange(32)[:, None]).astype(np.float32)
    return fold.astype(ml_dtypes.bfloat16), owner


def nn(a, b):
    return lax.dot_general(a, b, (((1,), (0,)), ((), ())), preferred_element_type=F32)


def nt(a, b):
    return lax.dot_general(a, b, (((1,), (1,)), ((), ())), preferred_element_type=F32)


def tn(a, b):
    return lax.dot_general(a, b, (((0,), (0,)), ((), ())), preferred_element_type=F32)


def rcopy(src, dst, ss, rs, dev):
    return pltpu.make_async_remote_copy(
        src_ref=src, dst_ref=dst, send_sem=ss, recv_sem=rs, device_id=dev, device_id_type=MESH
    )


def place():
    b = lax.axis_index("batch")
    s = lax.axis_index("seq")
    c = lax.rem(s, 2)
    p = lax.div(s, 2)
    return b, s, c, p, lax.div(p, 4), lax.rem(p, 4)


def seq_of(y, x, c):
    return (y * 4 + x) * 2 + c


def hop(i, d):
    return lax.rem(i + d, 4)


def hail(devices):
    bar = pltpu.get_barrier_semaphore()
    for dev in devices:
        pl.semaphore_signal(bar, inc=1, device_id=dev, device_id_type=MESH)
    return bar


def grid_partners(b, s, c, y, x):
    found = [(b, seq_of(y, x, 1 - c))]
    for d in (1, 2, 3):
        found += [
            (hop(b, d), s),
            (b, seq_of(y, hop(x, d), c)),
            (b, seq_of(hop(y, d), x, c)),
        ]
    return found


W_ORDER = (0, 3, 1, 2)


class Ring:
    def __init__(self, dev, ss, rs):
        self.dev, self.ss, self.rs = dev, ss, rs

    def copy(self, n, src, dst):
        du, dv = {0: (1, 0), 1: (3, 0), 2: (1, 0), 3: (3, 0)}.get(n, (0, 1 if n // 4 in (1, 3) else 3))
        return rcopy(src, dst, self.ss.at[n], self.rs.at[n], self.dev(du, dv))


def gather_kernel(
    wq, wk, wv, wo, wg, wu, wd, gains, tokens, cot, tok_o, cot_o, g_o,
    raw_f, dwn_f, raw, dwn, za, zd, blk, zsem, lsem, rsem, cs, zz, zl,
):
    b, s, c, p, y, x = place()
    early = jnp.minimum(s, 31 - s)
    slot = lax.div(s, 16)
    bar = hail(grid_partners(b, s, c, y, x))
    for src in (p, 31 - p):
        @pl.when(src != s)
        def _():
            pl.semaphore_signal(bar, inc=1, device_id=(b, src), device_id_type=MESH)
    raw_f[...] = jnp.zeros_like(raw_f)
    dwn_f[...] = jnp.zeros_like(dwn_f)
    for at, ref in ((0, wq), (18, wk), (24, wv), (32, wo), (64, wg), (112, wu)):
        raw_f[at : at + ref.shape[0], :] = ref[...].astype(F32)
    raw_f[30:32, 0:18] = gains[...].astype(F32)
    dwn_f[0:18, :] = wd[...].astype(F32)
    raw[...] = raw_f[...].astype(BF16)
    dwn[...] = dwn_f[...].astype(BF16)
    own_target = jnp.where(2 * early == s, 1, 0) + jnp.where(2 * early + 1 == s, 1, 0)
    pl.semaphore_wait(bar, 12 - own_target)

    za[pl.ds(b, 1)] = raw[...][None]
    zd[pl.ds(b, 1)] = dwn[...][None]

    def zcopies(n, at, part):
        dev = (hop(b, 1 if n in (0, 2) else 3), s)
        found = []
        for k, (ref, rows) in enumerate(((za, 80), (zd, 16))):
            view = ref.at[at] if part is None else ref.at[at, pl.ds(rows * part, rows)]
            found.append(rcopy(view, view, zsem.at[0, k, n], zsem.at[1, k, n], dev))
        return found

    def start(copies):
        for cp in copies:
            cp.start()

    zsent = [zcopies(0, b, None), zcopies(1, b, None)]
    start(zsent[0] + zsent[1])

    for m in (0, 1):
        dst = 2 * early + m
        for k, (src_ref, dst_ref) in enumerate(((tokens, tok_o), (cot, cot_o))):
            @pl.when(dst != s)
            def _():
                rcopy(src_ref.at[m], dst_ref.at[slot], zz.at[0, k, m], zz.at[1, k, slot], (b, dst)).start()

            @pl.when(dst == s)
            def _():
                pltpu.make_async_copy(src_ref.at[m], dst_ref.at[slot], zl.at[k]).start()

    for n, way in ((0, 3), (1, 1)):
        for cp in zcopies(n, hop(b, way), None):
            cp.wait_recv()
        zsent.append(zcopies(2 + n, hop(b, way), n))
        start(zsent[-1])
    for n in (2, 3):
        for cp in zcopies(n, hop(b, 2), n - 2):
            cp.wait_recv()
    main = jnp.concatenate([za[i].astype(F32) for i in range(4)], axis=1).astype(BF16)
    down = jnp.concatenate([zd[i] for i in range(4)], axis=1)
    blk[0:160, :] = main
    blk[160:256, 512:576] = jnp.zeros((96, 64), BF16)
    for k in range(3):
        blk[160 + 32 * k : 192 + 32 * k, 0:512] = down[:, 512 * k : 512 * (k + 1)]

    lc = pltpu.make_async_copy(blk, g_o.at[y, x, c], lsem)
    lc.start()
    other = (b, seq_of(y, x, 1 - c))
    sent = []
    swaps = []
    rings = []
    for h in (0, 1):
        def spot(du, dv):
            return (hop(y, dv), hop(x, du)) if h == 0 else (hop(y, du), hop(x, dv))

        def dev(du, dv, spot=spot):
            return (b, seq_of(*spot(du, dv), c))

        def view(du, dv, part=None, spot=spot, h=h):
            rows = pl.ds(128 * h, 128) if part is None else pl.ds(128 * h + 64 * part, 64)
            return g_o.at[(*spot(du, dv), c, rows)]

        rings.append((Ring(dev, rsem.at[0, h], rsem.at[1, h]), view))

    def go(h, n, src, dst):
        cp = rings[h][0].copy(n, src, dst)
        cp.start()
        sent.append(cp)

    def swap(h, du, dv, src=None):
        ref = rings[h][1](du, dv)
        n = 4 * dv + du
        cp = rcopy(ref if src is None else src, ref, cs.at[0, h, n], cs.at[1, h, n], other)
        cp.start()
        swaps.append(cp)

    def arrive(h, n, du, dv, part=None):
        ref = rings[h][1](du, dv, part)
        rings[h][0].copy(n, ref, ref).wait_recv()

    def pass_on(h, n, du, dv, part=None):
        ref = rings[h][1](du, dv, part)
        go(h, n, ref, ref)

    for h in (0, 1):
        src = blk.at[pl.ds(128 * h, 128)]
        dst = rings[h][1](0, 0)
        for n in (0, 1, 4, 8):
            go(h, n, src, dst)
        swap(h, 0, 0, src)
    for h in (0, 1):
        for n, du in ((0, 3), (1, 1)):
            arrive(h, n, du, 0)
            pass_on(h, 2 + n, du, 0, n)
            pass_on(h, 4 + du, du, 0)
            pass_on(h, 8 + du, du, 0)
            swap(h, du, 0)

    def line(h, w):
        arrive(h, 4 + w, w, 3)
        pass_on(h, 12 + w, w, 3, 0)
        swap(h, w, 3)
        arrive(h, 8 + w, w, 1)
        pass_on(h, 16 + w, w, 1, 1)
        swap(h, w, 1)

    for h in (0, 1):
        line(h, 0)
    for h in (0, 1):
        arrive(h, 2, 2, 0, 0)
        arrive(h, 3, 2, 0, 1)
        pass_on(h, 6, 2, 0)
        pass_on(h, 10, 2, 0)
        swap(h, 2, 0)
    for w in (3, 1, 2):
        for h in (0, 1):
            line(h, w)
    for w in W_ORDER:
        for h in (0, 1):
            arrive(h, 12 + w, w, 2, 0)
            arrive(h, 16 + w, w, 2, 1)
            swap(h, w, 2)
    lc.wait()
    for cp in sent:
        cp.wait_send()
    for cp in swaps:
        cp.wait()
    for group in zsent:
        for cp in group:
            cp.wait_send()

    for m in (0, 1):
        dst = 2 * early + m
        for k, (src_ref, dst_ref) in enumerate(((tokens, tok_o), (cot, cot_o))):
            @pl.when(dst != s)
            def _():
                rcopy(src_ref.at[m], dst_ref.at[slot], zz.at[0, k, m], zz.at[1, k, slot], (b, dst)).wait_send()

            @pl.when(dst == s)
            def _():
                pltpu.make_async_copy(src_ref.at[m], dst_ref.at[slot], zl.at[k]).wait()
    for q, src in enumerate((p, 31 - p)):
        for k, (src_ref, dst_ref) in enumerate(((tokens, tok_o), (cot, cot_o))):
            @pl.when(src != s)
            def _():
                rcopy(src_ref.at[0], dst_ref.at[q], zz.at[0, k, 0], zz.at[1, k, q], (b, src)).wait_recv()


def gather_call(shards, tokens, cot):
    dma = pltpu.SemaphoreType.DMA
    any_ = pl.BlockSpec(memory_space=pl.ANY)
    vm = pl.BlockSpec(memory_space=pltpu.VMEM)
    return pl.pallas_call(
        gather_kernel,
        out_shape=(
            jax.ShapeDtypeStruct((2, D, PIECE), BF16),
            jax.ShapeDtypeStruct((2, D, PIECE), BF16),
            jax.ShapeDtypeStruct((4, 4, 2, 256, D), BF16),
        ),
        in_specs=[vm] * 8 + [any_, any_],
        out_specs=(any_, any_, any_),
        scratch_shapes=[
            pltpu.VMEM((160, 144), F32),
            pltpu.VMEM((32, 384), F32),
            pltpu.VMEM((160, 144), BF16),
            pltpu.VMEM((32, 384), BF16),
            pltpu.VMEM((4, 160, 144), BF16),
            pltpu.VMEM((4, 32, 384), BF16),
            pltpu.VMEM((256, D), BF16),
            dma((2, 2, 4)),
            dma(()),
            dma((2, 2, 20)),
            dma((2, 2, 16)),
            dma((2, 2, 2)),
            dma((2,)),
        ],
        compiler_params=pltpu.CompilerParams(
            collective_id=0, has_side_effects=True, vmem_limit_bytes=VLIMIT
        ),
        name="gather_weights",
    )(*shards, tokens, cot)


def token_rows(ref):
    return jnp.concatenate([ref[0].astype(F32).T, ref[1].astype(F32).T], axis=0)


def gain_row(rows, fold, owner):
    spread = nt(rows, fold[:, 0:128])
    return jnp.sum(spread * owner, axis=0, keepdims=True)


def pre_kernel(g, tok, cos, sin, spread, fold, owner, kv_o, qt_o, h1_o):
    wa = g[:, :, :]
    g1 = gain_row(wa[:, 30, 0:128], fold[...], owner[...])
    w = nn(spread[...], wa.reshape(1024, D)).astype(BF16)
    x = token_rows(tok)
    r1 = lax.rsqrt(jnp.sum(x * x, axis=-1, keepdims=True) * (1.0 / D) + EPS)
    h1 = (x * r1 * g1).astype(BF16)
    h1_o[...] = h1
    z = nt(w, h1)
    co, si = cos[...], sin[...]

    def rot(u):
        u1, u2 = u[0:32], u[32:64]
        return jnp.concatenate([u1 * co - u2 * si, u2 * co + u1 * si], axis=0)

    for h in range(HEADS):
        q = (rot(z[64 * h : 64 * h + 64]).astype(BF16).astype(F32) * 0.125).astype(BF16)
        kvh, gi = h // 3, h % 3
        for piece in range(2):
            lane = piece * 384 + gi * 128
            qt_o[kvh, 0:64, lane : lane + 128] = q[:, piece * 128 : piece * 128 + 128]
    for h in range(KV):
        qt_o[h, 64:128, :] = jnp.zeros((64, LANES), BF16)
        k = rot(z[576 + 64 * h : 640 + 64 * h])
        v = z[768 + 64 * h : 832 + 64 * h]
        kv_o[h] = jnp.concatenate([k, v], axis=0).T.astype(BF16)


def with_row(blocks, row, values):
    at = lax.broadcasted_iota(jnp.int32, (1, 32, 1), 1)
    return jnp.where(at == row, values[:, None, :], blocks)


def whole(shape):
    return pl.BlockSpec(shape, lambda i: (0,) * len(shape))


def pre_call(g, tok, cos, sin, spread, fold, owner):
    vm = pl.BlockSpec(memory_space=pltpu.VMEM)
    return pl.pallas_call(
        pre_kernel,
        out_shape=(
            jax.ShapeDtypeStruct((KV, T, 128), BF16),
            jax.ShapeDtypeStruct((KV, 128, LANES), BF16),
            jax.ShapeDtypeStruct((T, D), BF16),
        ),
        grid=(1,),
        in_specs=[whole((32, 32, D))] + [vm] * 6,
        out_specs=(vm, vm, vm),
        compiler_params=pltpu.CompilerParams(vmem_limit_bytes=VLIMIT),
        name="project_qkv",
    )(g, tok, cos, sin, spread, fold, owner)


def diagonal_mask(p, qpos, qstart):
    row = lax.broadcasted_iota(jnp.int32, (T, 1), 0)
    kpos = jnp.where(row < PIECE, p * PIECE + row, (31 - p) * PIECE + row - PIECE)
    return (kpos <= qpos) & (kpos >= qstart)


def first_mask(qstart):
    row = lax.broadcasted_iota(jnp.int32, (PIECE, 1), 0)
    return row >= qstart


def plane_ring(b, c, p, y, x, ss, rs):
    u, v = jnp.where(c == 0, x, y), jnp.where(c == 0, y, x)
    su, sv = 1 + 3 * c, 4 - 3 * c

    def index(du, dv):
        return lax.rem(u + du, 4) * su + lax.rem(v + dv, 4) * sv

    def dev(du, dv):
        return (b, 2 * index(du, dv) + c)

    bar = pltpu.get_barrier_semaphore()
    for du, dv in ((1, 0), (3, 0), (0, 1), (0, 3)):
        pl.semaphore_signal(bar, inc=1, device_id=dev(du, dv), device_id_type=MESH)
    pl.semaphore_wait(bar, 4)
    return Ring(dev, ss, rs), index


def pick(i, values):
    found = values[0]
    for k, value in enumerate(values[1:]):
        found = jnp.where(i == k + 1, value, found)
    return found


FORWARD = ((0, 0), (3, 0), (1, 0), (0, 3), (0, 1), (2, 0), (3, 3), (3, 1), (1, 3), (1, 1), (2, 3), (2, 1), (0, 2), (3, 2), (1, 2), (2, 2))
BACKWARD = ((0, 0), (2, 2), (1, 2), (3, 2), (0, 2), (2, 1), (2, 3), (1, 1), (1, 3), (3, 1), (3, 3), (0, 1), (0, 3), (2, 0), (1, 0), (3, 0))
HALVES = (pl.ds(0, PIECE), pl.ds(PIECE, PIECE))


def attend_kernel(kv, qt, qpos, qstart, kv_o, att_o, lse_o, m_s, l_s, acc, ss, rs):
    b, s, c, p, y, x = place()
    ring, index = plane_ring(b, c, p, y, x, ss, rs)

    def view(du, dv, part=None):
        at = index(du, dv)
        return kv_o.at[at] if part is None else kv_o.at[at, :, HALVES[part]]

    def send(n, du, dv, part=None):
        ref = view(du, dv, part)
        return ring.copy(n, kv if (du, dv) == (0, 0) else ref, ref)

    def arrive(n, du, dv, part=None):
        ref = view(du, dv, part)
        ring.copy(n, ref, ref).wait_recv()

    own = [send(n, 0, 0) for n in (0, 1, 4, 8)]
    for cp in own:
        cp.start()

    def near(n, du):
        def event():
            arrive(n, du, 0)
            send(2 + n, du, 0, n).start()
            send(4 + du, du, 0).start()
            send(8 + du, du, 0).start()
        return event

    def far():
        arrive(2, 2, 0, 0)
        arrive(3, 2, 0, 1)
        send(6, 2, 0).start()
        send(10, 2, 0).start()

    def line(w):
        def event():
            arrive(4 + w, w, 3)
            send(12 + w, w, 3, 0).start()
            arrive(8 + w, w, 1)
            send(16 + w, w, 1, 1).start()
        return event

    def last(w):
        def event():
            arrive(12 + w, w, 2, 0)
            arrive(16 + w, w, 2, 1)
        return event

    events = {
        1: [near(0, 3), near(1, 1)], 2: [line(0)], 3: [far], 4: [line(3)], 5: [line(1)], 7: [line(2)],
        12: [last(0)], 13: [last(3)], 14: [last(1)], 15: [last(2)],
    }
    later = [(2, 3, 0, 0), (3, 1, 0, 1), (6, 2, 0, None), (10, 2, 0, None)]
    for du in (3, 1):
        later += [(4 + du, du, 0, None), (8 + du, du, 0, None)]
    for w in range(4):
        later += [(12 + w, w, 3, 0), (16 + w, w, 1, 1)]

    kv_o[pl.ds(p, 1)] = kv[...][None]
    m_s[...] = jnp.full_like(m_s, MASKED)
    l_s[...] = jnp.zeros_like(l_s)
    acc[...] = jnp.zeros_like(acc)

    def step(block, h, lanes, mask, drop):
        st = nn(block, qt[h, :, lanes])
        if mask is not None:
            st = jnp.where(mask, st, MASKED)
        m_old = m_s[h, :, lanes]
        top = jnp.max(st, axis=0, keepdims=True)
        if drop is None:
            m_new = jnp.maximum(m_old, top)
            m_sub = m_new
        else:
            m_new = jnp.maximum(m_old, jnp.where(drop, MASKED, top))
            m_sub = jnp.where(drop, -MASKED, m_new)
        pt = jnp.exp(st - m_sub)
        a = jnp.exp(m_old - m_new)
        m_s[h, :, lanes] = m_new
        l_s[h, :, lanes] = l_s[h, :, lanes] * a + jnp.sum(pt, axis=0, keepdims=True)
        acc[h, :, lanes] = acc[h, :, lanes] * a + tn(block, pt.astype(BF16))[64:128]

    every = pl.ds(0, LANES)
    late = pl.ds(384, 384)
    mask = diagonal_mask(p, qpos[...], qstart[...])
    for h in range(KV):
        step(kv[h], h, every, mask, None)

    def visit(i, carry):
        for k, todo in events.items():
            @pl.when(i == k)
            def _():
                for event in todo:
                    event()

        j = index(pick(i, [o[0] for o in FORWARD]), pick(i, [o[1] for o in FORWARD]))

        @pl.when((j < p) & (j > 0))
        def _():
            for h in range(KV):
                step(kv_o[j, h, 0:PIECE, :], h, every, None, None)

        @pl.when((j < p) & (j == 0))
        def _():
            keep = first_mask(qstart[...])
            for h in range(KV):
                step(kv_o[0, h, 0:PIECE, :], h, every, keep, None)

        @pl.when(j > p)
        def _():
            drop = qstart[:, late] >= PIECE
            for h in range(KV):
                step(kv_o[j, h], h, late, None, drop)

        return carry

    lax.fori_loop(1, 16, visit, 0)
    for h in range(KV):
        total = l_s[h]
        att_o[h] = acc[h] / total
        lse_o[h] = m_s[h] + jnp.log(total)

    for cp in own:
        cp.wait_send()
    for item in later:
        send(*item).wait_send()


def attend_call(kv, qt, qpos, qstart):
    vm = pl.BlockSpec(memory_space=pltpu.VMEM)
    dma = pltpu.SemaphoreType.DMA
    return pl.pallas_call(
        attend_kernel,
        out_shape=(
            jax.ShapeDtypeStruct((16, KV, T, 128), BF16),
            jax.ShapeDtypeStruct((KV, HD, LANES), F32),
            jax.ShapeDtypeStruct((KV, 1, LANES), F32),
        ),
        in_specs=[vm] * 4,
        out_specs=(vm, vm, vm),
        scratch_shapes=[
            pltpu.VMEM((KV, 1, LANES), F32),
            pltpu.VMEM((KV, 1, LANES), F32),
            pltpu.VMEM((KV, HD, LANES), F32),
            dma((20,)),
            dma((20,)),
        ],
        compiler_params=pltpu.CompilerParams(
            collective_id=1, has_side_effects=True, vmem_limit_bytes=VLIMIT
        ),
        name="attend_forward",
    )(kv, qt, qpos, qstart)


def mlp_kernel(
    g, tok, cot, att, spread, sprt, fold, owner,
    mixed_o, dmid_o, dot_o, delta_o, dw_o, wd, act_s, wo_s, h2_s, dh2_s, mix_s,
):
    p2 = spread[0:576, :]
    p2t = sprt[:, 0:576]
    owner_rows = owner[...]
    g2 = gain_row(g[:, 31, 0:128], fold[...], owner_rows)
    wo_s[...] = nn(p2, g[:, 32:64, :].reshape(1024, D)).astype(BF16)
    for k in range(3):
        third = g[:, 160 + 32 * k : 192 + 32 * k, 0:512].reshape(1024, 512)
        wd[:, 512 * k : 512 * k + 512] = nn(p2, third).astype(BF16)
    rows = []
    for h in range(HEADS):
        kvh, gi = h // 3, h % 3
        rows.append(
            jnp.concatenate(
                [att[kvh, :, q * 384 + gi * 128 : q * 384 + gi * 128 + 128] for q in range(2)], axis=1
            )
        )
    att_f = jnp.concatenate(rows, axis=0)
    att_t = att_f.T.astype(BF16)
    middle = token_rows(tok) + nt(att_t, wo_s[...])
    r2 = lax.rsqrt(jnp.sum(middle * middle, axis=-1, keepdims=True) * (1.0 / D) + EPS)
    n2 = middle * r2
    h2_s[...] = (n2 * g2).astype(BF16)
    mix_s[...] = middle
    dh2_s[...] = jnp.zeros_like(dh2_s)
    dy = token_rows(cot).astype(BF16)
    dyt_rows = jnp.concatenate([cot[0], cot[1]], axis=1)

    def chunk(f, carry):
        at = pl.ds(8 * f, 8)
        lanes = pl.ds(pl.multiple_of(384 * f, 128), 384)
        wg = g[at, 64:112, :].reshape(384, D)
        wu = g[at, 112:160, :].reshape(384, D)
        h2 = h2_s[...]
        gate = nt(h2, wg)
        up = nt(h2, wu)
        sig = 1.0 / (1.0 + jnp.exp(-gate))
        silu = gate * sig
        act = (silu * up).astype(BF16)
        act_s[:, lanes] = act
        wdf = wd[:, lanes]
        mix_s[...] += nt(act, wdf)
        da = nn(dy, wdf)
        dup = (da * silu).astype(BF16)
        dgate = (da * up * sig * (1.0 + gate * (1.0 - sig))).astype(BF16)
        dh2_s[...] += nn(dgate, wg) + nn(dup, wu)
        dw_o[at, 64:112, :] = tn(dgate, h2).astype(BF16).reshape(8, 48, D)
        dw_o[at, 112:160, :] = tn(dup, h2).astype(BF16).reshape(8, 48, D)
        return carry

    lax.fori_loop(0, 4, chunk, 0)
    for q in range(2):
        mixed_o[q] = mix_s[PIECE * q : PIECE * (q + 1), :].T.astype(BF16)
    dyt = nn(p2t, dyt_rows).astype(BF16)
    dw_o[:, 160:256, 512:576] = jnp.zeros((32, 96, 64), BF16)
    for k in range(3):
        part = nn(dyt, act_s[:, 512 * k : 512 * k + 512]).astype(BF16)
        dw_o[:, 160 + 32 * k : 192 + 32 * k, 0:512] = part.reshape(32, 32, 512)
    dh2 = dh2_s[...]
    gsum = jnp.sum(dh2 * n2, axis=0, keepdims=True)
    gain = nn((gsum * owner_rows).astype(BF16), fold[...])
    g2v = dh2 * g2
    dmid = dy.astype(F32) + r2 * (g2v - n2 * (jnp.sum(g2v * n2, axis=-1, keepdims=True) * (1.0 / D)))
    dmid_o[...] = dmid
    dbr = dmid.astype(BF16)
    dbt = nn(p2t, dmid.T.astype(BF16)).astype(BF16)
    dw_o[:, 32:64, :] = with_row(nn(dbt, att_t).reshape(32, 32, D), 18, gain).astype(BF16)
    dw_o[:, 0:32, :] = jnp.zeros((32, 32, D), BF16)
    datt = nn(dbr, wo_s[...]).astype(BF16).astype(F32).T
    for h in range(HEADS):
        kvh, gi = h // 3, h % 3
        for q in range(2):
            lane = q * 384 + gi * 128
            part = datt[64 * h : 64 * h + 64, 128 * q : 128 * q + 128]
            dot_o[kvh, 64:128, lane : lane + 128] = part.astype(BF16)
            delta_o[kvh, :, lane : lane + 128] = jnp.sum(
                part * att[kvh, :, lane : lane + 128], axis=0, keepdims=True
            )
    for h in range(KV):
        dot_o[h, 0:64, :] = jnp.zeros((64, LANES), BF16)


def mlp_call(g, tok, cot, att, spread, sprt, fold, owner):
    vm = pl.BlockSpec(memory_space=pltpu.VMEM)
    return pl.pallas_call(
        mlp_kernel,
        out_shape=(
            jax.ShapeDtypeStruct((2, D, PIECE), BF16),
            jax.ShapeDtypeStruct((T, D), F32),
            jax.ShapeDtypeStruct((KV, 128, LANES), BF16),
            jax.ShapeDtypeStruct((KV, 1, LANES), F32),
            jax.ShapeDtypeStruct((32, 256, D), BF16),
        ),
        in_specs=[vm] * 8,
        out_specs=(vm,) * 5,
        scratch_shapes=[
            pltpu.VMEM((D, FF), BF16),
            pltpu.VMEM((T, FF), BF16),
            pltpu.VMEM((D, D), BF16),
            pltpu.VMEM((T, D), BF16),
            pltpu.VMEM((T, D), F32),
            pltpu.VMEM((T, D), F32),
        ],
        compiler_params=pltpu.CompilerParams(vmem_limit_bytes=VLIMIT),
        name="feed_forward",
    )(g, tok, cot, att, spread, sprt, fold, owner)


def attend_back_kernel(
    kv, qt, dot, lse, delta, qpos, qstart, dq_o, dkv_o, sent, va, vb, vp, vm, ua, ub, up, um, ss, rs
):
    b, s, c, p, y, x = place()
    ring, index = plane_ring(b, c, p, y, x, ss, rs)
    lo, hi = HALVES
    dq_o[...] = jnp.zeros_like(dq_o)

    def view(du, dv, part=None):
        at = index(du, dv)
        return sent.at[at] if part is None else sent.at[at, :, HALVES[part]]

    def add(du, dv, buf, part=None):
        at = index(du, dv)
        for h in range(KV):
            if part is None:
                sent[at, h] = (sent[at, h].astype(F32) + buf[h].astype(F32)).astype(BF16)
            else:
                rows = slice(PIECE * part, PIECE * (part + 1))
                sent[at, h, rows, :] = (sent[at, h, rows, :].astype(F32) + buf[h].astype(F32)).astype(BF16)

    def link(n, src, dst):
        return ring.copy(n, src, dst)

    pieces = {}
    for w in range(4):
        pieces[12 + w] = (w, 2, 0, va.at[w])
        pieces[16 + w] = (w, 2, 1, vb.at[w])
        pieces[4 + w] = (w, 1, None, vp.at[w])
        pieces[8 + w] = (w, 3, None, vm.at[w])
    pieces[2] = (2, 0, 0, ua)
    pieces[3] = (2, 0, 1, ub)
    pieces[0] = (1, 0, None, up)
    pieces[1] = (3, 0, None, um)

    def send(n):
        du, dv, part, dst = pieces[n]
        return link(n, view(du, dv, part), dst)

    def event(du, dv):
        if dv == 2:
            send(12 + du).start()
            send(16 + du).start()
        elif dv == 1:
            send(12 + du).wait_recv()
            add(du, 1, va.at[du], 0)
            send(4 + du).start()
        elif dv == 3:
            send(16 + du).wait_recv()
            add(du, 3, vb.at[du], 1)
            send(8 + du).start()
        else:
            send(4 + du).wait_recv()
            send(8 + du).wait_recv()
            if du:
                add(du, 0, vp.at[du])
                add(du, 0, vm.at[du])
            if du == 2:
                send(2).start()
                send(3).start()
            elif du == 1:
                send(2).wait_recv()
                add(1, 0, ua, 0)
                send(0).start()
            elif du == 3:
                send(3).wait_recv()
                add(3, 0, ub, 1)
                send(1).start()

    def step(block, h, lanes, mask, drop):
        q = qt[h, :, lanes]
        do = dot[h, :, lanes]
        st = nn(block, q)
        if mask is not None:
            st = jnp.where(mask, st, MASKED)
        base = lse[h, :, lanes]
        if drop is not None:
            base = jnp.where(drop, -MASKED, base)
        pt = jnp.exp(st - base)
        dp = nn(block, do)
        ds = (pt * (dp - delta[h, :, lanes])).astype(BF16)
        dq_o[h, :, lanes] += tn(block, ds)[0:64]
        return nt(ds, q) + nt(pt.astype(BF16), do)

    every = pl.ds(0, LANES)
    late = pl.ds(384, 384)

    def visit(i, carry):
        j = index(pick(i, [o[0] for o in BACKWARD]), pick(i, [o[1] for o in BACKWARD]))

        @pl.when(j < p)
        def _():
            sent[j, :, PIECE:T, :] = jnp.zeros((KV, PIECE, 128), BF16)

        @pl.when((j < p) & (j > 0))
        def _():
            for h in range(KV):
                sent[j, h, 0:PIECE, :] = step(kv[j, h, 0:PIECE, :], h, every, None, None).astype(BF16)

        @pl.when((j < p) & (j == 0))
        def _():
            keep = first_mask(qstart[...])
            for h in range(KV):
                sent[0, h, 0:PIECE, :] = step(kv[0, h, 0:PIECE, :], h, every, keep, None).astype(BF16)

        @pl.when(j > p)
        def _():
            drop = qstart[:, late] >= PIECE
            for h in range(KV):
                sent[j, h] = step(kv[j, h], h, late, None, drop).astype(BF16)

        for k, offset in enumerate(BACKWARD):
            if k:
                @pl.when(i == k)
                def _():
                    event(*offset)

        return carry

    lax.fori_loop(1, 16, visit, 0)
    mask = diagonal_mask(p, qpos[...], qstart[...])
    for h in range(KV):
        dkv_o[h] = step(kv[p, h], h, every, mask, None)

    event(0, 0)
    send(0).wait_recv()
    send(1).wait_recv()
    for h in range(KV):
        total = dkv_o[h] + vp[0, h].astype(F32) + vm[0, h].astype(F32)
        dkv_o[h] = total + up[h].astype(F32) + um[h].astype(F32)
    for n in pieces:
        send(n).wait_send()


def attend_back_call(kv, qt, dot, lse, delta, qpos, qstart):
    vm = pl.BlockSpec(memory_space=pltpu.VMEM)
    dma = pltpu.SemaphoreType.DMA
    return pl.pallas_call(
        attend_back_kernel,
        out_shape=(
            jax.ShapeDtypeStruct((KV, HD, LANES), F32),
            jax.ShapeDtypeStruct((KV, T, 128), F32),
        ),
        in_specs=[vm] * 7,
        out_specs=(vm, vm),
        scratch_shapes=[
            pltpu.VMEM((16, KV, T, 128), BF16),
            pltpu.VMEM((4, KV, PIECE, 128), BF16),
            pltpu.VMEM((4, KV, PIECE, 128), BF16),
            pltpu.VMEM((4, KV, T, 128), BF16),
            pltpu.VMEM((4, KV, T, 128), BF16),
            pltpu.VMEM((KV, PIECE, 128), BF16),
            pltpu.VMEM((KV, PIECE, 128), BF16),
            pltpu.VMEM((KV, T, 128), BF16),
            pltpu.VMEM((KV, T, 128), BF16),
            dma((20,)),
            dma((20,)),
        ],
        compiler_params=pltpu.CompilerParams(
            collective_id=2, has_side_effects=True, vmem_limit_bytes=VLIMIT
        ),
        name="attend_backward",
    )(kv, qt, dot, lse, delta, qpos, qstart)


def post_kernel(
    dw_in, g, tok, h1, dq, dkv, dmid, cos, sin, sprt, fold, owner, tg_o, dw_o, stage, sem
):
    co, si = cos[...], sin[...]

    def unrot(u):
        u1, u2 = u[0:32], u[32:64]
        return jnp.concatenate([u1 * co + u2 * si, u2 * co - u1 * si], axis=0)

    rows, vals = [], []
    for h in range(HEADS):
        kvh, gi = h // 3, h % 3
        part = jnp.concatenate(
            [dq[kvh, :, q * 384 + gi * 128 : q * 384 + gi * 128 + 128] for q in range(2)], axis=1
        )
        rows.append(unrot(part * 0.125))
    for h in range(KV):
        both = dkv[h].T
        rows.append(unrot(both[0:64]))
        vals.append(both[64:128])
    dz = jnp.concatenate(rows + vals, axis=0).astype(BF16)
    dzp = nn(sprt[...], dz).astype(BF16)
    wa = g[:, :, :]
    owner_rows = owner[...]
    g1 = gain_row(wa[:, 30, 0:128], fold[...], owner_rows)
    dh1 = tn(dzp, wa.reshape(1024, D))
    x = token_rows(tok)
    r1 = lax.rsqrt(jnp.sum(x * x, axis=-1, keepdims=True) * (1.0 / D) + EPS)
    n1 = x * r1
    gsum = jnp.sum(dh1 * n1, axis=0, keepdims=True)
    gain = nn((gsum * owner_rows).astype(BF16), fold[...])
    stage[...] = with_row(nn(dzp, h1[...]).reshape(32, 32, D), 30, gain).astype(BF16)
    g1v = dh1 * g1
    tg = dmid[...] + r1 * (g1v - n1 * (jnp.sum(g1v * n1, axis=-1, keepdims=True) * (1.0 / D)))
    for q in range(2):
        tg_o[q] = tg[PIECE * q : PIECE * (q + 1), :].T.astype(BF16)
    cp = pltpu.make_async_copy(stage, dw_o.at[:, 0:32], sem)
    cp.start()
    cp.wait()


def post_call(dw, g, tok, h1, dq, dkv, dmid, cos, sin, sprt, fold, owner):
    vm = pl.BlockSpec(memory_space=pltpu.VMEM)
    any_ = pl.BlockSpec(memory_space=pl.ANY)
    return pl.pallas_call(
        post_kernel,
        out_shape=(
            jax.ShapeDtypeStruct((2, D, PIECE), BF16),
            jax.ShapeDtypeStruct((32, 256, D), BF16),
        ),
        grid=(1,),
        in_specs=[any_, whole((32, 32, D))] + [vm] * 10,
        out_specs=(vm, any_),
        scratch_shapes=[pltpu.VMEM((32, 32, D), BF16), pltpu.SemaphoreType.DMA(())],
        input_output_aliases={0: 1},
        compiler_params=pltpu.CompilerParams(vmem_limit_bytes=VLIMIT),
        name="project_back",
    )(dw, g, tok, h1, dq, dkv, dmid, cos, sin, sprt, fold, owner)


def scatter_kernel(
    dw, mixed, tgrad, mixed_o, tgrad_o, raw_o, down_o,
    own, r0, va, vb, vp, vm, ua, ub, up, um, zs, zd, za, zb, zp, zm, ya, yb, yp, ym,
    c0, lsem, rsem, zsem, zz, zl,
):
    b, s, c, p, y, x = place()
    early = jnp.minimum(s, 31 - s)
    slot = lax.div(s, 16)
    bar = hail(grid_partners(b, s, c, y, x))
    for m in (0, 1):
        src = 2 * early + m
        @pl.when(src != s)
        def _():
            pl.semaphore_signal(bar, inc=1, device_id=(b, src), device_id_type=MESH)
    own_target = jnp.where(2 * early == s, 1, 0) + jnp.where(2 * early + 1 == s, 1, 0)
    pl.semaphore_wait(bar, 12 - own_target)
    other = (b, seq_of(y, x, 1 - c))

    order = [(dy, dx) for dy in range(4) for dx in range(4)]
    far = [o for o in order if 2 in o]
    mid = [o for o in order if 2 not in o and 0 not in o]
    near = [o for o in order if 2 not in o and 0 in o]
    near.sort(key=lambda o: o == (0, 0))
    fold = {}
    for o in far + mid + near:
        dy, dx = o
        n = 4 * dy + dx
        yy, xx = hop(y, dy), hop(x, dx)
        cp = rcopy(dw.at[yy, xx, 1 - c], r0.at[yy, xx], c0.at[0, n], c0.at[1, n], other)
        lc = pltpu.make_async_copy(dw.at[yy, xx, c], own.at[yy, xx], lsem.at[n])
        cp.start()
        lc.start()
        fold[o] = (cp, lc)

    for q, dst in enumerate((p, 31 - p)):
        for k, (src_ref, dst_ref) in enumerate(((mixed, mixed_o), (tgrad, tgrad_o))):
            @pl.when(dst != s)
            def _():
                rcopy(src_ref.at[q], dst_ref.at[c], zz.at[0, k, q], zz.at[1, k, c], (b, dst)).start()

            @pl.when(dst == s)
            def _():
                pltpu.make_async_copy(src_ref.at[q], dst_ref.at[c], zl.at[k]).start()

    sent = []
    rings = []
    for h in (0, 1):
        def spot(du, dv, h=h):
            return (hop(y, dv), hop(x, du)) if h == 0 else (hop(y, du), hop(x, dv))

        def dev(du, dv, spot=spot):
            return (b, seq_of(*spot(du, dv), c))

        rings.append((Ring(dev, rsem.at[0, h], rsem.at[1, h]), spot))

    def rows(h, part=None):
        return pl.ds(128 * h, 128) if part is None else pl.ds(128 * h + 64 * part, 64)

    landing = []
    for h in (0, 1):
        found = {}
        for w in range(4):
            found[12 + w] = (w, 2, 0, va.at[h, w])
            found[16 + w] = (w, 2, 1, vb.at[h, w])
            found[4 + w] = (w, 1, None, vp.at[h, w])
            found[8 + w] = (w, 3, None, vm.at[h, w])
        found[2] = (2, 0, 0, ua.at[h])
        found[3] = (2, 0, 1, ub.at[h])
        found[0] = (1, 0, None, up.at[h])
        found[1] = (3, 0, None, um.at[h])
        landing.append(found)

    def link(h, n):
        du, dv, part, dst = landing[h][n]
        ring, spot = rings[h]
        return ring.copy(n, own.at[(*spot(du, dv), rows(h, part))], dst)

    def go(h, *numbers):
        for n in numbers:
            cp = link(h, n)
            cp.start()
            sent.append(cp)

    def add(h, du, dv, part, *refs):
        at = (*rings[h][1](du, dv), rows(h, part))
        total = own[at].astype(F32)
        for ref in refs:
            total += ref[...].astype(F32)
        own[at] = total.astype(BF16)

    def folded(offsets):
        for o in offsets:
            cp, lc = fold[o]
            lc.wait()
            cp.wait_recv()
            at = (hop(y, o[0]), hop(x, o[1]))
            own[at] = (own[at].astype(F32) + r0[at].astype(F32)).astype(BF16)

    def sides(h, w):
        link(h, 12 + w).wait_recv()
        add(h, w, 1, 0, va.at[h, w])
        go(h, 4 + w)
        link(h, 16 + w).wait_recv()
        add(h, w, 3, 1, vb.at[h, w])
        go(h, 8 + w)

    def home(h, w):
        link(h, 4 + w).wait_recv()
        link(h, 8 + w).wait_recv()
        add(h, w, 0, None, vp.at[h, w], vm.at[h, w])
        if w == 2:
            go(h, 2, 3)
        elif w == 1:
            link(h, 2).wait_recv()
            add(h, 1, 0, 0, ua.at[h])
            go(h, 0)
        elif w == 3:
            link(h, 3).wait_recv()
            add(h, 3, 0, 1, ub.at[h])
            go(h, 1)

    folded(far)
    for w in (2, 1, 3, 0):
        for h in (0, 1):
            go(h, 12 + w, 16 + w)
    folded(mid)
    for w in (2, 1, 3):
        for h in (0, 1):
            sides(h, w)
    folded(near)
    for h in (0, 1):
        sides(h, 0)
    for w in (2, 1, 3, 0):
        for h in (0, 1):
            home(h, w)
    final = []
    for h in (0, 1):
        link(h, 0).wait_recv()
        link(h, 1).wait_recv()
        final.append(own[y, x, rows(h)].astype(F32) + up[h].astype(F32) + um[h].astype(F32))
    fa, fb = final
    main = jnp.concatenate([fa, fb[0:32]], axis=0)
    down = jnp.concatenate([fb[32 + 32 * k : 64 + 32 * k, 0:512] for k in range(3)], axis=1)
    for k in range(4):
        zs[k] = main[:, 144 * k : 144 * k + 144].astype(BF16)
        zd[k] = down[:, 384 * k : 384 * k + 384].astype(BF16)

    def zlink(n):
        at = hop(b, 2 if n > 1 else 1 + 2 * n)
        dev = (hop(b, 1 if n in (0, 2) else 3), s)
        found = []
        for k, (ref, size, dst) in enumerate(((zs, 80, (zp, zm, za, zb)[n]), (zd, 16, (yp, ym, ya, yb)[n]))):
            src = ref.at[at] if n < 2 else ref.at[at, pl.ds(size * (n - 2), size)]
            found.append(rcopy(src, dst, zsem.at[0, k, n], zsem.at[1, k, n], dev))
        return found

    def zgo(n):
        for cp in zlink(n):
            cp.start()
            sent.append(cp)

    def zarrive(n):
        for cp in zlink(n):
            cp.wait_recv()

    zgo(2)
    zgo(3)
    for n, bufs in ((2, (za, ya)), (3, (zb, yb))):
        zarrive(n)
        at = hop(b, 1 if n == 2 else 3)
        for ref, size, buf in ((zs, 80, bufs[0]), (zd, 16, bufs[1])):
            part = (at, pl.ds(size * (n - 2), size))
            ref[part] = (ref[part].astype(F32) + buf[...].astype(F32)).astype(BF16)
        zgo(n - 2)
    zarrive(0)
    zarrive(1)
    raw_o[...] = zs[b].astype(F32) + zp[...].astype(F32) + zm[...].astype(F32)
    down_o[...] = zd[b].astype(F32) + yp[...].astype(F32) + ym[...].astype(F32)
    for cp, lc in fold.values():
        cp.wait_send()
    for cp in sent:
        cp.wait_send()
    for q, dst in enumerate((p, 31 - p)):
        for k, (src_ref, dst_ref) in enumerate(((mixed, mixed_o), (tgrad, tgrad_o))):
            @pl.when(dst != s)
            def _():
                rcopy(src_ref.at[q], dst_ref.at[c], zz.at[0, k, q], zz.at[1, k, c], (b, dst)).wait_send()

            @pl.when(dst == s)
            def _():
                pltpu.make_async_copy(src_ref.at[q], dst_ref.at[c], zl.at[k]).wait()
    for m in (0, 1):
        src = 2 * early + m
        for k, (src_ref, dst_ref) in enumerate(((mixed, mixed_o), (tgrad, tgrad_o))):
            @pl.when(src != s)
            def _():
                rcopy(src_ref.at[0], dst_ref.at[m], zz.at[0, k, 0], zz.at[1, k, m], (b, src)).wait_recv()


def scatter_call(dw, mixed, tgrad):
    dma = pltpu.SemaphoreType.DMA
    any_ = pl.BlockSpec(memory_space=pl.ANY)
    vm = pl.BlockSpec(memory_space=pltpu.VMEM)
    return pl.pallas_call(
        scatter_kernel,
        out_shape=(
            jax.ShapeDtypeStruct((2, D, PIECE), BF16),
            jax.ShapeDtypeStruct((2, D, PIECE), BF16),
            jax.ShapeDtypeStruct((160, 144), F32),
            jax.ShapeDtypeStruct((32, 384), F32),
        ),
        in_specs=[any_, any_, any_],
        out_specs=(any_, any_, vm, vm),
        scratch_shapes=[
            pltpu.VMEM((4, 4, 256, D), BF16),
            pltpu.VMEM((4, 4, 256, D), BF16),
            pltpu.VMEM((2, 4, 64, D), BF16),
            pltpu.VMEM((2, 4, 64, D), BF16),
            pltpu.VMEM((2, 4, 128, D), BF16),
            pltpu.VMEM((2, 4, 128, D), BF16),
            pltpu.VMEM((2, 64, D), BF16),
            pltpu.VMEM((2, 64, D), BF16),
            pltpu.VMEM((2, 128, D), BF16),
            pltpu.VMEM((2, 128, D), BF16),
            pltpu.VMEM((4, 160, 144), BF16),
            pltpu.VMEM((4, 32, 384), BF16),
            pltpu.VMEM((80, 144), BF16),
            pltpu.VMEM((80, 144), BF16),
            pltpu.VMEM((160, 144), BF16),
            pltpu.VMEM((160, 144), BF16),
            pltpu.VMEM((16, 384), BF16),
            pltpu.VMEM((16, 384), BF16),
            pltpu.VMEM((32, 384), BF16),
            pltpu.VMEM((32, 384), BF16),
            dma((2, 16)),
            dma((16,)),
            dma((2, 2, 20)),
            dma((2, 2, 4)),
            dma((2, 2, 2)),
            dma((2,)),
        ],
        compiler_params=pltpu.CompilerParams(
            collective_id=3, has_side_effects=True, vmem_limit_bytes=VLIMIT
        ),
        name="scatter_grads",
    )(dw, mixed, tgrad)


def finish_kernel(mixed, tgrad, raw, down, mixed_o, tgrad_o, g1, wq, wk, wv, wo, g2, wg, wu, wd):
    mixed_o[...] = mixed[...]
    tgrad_o[...] = tgrad[...]
    g1[...] = raw[30:31, 0:18]
    g2[...] = raw[50:51, 0:18]
    for at, ref in ((0, wq), (18, wk), (24, wv), (32, wo), (64, wg), (112, wu)):
        ref[...] = raw[at : at + ref.shape[0], :]
    wd[...] = down[0:18, :]


def finish_call(mixed, tgrad, raw, down):
    vm = pl.BlockSpec(memory_space=pltpu.VMEM)
    shapes = [(1, 18), (18, 144), (6, 144), (6, 144), (18, 144), (1, 18), (48, 144), (48, 144), (18, 384)]
    return pl.pallas_call(
        finish_kernel,
        out_shape=tuple([jax.ShapeDtypeStruct((2, D, PIECE), BF16)] * 2 + [jax.ShapeDtypeStruct(n, F32) for n in shapes]),
        in_specs=[vm] * 4,
        out_specs=(vm,) * 11,
        name="write_outputs",
    )(mixed, tgrad, raw, down)


def body(
    tokens, doc_lengths, first_gain, query_weight, key_matrix, value_matrix,
    output_weight, second_gain, gate_weight, up_weight, down_weight, cotangent,
):
    s = lax.axis_index("seq")
    c, p = s % 2, s // 2
    gains = jnp.stack([first_gain, second_gain])
    spread = jnp.asarray(spread_matrix())
    sprt = jnp.asarray(spread_matrix().T.copy())
    fold, owner = (jnp.asarray(m) for m in gain_matrix())

    lens = lax.dynamic_index_in_dim(doc_lengths[:, 0, :], c, 0, False)
    starts = [jnp.zeros((), jnp.int32), lens[0], lens[0] + lens[1]]
    at = jnp.arange(PIECE, dtype=jnp.int32)
    spots = jnp.stack([p * PIECE + at, (31 - p) * PIECE + at])
    begins = jnp.where(spots >= starts[2], starts[2], jnp.where(spots >= starts[1], starts[1], 0))
    rates = THETA ** (-2.0 * jnp.arange(HD // 2, dtype=F32) / HD)
    angles = (spots - begins).reshape(T).astype(F32)[None, :] * rates[:, None]
    cos, sin = jnp.cos(angles), jnp.sin(angles)
    qpos = jnp.broadcast_to(spots[:, None], (2, 3, PIECE)).reshape(1, LANES)
    qstart = jnp.broadcast_to(begins[:, None], (2, 3, PIECE)).reshape(1, LANES)

    shards = [
        query_weight.T, key_matrix.T, value_matrix.T, output_weight.T,
        gate_weight.T, up_weight.T, down_weight.T, gains,
    ]
    turn = lambda a: jnp.swapaxes(a[:, 0], 1, 2)
    tok, cot, gathered = gather_call(shards, turn(tokens), turn(cotangent))
    g = gathered.reshape(32, 256, D)
    kv, qt, h1 = pre_call(g, tok, cos, sin, spread, fold, owner)
    kv_all, att, lse = attend_call(kv, qt, qpos, qstart)
    mixed, dmid, dot, delta, dw = mlp_call(g, tok, cot, att, spread, sprt, fold, owner)
    dq, dkv = attend_back_call(kv_all, qt, dot, lse, delta, qpos, qstart)
    tgrad, dw = post_call(dw, g, tok, h1, dq, dkv, dmid, cos, sin, sprt, fold, owner)
    mixed, tgrad, raw, down = scatter_call(dw.reshape(4, 4, 2, 256, D), mixed, tgrad)
    mixed, tgrad, g1, wq, wk, wv, wo, g2, wg, wu, wd = finish_call(mixed, tgrad, raw, down)
    back = lambda a: jnp.swapaxes(a, 1, 2)[:, None]
    return (
        back(mixed), back(tgrad), g1.reshape(18), wq.T, wk.T, wv.T, wo.T, g2.reshape(18), wg.T, wu.T, wd.T,
    )


def solution(mesh):
    weight = P("batch", "seq")
    rows = P(None, "batch", "seq", None)
    return jax.shard_map(
        body,
        mesh=mesh,
        in_specs=(
            rows, P(None, "batch", None), P("seq"), weight, weight, weight, weight,
            P("seq"), weight, weight, weight, rows,
        ),
        out_specs=(
            rows, rows, P("seq"), weight, weight, weight, weight,
            P("seq"), weight, weight, weight,
        ),
        check_vma=False,
    )
```

```python
import numpy as np
import ml_dtypes
import jax
import jax.numpy as jnp
from jax import lax
from jax.experimental import pallas as pl
from jax.experimental.pallas import tpu as pltpu
from jax.sharding import PartitionSpec as P

D = 576
HEADS = 9
KV = 3
HD = 64
FF = 1536
PIECE = 128
T = 2 * PIECE
LANES = 3 * T
EPS = 1e-05
THETA = 100000.0
MASKED = -1e30
MESH = pl.DeviceIdType.MESH
F32 = jnp.float32
BF16 = jnp.bfloat16
VLIMIT = 58 * 1024 * 1024


def spread_matrix():
    m = np.zeros((960, 1024), np.float32)
    n = np.arange(576)
    m[n, 32 * (n // 18) + n % 18] = 1
    n = np.arange(192)
    m[576 + n, 32 * (n // 6) + 18 + n % 6] = 1
    m[768 + n, 32 * (n // 6) + 24 + n % 6] = 1
    return m.astype(ml_dtypes.bfloat16)


def gain_matrix():
    n = np.arange(576)
    fold = np.zeros((576, 576), np.float32)
    for b in range(4):
        fold[n, 144 * b + n % 18] = 1
    owner = (n[None, :] // 18 == np.arange(32)[:, None]).astype(np.float32)
    return fold.astype(ml_dtypes.bfloat16), owner


def nn(a, b):
    return lax.dot_general(a, b, (((1,), (0,)), ((), ())), preferred_element_type=F32)


def nt(a, b):
    return lax.dot_general(a, b, (((1,), (1,)), ((), ())), preferred_element_type=F32)


def tn(a, b):
    return lax.dot_general(a, b, (((0,), (0,)), ((), ())), preferred_element_type=F32)


def rcopy(src, dst, ss, rs, dev):
    return pltpu.make_async_remote_copy(
        src_ref=src, dst_ref=dst, send_sem=ss, recv_sem=rs, device_id=dev, device_id_type=MESH
    )


def place():
    b = lax.axis_index("batch")
    s = lax.axis_index("seq")
    c = lax.rem(s, 2)
    p = lax.div(s, 2)
    return b, s, c, p, lax.div(p, 4), lax.rem(p, 4)


def seq_of(y, x, c):
    return (y * 4 + x) * 2 + c


def hop(i, d):
    return lax.rem(i + d, 4)


def hail(devices):
    bar = pltpu.get_barrier_semaphore()
    for dev in devices:
        pl.semaphore_signal(bar, inc=1, device_id=dev, device_id_type=MESH)
    return bar


def neighbours(b, s, c, y, x):
    found = [(b, seq_of(y, x, 1 - c))]
    for d in (1, 3):
        found += [
            (hop(b, d), s),
            (b, seq_of(y, hop(x, d), c)),
            (b, seq_of(hop(y, d), x, c)),
        ]
    return found


class Ring:
    def __init__(self, dev, ss, rs):
        self.dev, self.ss, self.rs = dev, ss, rs

    def copy(self, n, src, dst):
        du, dv = {0: (1, 0), 1: (3, 0), 2: (1, 0), 3: (3, 0)}.get(n, (0, 1 if n // 4 in (1, 3) else 3))
        return rcopy(src, dst, self.ss.at[n], self.rs.at[n], self.dev(du, dv))


def token_rows(ref):
    return jnp.concatenate([ref[0].astype(F32).T, ref[1].astype(F32).T], axis=0)


def gain_row(blocks, row, fold, owner):
    at = lax.broadcasted_iota(jnp.int32, (32, 1024), 0) * 32 + row
    one = (lax.broadcasted_iota(jnp.int32, (32, 1024), 1) == at).astype(F32).astype(BF16)
    spread = nt(nn(one, blocks[:, 0:128]).astype(BF16), fold[:, 0:128])
    return jnp.sum(spread * owner, axis=0, keepdims=True)


def place_row(row, values):
    at = lax.broadcasted_iota(jnp.int32, (1024, 32), 1) * 32 + row
    one = (lax.broadcasted_iota(jnp.int32, (1024, 32), 0) == at).astype(F32).astype(BF16)
    return nn(one, values.astype(BF16))


def diagonal_mask(p, qpos, qstart):
    row = lax.broadcasted_iota(jnp.int32, (T, 1), 0)
    kpos = jnp.where(row < PIECE, p * PIECE + row, (31 - p) * PIECE + row - PIECE)
    return (kpos <= qpos) & (kpos >= qstart)


def first_mask(qstart):
    row = lax.broadcasted_iota(jnp.int32, (PIECE, 1), 0)
    return row >= qstart


def pick(i, values):
    found = values[0]
    for k, value in enumerate(values[1:]):
        found = jnp.where(i == k + 1, value, found)
    return found


FORWARD = ((0, 0), (3, 0), (1, 0), (0, 3), (0, 1), (2, 0), (3, 3), (3, 1), (1, 3), (1, 1), (2, 3), (2, 1), (0, 2), (3, 2), (1, 2), (2, 2))
BACKWARD = ((0, 0), (2, 2), (1, 2), (3, 2), (0, 2), (2, 1), (2, 3), (1, 1), (1, 3), (3, 1), (3, 3), (0, 1), (0, 3), (2, 0), (1, 0), (3, 0))
HALVES = (pl.ds(0, PIECE), pl.ds(PIECE, PIECE))


ROWS = 224


class Plane:
    def __init__(self):
        self.b, self.s, self.c, self.p, self.y, self.x = place()
        c, y, x = self.c, self.y, self.x
        self.u, self.v = jnp.where(c == 0, x, y), jnp.where(c == 0, y, x)
        self.su, self.sv = 1 + 3 * c, 4 - 3 * c
        self.other = (self.b, seq_of(y, x, 1 - c))

    def index(self, du, dv):
        return lax.rem(self.u + du, 4) * self.su + lax.rem(self.v + dv, 4) * self.sv

    def dev(self, du, dv):
        return (self.b, 2 * self.index(du, dv) + self.c)

    def common(self, du, dv):
        return du * self.su + dv * self.sv


class Gather:
    def __init__(self, plane, view, own, sems, swap=None):
        self.ring = Ring(plane.dev, sems.at[0], sems.at[1])
        self.view, self.own, self.swap = view, own, swap
        self.later = []

    def copy(self, n, du, dv, part=None):
        ref = self.view(du, dv, part)
        return self.ring.copy(n, self.own if (du, dv) == (0, 0) else ref, ref)

    def send(self, *item):
        self.copy(*item).start()
        self.later.append(item)

    def arrive(self, n, du, dv, part=None):
        ref = self.view(du, dv, part)
        self.ring.copy(n, ref, ref).wait_recv()

    def done(self, du, dv):
        if self.swap is not None:
            self.swap(du, dv).start()

    def begin_u(self):
        self.send(0, 0, 0)
        self.send(1, 0, 0)

    def begin_v(self):
        self.send(4, 0, 0)
        self.send(8, 0, 0)
        self.done(0, 0)

    def near(self):
        for n, du in ((0, 3), (1, 1)):
            self.arrive(n, du, 0)
            self.send(2 + n, du, 0, n)
            self.send(4 + du, du, 0)
            self.send(8 + du, du, 0)
            self.done(du, 0)

    def far(self):
        self.arrive(2, 2, 0, 0)
        self.arrive(3, 2, 0, 1)
        self.send(6, 2, 0)
        self.send(10, 2, 0)
        self.done(2, 0)

    def line(self, w):
        self.arrive(4 + w, w, 3)
        self.send(12 + w, w, 3, 0)
        self.done(w, 3)
        self.arrive(8 + w, w, 1)
        self.send(16 + w, w, 1, 1)
        self.done(w, 1)

    def last(self, w):
        self.arrive(12 + w, w, 2, 0)
        self.arrive(16 + w, w, 2, 1)
        self.done(w, 2)

    def finish(self):
        for item in self.later:
            self.copy(*item).wait_send()
        if self.swap is not None:
            for du in range(4):
                for dv in range(4):
                    self.swap(du, dv).wait()


class Reduce:
    def __init__(self, plane, view, add, bufs, sems):
        self.ring = Ring(plane.dev, sems.at[0], sems.at[1])
        self.view, self.add = view, add
        va, vb, vp, vm, ua, ub, up, um = bufs
        self.pieces = {
            2: (2, 0, 0, ua), 3: (2, 0, 1, ub), 0: (1, 0, None, up), 1: (3, 0, None, um),
        }
        for w in range(4):
            self.pieces[12 + w] = (w, 2, 0, va.at[w])
            self.pieces[16 + w] = (w, 2, 1, vb.at[w])
            self.pieces[4 + w] = (w, 1, None, vp.at[w])
            self.pieces[8 + w] = (w, 3, None, vm.at[w])

    def copy(self, n):
        du, dv, part, dst = self.pieces[n]
        return self.ring.copy(n, self.view(du, dv, part), dst)

    def take(self, n, du, dv, part=None):
        self.copy(n).wait_recv()
        self.add(du, dv, part, self.pieces[n][3])

    def event(self, du, dv):
        if dv == 2:
            self.copy(12 + du).start()
            self.copy(16 + du).start()
        elif dv == 1:
            self.take(12 + du, du, 1, 0)
            self.copy(4 + du).start()
        elif dv == 3:
            self.take(16 + du, du, 3, 1)
            self.copy(8 + du).start()
        else:
            self.take(4 + du, du, 0)
            self.take(8 + du, du, 0)
            if du == 2:
                self.copy(2).start()
                self.copy(3).start()
            elif du == 1:
                self.take(2, 1, 0, 0)
                self.copy(0).start()
            elif du == 3:
                self.take(3, 3, 0, 1)
                self.copy(1).start()

    def end(self):
        self.take(0, 0, 0)
        self.take(1, 0, 0)

    def finish(self):
        for n in self.pieces:
            self.copy(n).wait_send()


class SumZ:
    def __init__(self, b, s, items, sems):
        self.b, self.s, self.items, self.sems = b, s, items, sems

    def copies(self, n):
        at = hop(self.b, 2 if n > 1 else 1 + 2 * n)
        dev = (hop(self.b, 1 if n in (0, 2) else 3), self.s)
        found = []
        for k, (ref, bufs) in enumerate(self.items):
            size = ref.shape[1] // 2
            src = ref.at[at] if n < 2 else ref.at[at, pl.ds(size * (n - 2), size)]
            found.append(rcopy(src, bufs[n], self.sems.at[0, k, n], self.sems.at[1, k, n], dev))
        return found

    def start(self, n):
        for cp in self.copies(n):
            cp.start()

    def begin(self):
        self.start(2)
        self.start(3)

    def middle(self):
        for n in (2, 3):
            for cp in self.copies(n):
                cp.wait_recv()
            at = hop(self.b, 1 if n == 2 else 3)
            for ref, bufs in self.items:
                size = ref.shape[1] // 2
                part = (at, pl.ds(size * (n - 2), size))
                ref[part] = ref[part] + bufs[n][...]
            self.start(n - 2)

    def result(self):
        for n in (0, 1):
            for cp in self.copies(n):
                cp.wait_recv()
        found = []
        for ref, bufs in self.items:
            found.append(ref[self.b].astype(F32) + bufs[0][...].astype(F32) + bufs[1][...].astype(F32))
        return found

    def finish(self):
        for n in range(4):
            for cp in self.copies(n):
                cp.wait_send()


SCRATCH = {
    "spread": ((960, 1024), BF16), "sprt": ((1024, 960), BF16), "fold": ((D, D), BF16),
    "raw_f": ((160, 144), F32), "dwn_f": ((32, 384), F32),
    "za": ((4, 160, 144), BF16), "zd": ((4, 32, 384), BF16),
    "blk1": ((32, D), BF16), "blk2": ((ROWS, D), BF16),
    "g1": ((32, 32, D), BF16), "g2": ((32, ROWS, D), BF16),
    "tok": ((2, D, PIECE), BF16), "cot": ((2, D, PIECE), BF16),
    "gain_s": ((4, 8, D), F32), "x_s": ((T, D), F32), "h1": ((T, D), BF16),
    "kv": ((KV, T, 128), BF16), "qt": ((KV, 128, LANES), BF16), "dot": ((KV, 128, LANES), BF16),
    "kva": ((16, KV, T, 128), BF16),
    "m_s": ((KV, 1, LANES), F32), "l_s": ((KV, 1, LANES), F32), "delta": ((KV, 1, LANES), F32),
    "acc": ((KV, HD, LANES), F32), "dq": ((KV, HD, LANES), F32), "dkv": ((KV, T, 128), F32),
    "wd_s": ((D, FF), BF16), "act_s": ((T, FF), BF16), "wo_s": ((D, D), BF16),
    "h2_s": ((T, D), BF16), "dh2_s": ((T, D), F32), "mix_s": ((T, D), F32),
    "mixed": ((2, D, PIECE), BF16), "tgrad": ((2, D, PIECE), BF16),
    "sent": ((16, KV, T, 128), BF16),
    "kva_": ((4, KV, PIECE, 128), BF16), "kvb_": ((4, KV, PIECE, 128), BF16),
    "kvp_": ((4, KV, T, 128), BF16), "kvm_": ((4, KV, T, 128), BF16),
    "kua_": ((KV, PIECE, 128), BF16), "kub_": ((KV, PIECE, 128), BF16),
    "kup_": ((KV, T, 128), BF16), "kum_": ((KV, T, 128), BF16),
    "r2": ((16, ROWS, D), BF16),
    "wva": ((4, ROWS // 2, D), BF16), "wvb": ((4, ROWS // 2, D), BF16),
    "wvp": ((4, ROWS, D), BF16), "wvm": ((4, ROWS, D), BF16),
    "wua": ((ROWS // 2, D), BF16), "wub": ((ROWS // 2, D), BF16),
    "wup": ((ROWS, D), BF16), "wum": ((ROWS, D), BF16),
    "r1": ((16, 32, D), BF16),
    "ava": ((4, 16, D), BF16), "avb": ((4, 16, D), BF16),
    "avp": ((4, 32, D), BF16), "avm": ((4, 32, D), BF16),
    "aua": ((16, D), BF16), "aub": ((16, D), BF16),
    "aup": ((32, D), BF16), "aum": ((32, D), BF16),
    "zs2": ((4, 128, 144), BF16), "zd2": ((4, 32, 384), BF16), "zs1": ((4, 32, 144), BF16),
    "zs2p": ((128, 144), BF16), "zs2m": ((128, 144), BF16), "zs2a": ((64, 144), BF16), "zs2b": ((64, 144), BF16),
    "zd2p": ((32, 384), BF16), "zd2m": ((32, 384), BF16), "zd2a": ((16, 384), BF16), "zd2b": ((16, 384), BF16),
    "zs1p": ((32, 144), BF16), "zs1m": ((32, 144), BF16), "zs1a": ((16, 144), BF16), "zs1b": ((16, 144), BF16),
}
SEMS = {
    "lsem": (4,), "zsem": (2, 2, 4), "zz": (4, 2, 2), "zl": (4,),
    "g1sem": (2, 20), "g1swap": (2, 16), "g2sem": (2, 20), "g2swap": (2, 16), "kvsem": (2, 20),
    "dksem": (2, 20), "d2fold": (2, 16), "d2sem": (2, 20), "d1fold": (2, 16), "d1sem": (2, 20),
    "z2sem": (2, 2, 4), "z1sem": (2, 1, 4),
}
INPUTS = (
    "wq", "wk", "wv", "wo", "wg", "wu", "wd", "gains", "tokens", "cotin", "cos", "sin", "qpos", "qstart",
    "owner", "spread_in", "sprt_in", "fold_in",
)
OUTPUTS = ("mixed_o", "tgrad_o", "raw_o", "down_o")


class Refs:
    def __init__(self, refs):
        for name, ref in zip((*INPUTS, *OUTPUTS, *SCRATCH, *SEMS), refs, strict=True):
            setattr(self, name, ref)


def layer_kernel(*refs):
    r = Refs(refs)
    plane = Plane()
    b, s, c, p, y, x = plane.b, plane.s, plane.c, plane.p, plane.y, plane.x
    early = jnp.minimum(s, 31 - s)
    slot = lax.div(s, 16)
    bar = hail(neighbours(b, s, c, y, x))
    around = [2 * early, 2 * early + 1, p, 31 - p]
    for peer in around:
        @pl.when(peer != s)
        def _():
            pl.semaphore_signal(bar, inc=1, device_id=(b, peer), device_id_type=MESH)
    constants = [
        pltpu.make_async_copy(src, dst, r.lsem.at[k])
        for k, (src, dst) in enumerate(((r.spread_in, r.spread), (r.sprt_in, r.sprt), (r.fold_in, r.fold)))
    ]
    for cp in constants:
        cp.start()
    r.raw_f[...] = jnp.zeros_like(r.raw_f)
    r.dwn_f[...] = jnp.zeros_like(r.dwn_f)
    for at, ref in ((0, r.wq), (18, r.wk), (24, r.wv), (32, r.wo), (64, r.wg), (112, r.wu)):
        r.raw_f[at : at + ref.shape[0], :] = ref[...].astype(F32)
    r.raw_f[30:32, 0:18] = r.gains[...].astype(F32)
    r.dwn_f[0:18, :] = r.wd[...].astype(F32)
    r.za[pl.ds(b, 1)] = r.raw_f[...].astype(BF16)[None]
    r.zd[pl.ds(b, 1)] = r.dwn_f[...].astype(BF16)[None]
    peers = 7
    for peer in around:
        peers = peers + jnp.where(peer != s, 1, 0)
    pl.semaphore_wait(bar, peers)

    def zcopies(n, at, part):
        dev = (hop(b, 1 if n in (0, 2) else 3), s)
        found = []
        for k, (ref, rows) in enumerate(((r.za, 80), (r.zd, 16))):
            view = ref.at[at] if part is None else ref.at[at, pl.ds(rows * part, rows)]
            found.append(rcopy(view, view, r.zsem.at[0, k, n], r.zsem.at[1, k, n], dev))
        return found

    def start(copies):
        for cp in copies:
            cp.start()

    zsent = [zcopies(0, b, None), zcopies(1, b, None)]
    start(zsent[0] + zsent[1])

    def outward(k, src_ref, dst_ref, act_remote, act_local):
        for m in (0, 1):
            dst = 2 * early + m

            @pl.when(dst != s)
            def _():
                act_remote(rcopy(src_ref.at[m], dst_ref.at[slot], r.zz.at[k, 0, m], r.zz.at[k, 1, slot], (b, dst)))

            @pl.when(dst == s)
            def _():
                act_local(pltpu.make_async_copy(src_ref.at[m], dst_ref.at[slot], r.zl.at[k]))

    def outward_wait(k, src_ref, dst_ref):
        for q, src in enumerate((p, 31 - p)):
            @pl.when(src != s)
            def _():
                rcopy(src_ref.at[0], dst_ref.at[q], r.zz.at[k, 0, 0], r.zz.at[k, 1, q], (b, src)).wait_recv()

    def homeward(k, src_ref, dst_ref, act_remote, act_local):
        for q, dst in enumerate((p, 31 - p)):
            @pl.when(dst != s)
            def _():
                act_remote(rcopy(src_ref.at[q], dst_ref.at[c], r.zz.at[k, 0, q], r.zz.at[k, 1, c], (b, dst)))

            @pl.when(dst == s)
            def _():
                act_local(pltpu.make_async_copy(src_ref.at[q], dst_ref.at[c], r.zl.at[k]))

    def homeward_wait(k, src_ref, dst_ref):
        for m in (0, 1):
            src = 2 * early + m

            @pl.when(src != s)
            def _():
                rcopy(src_ref.at[0], dst_ref.at[m], r.zz.at[k, 0, 0], r.zz.at[k, 1, m], (b, src)).wait_recv()

    begin = (lambda cp: cp.start(), lambda cp: cp.start())
    ended = (lambda cp: cp.wait_send(), lambda cp: cp.wait())
    outward(0, r.tokens, r.tok, *begin)
    outward(1, r.cotin, r.cot, *begin)

    for n, way in ((0, 3), (1, 1)):
        for cp in zcopies(n, hop(b, way), None):
            cp.wait_recv()
        zsent.append(zcopies(2 + n, hop(b, way), n))
        start(zsent[-1])
    for n in (2, 3):
        for cp in zcopies(n, hop(b, 2), n - 2):
            cp.wait_recv()
    main = jnp.concatenate([r.za[i].astype(F32) for i in range(4)], axis=1).astype(BF16)
    r.blk1[...] = main[0:32]

    def weights(ref, own, sems, swap_sems, half):
        def view(du, dv, part=None):
            at = 2 * plane.index(du, dv) + c
            return ref.at[at] if part is None else ref.at[at, pl.ds(half * part, half)]

        def swap(du, dv):
            n = plane.common(du, dv)
            dst = view(du, dv)
            src = own if (du, dv) == (0, 0) else dst
            return rcopy(src, dst, swap_sems.at[0, n], swap_sems.at[1, n], plane.other)

        return Gather(plane, view, own, sems, swap)

    first = weights(r.g1, r.blk1, r.g1sem, r.g1swap, 16)
    second = weights(r.g2, r.blk2, r.g2sem, r.g2swap, ROWS // 2)
    first.begin_u()
    first.begin_v()
    r.g1[pl.ds(s, 1)] = r.blk1[...][None]
    down = jnp.concatenate([r.zd[i] for i in range(4)], axis=1)
    r.blk2[0:128, :] = main[32:160]
    r.blk2[128:224, 512:576] = jnp.zeros((96, 64), BF16)
    for k in range(3):
        r.blk2[128 + 32 * k : 160 + 32 * k, 0:512] = down[:, 512 * k : 512 * (k + 1)]
    first.near()
    second.begin_u()
    r.g2[pl.ds(s, 1)] = r.blk2[...][None]
    first.line(0)
    first.far()
    outward_wait(0, r.tokens, r.tok)
    outward(0, r.tokens, r.tok, *ended)
    r.x_s[...] = token_rows(r.tok)
    for w in (3, 1, 2):
        first.line(w)
    second.begin_v()
    for w in (0, 3, 1, 2):
        first.last(w)
    first.finish()
    for cp in constants:
        cp.wait()

    owner_rows = r.owner[...]
    fold = r.fold[...]
    wa = r.g1[...].reshape(1024, D)
    gain1 = gain_row(wa, 30, fold, owner_rows)
    r.gain_s[0] = jnp.broadcast_to(gain1, (8, D))
    r.gain_s[1] = jnp.broadcast_to(gain_row(wa, 31, fold, owner_rows), (8, D))
    xin = r.x_s[...]
    inv1 = lax.rsqrt(jnp.sum(xin * xin, axis=-1, keepdims=True) * (1.0 / D) + EPS)
    r.h1[...] = (xin * inv1 * gain1).astype(BF16)
    w_all = nn(r.spread[...], wa).astype(BF16)
    z = nt(w_all, r.h1[...])
    co, si = r.cos[...], r.sin[...]

    def rot(a):
        a1, a2 = a[0:32], a[32:64]
        return jnp.concatenate([a1 * co - a2 * si, a2 * co + a1 * si], axis=0)

    def unrot(a):
        a1, a2 = a[0:32], a[32:64]
        return jnp.concatenate([a1 * co + a2 * si, a2 * co - a1 * si], axis=0)

    for h in range(KV):
        kh = rot(z[576 + 64 * h : 640 + 64 * h])
        vh = z[768 + 64 * h : 832 + 64 * h]
        r.kv[h] = jnp.concatenate([kh, vh], axis=0).T.astype(BF16)

    def kview(ref):
        def view(du, dv, part=None):
            at = plane.index(du, dv)
            return ref.at[at] if part is None else ref.at[at, :, HALVES[part]]
        return view

    keys = Gather(plane, kview(r.kva), r.kv, r.kvsem)
    keys.begin_u()
    keys.begin_v()
    r.kva[pl.ds(p, 1)] = r.kv[...][None]
    for h in range(HEADS):
        q = (rot(z[64 * h : 64 * h + 64]).astype(BF16).astype(F32) * 0.125).astype(BF16)
        kvh, gi = h // 3, h % 3
        for piece in range(2):
            lane = piece * 384 + gi * 128
            r.qt[kvh, 0:64, lane : lane + 128] = q[:, piece * 128 : piece * 128 + 128]
    for h in range(KV):
        r.qt[h, 64:128, :] = jnp.zeros((64, LANES), BF16)
        r.dot[h, 0:64, :] = jnp.zeros((64, LANES), BF16)

    r.m_s[...] = jnp.full_like(r.m_s, MASKED)
    r.l_s[...] = jnp.zeros_like(r.l_s)
    r.acc[...] = jnp.zeros_like(r.acc)
    every = pl.ds(0, LANES)
    late = pl.ds(384, 384)

    def step(block, h, lanes, mask, drop):
        st = nn(block, r.qt[h, :, lanes])
        if mask is not None:
            st = jnp.where(mask, st, MASKED)
        m_old = r.m_s[h, :, lanes]
        top = jnp.max(st, axis=0, keepdims=True)
        if drop is None:
            m_new = jnp.maximum(m_old, top)
            m_sub = m_new
        else:
            m_new = jnp.maximum(m_old, jnp.where(drop, MASKED, top))
            m_sub = jnp.where(drop, -MASKED, m_new)
        pt = jnp.exp(st - m_sub)
        a = jnp.exp(m_old - m_new)
        r.m_s[h, :, lanes] = m_new
        r.l_s[h, :, lanes] = r.l_s[h, :, lanes] * a + jnp.sum(pt, axis=0, keepdims=True)
        r.acc[h, :, lanes] = r.acc[h, :, lanes] * a + tn(block, pt.astype(BF16))[64:128]

    def allowed():
        return diagonal_mask(p, r.qpos[...], r.qstart[...])

    mask = allowed()
    for h in range(KV):
        step(r.kv[h], h, every, mask, None)

    events = {
        1: [keys.near, second.near], 2: [lambda: keys.line(0)], 3: [keys.far, lambda: second.line(0)],
        4: [lambda: keys.line(3)], 5: [lambda: keys.line(1), second.far], 7: [lambda: keys.line(2)],
        8: [lambda: second.line(3)], 10: [lambda: second.line(1)],
        12: [lambda: keys.last(0), lambda: second.line(2)], 13: [lambda: keys.last(3)],
        14: [lambda: keys.last(1), lambda: second.last(0)], 15: [lambda: keys.last(2)],
    }

    def visit(i, carry):
        for k, todo in events.items():
            @pl.when(i == k)
            def _():
                for event in todo:
                    event()

        j = plane.index(pick(i, [o[0] for o in FORWARD]), pick(i, [o[1] for o in FORWARD]))

        @pl.when((j < p) & (j > 0))
        def _():
            for h in range(KV):
                step(r.kva[j, h, 0:PIECE, :], h, every, None, None)

        @pl.when((j < p) & (j == 0))
        def _():
            keep = first_mask(r.qstart[...])
            for h in range(KV):
                step(r.kva[0, h, 0:PIECE, :], h, every, keep, None)

        @pl.when(j > p)
        def _():
            drop = r.qstart[:, late] >= PIECE
            for h in range(KV):
                step(r.kva[j, h], h, late, None, drop)

        return carry

    lax.fori_loop(1, 16, visit, 0)
    for h in range(KV):
        total = r.l_s[h]
        r.acc[h] = r.acc[h] / total
        r.m_s[h] = r.m_s[h] + jnp.log(total)
    rows = []
    for h in range(HEADS):
        kvh, gi = h // 3, h % 3
        rows.append(
            jnp.concatenate(
                [r.acc[kvh, :, q * 384 + gi * 128 : q * 384 + gi * 128 + 128] for q in range(2)], axis=1
            )
        )
    att_t = jnp.concatenate(rows, axis=0).T.astype(BF16)
    outward_wait(1, r.cotin, r.cot)
    outward(1, r.cotin, r.cot, *ended)
    dy = token_rows(r.cot).astype(BF16)
    dyt_rows = jnp.concatenate([r.cot[0], r.cot[1]], axis=1)
    for w in (3, 1, 2):
        second.last(w)
    keys.finish()
    second.finish()
    for group in zsent:
        for cp in group:
            cp.wait_send()

    p2 = r.spread[0:576, :]
    p2t = r.sprt[:, 0:576]
    r.wo_s[...] = nn(p2, r.g2[:, 0:32, :].reshape(1024, D)).astype(BF16)
    for k in range(3):
        third = r.g2[:, 128 + 32 * k : 160 + 32 * k, 0:512].reshape(1024, 512)
        r.wd_s[:, 512 * k : 512 * k + 512] = nn(p2, third).astype(BF16)
    middle = r.x_s[...] + nt(att_t, r.wo_s[...])
    inv2 = lax.rsqrt(jnp.sum(middle * middle, axis=-1, keepdims=True) * (1.0 / D) + EPS)
    n2 = middle * inv2
    r.h2_s[...] = (n2 * r.gain_s[1, 0:1, :]).astype(BF16)
    r.mix_s[...] = middle
    r.dh2_s[...] = jnp.zeros_like(r.dh2_s)

    def chunk(f, carry):
        at = pl.ds(8 * f, 8)
        lanes = pl.ds(pl.multiple_of(384 * f, 128), 384)
        wg = r.g2[at, 32:80, :].reshape(384, D)
        wu = r.g2[at, 80:128, :].reshape(384, D)
        h2 = r.h2_s[...]
        gate = nt(h2, wg)
        up = nt(h2, wu)
        sig = 1.0 / (1.0 + jnp.exp(-gate))
        silu = gate * sig
        act = (silu * up).astype(BF16)
        r.act_s[:, lanes] = act
        wdf = r.wd_s[:, lanes]
        r.mix_s[...] += nt(act, wdf)
        da = nn(dy, wdf)
        dup = (da * silu).astype(BF16)
        dgate = (da * up * sig * (1.0 + gate * (1.0 - sig))).astype(BF16)
        r.dh2_s[...] += nn(dgate, wg) + nn(dup, wu)
        r.g2[at, 32:80, :] = tn(dgate, h2).astype(BF16).reshape(8, 48, D)
        r.g2[at, 80:128, :] = tn(dup, h2).astype(BF16).reshape(8, 48, D)
        return carry

    lax.fori_loop(0, 4, chunk, 0)
    for q in range(2):
        r.mixed[q] = r.mix_s[PIECE * q : PIECE * (q + 1), :].T.astype(BF16)
    homeward(2, r.mixed, r.mixed_o, *begin)
    dyt = nn(p2t, dyt_rows).astype(BF16)
    r.g2[:, 128:224, 512:576] = jnp.zeros((32, 96, 64), BF16)
    for k in range(3):
        part = nn(dyt, r.act_s[:, 512 * k : 512 * k + 512]).astype(BF16)
        r.g2[:, 128 + 32 * k : 160 + 32 * k, 0:512] = part.reshape(32, 32, 512)
    dh2 = r.dh2_s[...]
    gsum = jnp.sum(dh2 * n2, axis=0, keepdims=True)
    r.gain_s[2] = jnp.broadcast_to(gsum, (8, D))
    gain = nn((jnp.concatenate([r.gain_s[2]] * 4, axis=0) * r.owner[...]).astype(BF16), r.fold[...])
    g2v = dh2 * r.gain_s[1, 0:1, :]
    dmid = dy.astype(F32) + inv2 * (g2v - n2 * (jnp.sum(g2v * n2, axis=-1, keepdims=True) * (1.0 / D)))
    r.mix_s[...] = dmid
    dbt = nn(p2t, dmid.T.astype(BF16)).astype(BF16)
    r.g2[:, 0:32, :] = (nn(dbt, att_t) + place_row(18, gain)).astype(BF16).reshape(32, 32, D)

    def folder(ref, land, sems):
        def copy(du, dv):
            at = plane.index(du, dv)
            n = plane.common(du, dv)
            return rcopy(ref.at[2 * at + 1 - c], land.at[at], sems.at[0, n], sems.at[1, n], plane.other)

        def fold_in(du, dv):
            copy(du, dv).wait_recv()
            at = plane.index(du, dv)
            ref[2 * at + c] = ref[2 * at + c] + land[at]

        return copy, fold_in

    def reducer(ref, bufs, sems, half):
        def view(du, dv, part=None):
            at = 2 * plane.index(du, dv) + c
            return ref.at[at] if part is None else ref.at[at, pl.ds(half * part, half)]

        def add(du, dv, part, buf):
            at = 2 * plane.index(du, dv) + c
            where = (at,) if part is None else (at, pl.ds(half * part, half))
            ref[where] = ref[where] + buf[...]

        return Reduce(plane, view, add, bufs, sems)

    copy2, fold2 = folder(r.g2, r.r2, r.d2fold)
    sum2 = reducer(r.g2, (r.wva, r.wvb, r.wvp, r.wvm, r.wua, r.wub, r.wup, r.wum), r.d2sem, ROWS // 2)
    order = BACKWARD[1:] + BACKWARD[:1]
    for du, dv in order:
        copy2(dv, du).start()
    datt = nn(dmid.astype(BF16), r.wo_s[...]).astype(BF16).astype(F32).T
    for h in range(HEADS):
        kvh, gi = h // 3, h % 3
        for q in range(2):
            lane = q * 384 + gi * 128
            part = datt[64 * h : 64 * h + 64, 128 * q : 128 * q + 128]
            r.dot[kvh, 64:128, lane : lane + 128] = part.astype(BF16)
            r.delta[kvh, :, lane : lane + 128] = jnp.sum(
                part * r.acc[kvh, :, lane : lane + 128], axis=0, keepdims=True
            )

    def add_keys(du, dv, part, buf):
        at = plane.index(du, dv)
        if part is None:
            r.sent[at] = r.sent[at] + buf[...]
        else:
            rows = slice(PIECE * part, PIECE * (part + 1))
            r.sent[at, :, rows, :] = r.sent[at, :, rows, :] + buf[...]

    sumk = Reduce(
        plane, kview(r.sent), add_keys,
        (r.kva_, r.kvb_, r.kvp_, r.kvm_, r.kua_, r.kub_, r.kup_, r.kum_), r.dksem,
    )
    r.dq[...] = jnp.zeros_like(r.dq)

    def back(block, h, lanes, mask, drop):
        q = r.qt[h, :, lanes]
        do = r.dot[h, :, lanes]
        st = nn(block, q)
        if mask is not None:
            st = jnp.where(mask, st, MASKED)
        base = r.m_s[h, :, lanes]
        if drop is not None:
            base = jnp.where(drop, -MASKED, base)
        pt = jnp.exp(st - base)
        dp = nn(block, do)
        ds = (pt * (dp - r.delta[h, :, lanes])).astype(BF16)
        r.dq[h, :, lanes] += tn(block, ds)[0:64]
        return nt(ds, q) + nt(pt.astype(BF16), do)

    def visit_back(i, carry):
        j = plane.index(pick(i, [o[0] for o in BACKWARD]), pick(i, [o[1] for o in BACKWARD]))

        @pl.when(j < p)
        def _():
            r.sent[j, :, PIECE:T, :] = jnp.zeros((KV, PIECE, 128), BF16)

        @pl.when((j < p) & (j > 0))
        def _():
            for h in range(KV):
                r.sent[j, h, 0:PIECE, :] = back(r.kva[j, h, 0:PIECE, :], h, every, None, None).astype(BF16)

        @pl.when((j < p) & (j == 0))
        def _():
            keep = first_mask(r.qstart[...])
            for h in range(KV):
                r.sent[0, h, 0:PIECE, :] = back(r.kva[0, h, 0:PIECE, :], h, every, keep, None).astype(BF16)

        @pl.when(j > p)
        def _():
            drop = r.qstart[:, late] >= PIECE
            for h in range(KV):
                r.sent[j, h] = back(r.kva[j, h], h, late, None, drop).astype(BF16)

        for k, offset in enumerate(BACKWARD):
            if k:
                @pl.when(i == k)
                def _():
                    sumk.event(*offset)
                    fold2(*offset)
                    sum2.event(*offset)

        return carry

    lax.fori_loop(1, 16, visit_back, 0)
    mask = allowed()
    for h in range(KV):
        r.dkv[h] = back(r.kva[p, h], h, every, mask, None)
    for n, buf in ((4, r.kvp_.at[0]), (8, r.kvm_.at[0]), (0, r.kup_), (1, r.kum_)):
        sumk.copy(n).wait_recv()
        r.dkv[...] += buf[...].astype(F32)

    fold2(0, 0)
    sum2.event(0, 0)
    parts, vals = [], []
    for h in range(HEADS):
        kvh, gi = h // 3, h % 3
        part = jnp.concatenate(
            [r.dq[kvh, :, q * 384 + gi * 128 : q * 384 + gi * 128 + 128] for q in range(2)], axis=1
        )
        parts.append(unrot(part * 0.125))
    for h in range(KV):
        both = r.dkv[h].T
        parts.append(unrot(both[0:64]))
        vals.append(both[64:128])
    dz = jnp.concatenate(parts + vals, axis=0).astype(BF16)
    dzp = nn(r.sprt[...], dz).astype(BF16)
    dh1 = tn(dzp, r.g1[...].reshape(1024, D))
    n1 = r.x_s[...] * inv1
    gsum1 = jnp.sum(dh1 * n1, axis=0, keepdims=True)
    r.gain_s[3] = jnp.broadcast_to(gsum1, (8, D))
    gain_sum = nn((jnp.concatenate([r.gain_s[3]] * 4, axis=0) * r.owner[...]).astype(BF16), r.fold[...])
    r.g1[...] = (nn(dzp, r.h1[...]) + place_row(30, gain_sum)).astype(BF16).reshape(32, 32, D)
    copy1, fold1 = folder(r.g1, r.r1, r.d1fold)
    sum1 = reducer(r.g1, (r.ava, r.avb, r.avp, r.avm, r.aua, r.aub, r.aup, r.aum), r.d1sem, 16)
    for du, dv in order:
        copy1(dv, du).start()
    sum2.end()
    total2 = r.g2[s].astype(F32)
    down2 = jnp.concatenate([total2[128 + 32 * k : 160 + 32 * k, 0:512] for k in range(3)], axis=1)
    for k in range(4):
        r.zs2[k] = total2[0:128, 144 * k : 144 * k + 144].astype(BF16)
        r.zd2[k] = down2[:, 384 * k : 384 * k + 384].astype(BF16)
    z2 = SumZ(b, s, [
        (r.zs2, (r.zs2p, r.zs2m, r.zs2a, r.zs2b)), (r.zd2, (r.zd2p, r.zd2m, r.zd2a, r.zd2b)),
    ], r.z2sem)
    z2.begin()
    g1v = dh1 * r.gain_s[0, 0:1, :]
    tg = r.mix_s[...] + inv1 * (g1v - n1 * (jnp.sum(g1v * n1, axis=-1, keepdims=True) * (1.0 / D)))
    for q in range(2):
        r.tgrad[q] = tg[PIECE * q : PIECE * (q + 1), :].T.astype(BF16)
    homeward(3, r.tgrad, r.tgrad_o, *begin)
    for offset in order:
        fold1(*offset)
        sum1.event(*offset)
        if offset == (0, 3):
            z2.middle()
    sum1.end()
    total1 = r.g1[s].astype(F32)
    for k in range(4):
        r.zs1[k] = total1[:, 144 * k : 144 * k + 144].astype(BF16)
    z1 = SumZ(b, s, [(r.zs1, (r.zs1p, r.zs1m, r.zs1a, r.zs1b))], r.z1sem)
    z1.begin()
    raw2, down_sum = z2.result()
    r.raw_o[32:160, :] = raw2
    r.down_o[...] = down_sum
    z1.middle()
    r.raw_o[0:32, :] = z1.result()[0]
    for offset in order:
        copy2(*offset).wait_send()
        copy1(*offset).wait_send()
    for part in (sumk, sum2, sum1, z2, z1):
        part.finish()
    for k, src, dst in ((2, r.mixed, r.mixed_o), (3, r.tgrad, r.tgrad_o)):
        homeward(k, src, dst, *ended)
        homeward_wait(k, src, dst)


def layer_call(shards, tokens, cot, tables, constants):
    any_ = pl.BlockSpec(memory_space=pl.ANY)
    vm = pl.BlockSpec(memory_space=pltpu.VMEM)
    return pl.pallas_call(
        layer_kernel,
        out_shape=(
            jax.ShapeDtypeStruct((2, D, PIECE), BF16),
            jax.ShapeDtypeStruct((2, D, PIECE), BF16),
            jax.ShapeDtypeStruct((160, 144), F32),
            jax.ShapeDtypeStruct((32, 384), F32),
        ),
        in_specs=[vm] * 8 + [any_] * 2 + [vm] * 5 + [any_] * 3,
        out_specs=(any_, any_, vm, vm),
        scratch_shapes=[pltpu.VMEM(shape, kind) for shape, kind in SCRATCH.values()]
        + [pltpu.SemaphoreType.DMA(shape) for shape in SEMS.values()],
        compiler_params=pltpu.CompilerParams(
            collective_id=0, has_side_effects=True, vmem_limit_bytes=VLIMIT
        ),
        name="decoder_layer",
    )(*shards, tokens, cot, *tables, *constants)


def finish_kernel(mixed, tgrad, raw, down, mixed_o, tgrad_o, g1, wq, wk, wv, wo, g2, wg, wu, wd):
    mixed_o[...] = mixed[...]
    tgrad_o[...] = tgrad[...]
    g1[...] = raw[30:31, 0:18]
    g2[...] = raw[50:51, 0:18]
    for at, ref in ((0, wq), (18, wk), (24, wv), (32, wo), (64, wg), (112, wu)):
        ref[...] = raw[at : at + ref.shape[0], :]
    wd[...] = down[0:18, :]


def finish_call(mixed, tgrad, raw, down):
    vm = pl.BlockSpec(memory_space=pltpu.VMEM)
    shapes = [(1, 18), (18, 144), (6, 144), (6, 144), (18, 144), (1, 18), (48, 144), (48, 144), (18, 384)]
    return pl.pallas_call(
        finish_kernel,
        out_shape=tuple([jax.ShapeDtypeStruct((2, D, PIECE), BF16)] * 2 + [jax.ShapeDtypeStruct(n, F32) for n in shapes]),
        in_specs=[vm] * 4,
        out_specs=(vm,) * 11,
        name="write_outputs",
    )(mixed, tgrad, raw, down)


def body(
    tokens, doc_lengths, first_gain, query_weight, key_matrix, value_matrix,
    output_weight, second_gain, gate_weight, up_weight, down_weight, cotangent,
):
    s = lax.axis_index("seq")
    c, p = s % 2, s // 2
    gains = jnp.stack([first_gain, second_gain])
    spread = jnp.asarray(spread_matrix())
    sprt = jnp.asarray(spread_matrix().T.copy())
    fold, owner = (jnp.asarray(m) for m in gain_matrix())

    lens = lax.dynamic_index_in_dim(doc_lengths[:, 0, :], c, 0, False)
    starts = [jnp.zeros((), jnp.int32), lens[0], lens[0] + lens[1]]
    at = jnp.arange(PIECE, dtype=jnp.int32)
    spots = jnp.stack([p * PIECE + at, (31 - p) * PIECE + at])
    begins = jnp.where(spots >= starts[2], starts[2], jnp.where(spots >= starts[1], starts[1], 0))
    rates = THETA ** (-2.0 * jnp.arange(HD // 2, dtype=F32) / HD)
    angles = (spots - begins).reshape(T).astype(F32)[None, :] * rates[:, None]
    cos, sin = jnp.cos(angles), jnp.sin(angles)
    qpos = jnp.broadcast_to(spots[:, None], (2, 3, PIECE)).reshape(1, LANES)
    qstart = jnp.broadcast_to(begins[:, None], (2, 3, PIECE)).reshape(1, LANES)

    shards = [
        query_weight.T, key_matrix.T, value_matrix.T, output_weight.T,
        gate_weight.T, up_weight.T, down_weight.T, gains,
    ]
    turn = lambda a: jnp.swapaxes(a[:, 0], 1, 2)
    mixed, tgrad, raw, down = layer_call(
        shards, turn(tokens), turn(cotangent), (cos, sin, qpos, qstart, owner), (spread, sprt, fold)
    )
    mixed, tgrad, g1, wq, wk, wv, wo, g2, wg, wu, wd = finish_call(mixed, tgrad, raw, down)
    back = lambda a: jnp.swapaxes(a, 1, 2)[:, None]
    return (
        back(mixed), back(tgrad), g1.reshape(18), wq.T, wk.T, wv.T, wo.T, g2.reshape(18), wg.T, wu.T, wd.T,
    )


def solution(mesh):
    weight = P("batch", "seq")
    rows = P(None, "batch", "seq", None)
    return jax.shard_map(
        body,
        mesh=mesh,
        in_specs=(
            rows, P(None, "batch", None), P("seq"), weight, weight, weight, weight,
            P("seq"), weight, weight, weight, rows,
        ),
        out_specs=(
            rows, rows, P("seq"), weight, weight, weight, weight,
            P("seq"), weight, weight, weight,
        ),
        check_vma=False,
    )
```

```python
import numpy as np
import ml_dtypes
import jax
import jax.numpy as jnp
from jax import lax
from jax.experimental import pallas as pl
from jax.experimental.pallas import tpu as pltpu
from jax.sharding import PartitionSpec as P

D = 576
HEADS = 9
KV = 3
HD = 64
FF = 1536
PIECE = 128
T = 2 * PIECE
LANES = 3 * T
EPS = 1e-05
THETA = 100000.0
MASKED = -1e30
MESH = pl.DeviceIdType.MESH
F32 = jnp.float32
BF16 = jnp.bfloat16
VLIMIT = 58 * 1024 * 1024


def spread_matrix():
    m = np.zeros((960, 1024), np.float32)
    n = np.arange(576)
    m[n, 32 * (n // 18) + n % 18] = 1
    n = np.arange(192)
    m[576 + n, 32 * (n // 6) + 18 + n % 6] = 1
    m[768 + n, 32 * (n // 6) + 24 + n % 6] = 1
    return m.astype(ml_dtypes.bfloat16)


def gain_matrix():
    n = np.arange(576)
    fold = np.zeros((576, 576), np.float32)
    for b in range(4):
        fold[n, 144 * b + n % 18] = 1
    owner = (n[None, :] // 18 == np.arange(32)[:, None]).astype(np.float32)
    return fold.astype(ml_dtypes.bfloat16), owner


def nn(a, b):
    return lax.dot_general(a, b, (((1,), (0,)), ((), ())), preferred_element_type=F32)


def nt(a, b):
    return lax.dot_general(a, b, (((1,), (1,)), ((), ())), preferred_element_type=F32)


def tn(a, b):
    return lax.dot_general(a, b, (((0,), (0,)), ((), ())), preferred_element_type=F32)


def rcopy(src, dst, ss, rs, dev):
    return pltpu.make_async_remote_copy(
        src_ref=src, dst_ref=dst, send_sem=ss, recv_sem=rs, device_id=dev, device_id_type=MESH
    )


def place():
    b = lax.axis_index("batch")
    s = lax.axis_index("seq")
    c = lax.rem(s, 2)
    p = lax.div(s, 2)
    return b, s, c, p, lax.div(p, 4), lax.rem(p, 4)


def chip_of(piece):
    i = jnp.minimum(piece, 31 - piece)
    half = lax.div(i, 2)
    return jnp.where(lax.rem(i, 2) == 0, half, 15 - half)


def early_piece(chip):
    return jnp.where(chip < 8, 2 * chip, 31 - 2 * chip)


def seq_of(y, x, c):
    return (y * 4 + x) * 2 + c


def hop(i, d):
    return lax.rem(i + d, 4)


def hail(devices):
    bar = pltpu.get_barrier_semaphore()
    for dev in devices:
        pl.semaphore_signal(bar, inc=1, device_id=dev, device_id_type=MESH)
    return bar


def neighbours(b, s, c, y, x):
    found = [(b, seq_of(y, x, 1 - c))]
    for d in (1, 2, 3):
        found += [
            (hop(b, d), s),
            (b, seq_of(y, hop(x, d), c)),
            (b, seq_of(hop(y, d), x, c)),
        ]
    return found


class Ring:
    def __init__(self, dev, ss, rs, direct=False):
        self.dev, self.ss, self.rs, self.direct = dev, ss, rs, direct

    def copy(self, n, src, dst):
        if n == 2 and self.direct:
            return rcopy(src, dst, self.ss.at[n], self.rs.at[n], self.dev(2, 0))
        du, dv = {0: (1, 0), 1: (3, 0), 2: (1, 0), 3: (3, 0)}.get(n, (0, 1 if n // 4 in (1, 3) else 3))
        return rcopy(src, dst, self.ss.at[n], self.rs.at[n], self.dev(du, dv))


def token_rows(ref):
    return jnp.concatenate([ref[0].astype(F32).T, ref[1].astype(F32).T], axis=0)


def gain_row(blocks, row, fold, owner):
    at = lax.broadcasted_iota(jnp.int32, (32, 1024), 0) * 32 + row
    one = (lax.broadcasted_iota(jnp.int32, (32, 1024), 1) == at).astype(F32).astype(BF16)
    spread = nt(nn(one, blocks[:, 0:128]).astype(BF16), fold[:, 0:128])
    return jnp.sum(spread * owner, axis=0, keepdims=True)


def place_row(row, values):
    at = lax.broadcasted_iota(jnp.int32, (1024, 32), 1) * 32 + row
    one = (lax.broadcasted_iota(jnp.int32, (1024, 32), 0) == at).astype(F32).astype(BF16)
    return nn(one, values.astype(BF16))


def diagonal_mask(p, qpos, qstart):
    row = lax.broadcasted_iota(jnp.int32, (T, 1), 0)
    kpos = jnp.where(row < PIECE, p * PIECE + row, (31 - p) * PIECE + row - PIECE)
    return (kpos <= qpos) & (kpos >= qstart)


def first_mask(qstart):
    row = lax.broadcasted_iota(jnp.int32, (PIECE, 1), 0)
    return row >= qstart


def pick(i, values):
    found = values[0]
    for k, value in enumerate(values[1:]):
        found = jnp.where(i == k + 1, value, found)
    return found


FORWARD = ((0, 0), (3, 0), (1, 0), (0, 3), (0, 1), (2, 0), (3, 3), (3, 1), (1, 3), (1, 1), (2, 3), (2, 1), (0, 2), (3, 2), (1, 2), (2, 2))
BACKWARD = ((0, 0), (2, 2), (1, 2), (3, 2), (0, 2), (2, 1), (2, 3), (1, 1), (1, 3), (3, 1), (3, 3), (0, 1), (0, 3), (2, 0), (1, 0), (3, 0))
HALVES = (pl.ds(0, PIECE), pl.ds(PIECE, PIECE))


ROWS = 224


class Plane:
    def __init__(self):
        self.b, self.s, self.c, self.p, self.y, self.x = place()
        c, y, x = self.c, self.y, self.x
        self.u, self.v = jnp.where(c == 0, x, y), jnp.where(c == 0, y, x)
        self.su, self.sv = 1 + 3 * c, 4 - 3 * c
        self.other = (self.b, seq_of(y, x, 1 - c))

    def index(self, du, dv):
        return lax.rem(self.u + du, 4) * self.su + lax.rem(self.v + dv, 4) * self.sv

    def dev(self, du, dv):
        return (self.b, 2 * self.index(du, dv) + self.c)

    def common(self, du, dv):
        return du * self.su + dv * self.sv


class Gather:
    def __init__(self, plane, view, own, sems, swap=None, direct=False):
        self.ring = Ring(plane.dev, sems.at[0], sems.at[1], direct)
        self.view, self.own, self.swap = view, own, swap
        self.later = []

    def copy(self, n, du, dv, part=None):
        ref = self.view(du, dv, part)
        return self.ring.copy(n, self.own if (du, dv) == (0, 0) else ref, ref)

    def send(self, *item):
        self.copy(*item).start()
        self.later.append(item)

    def arrive(self, n, du, dv, part=None):
        ref = self.view(du, dv, part)
        self.ring.copy(n, ref, ref).wait_recv()

    def done(self, du, dv):
        if self.swap is not None:
            self.swap(du, dv).start()

    def begin_u(self):
        self.send(0, 0, 0)
        self.send(1, 0, 0)
        if self.ring.direct:
            self.send(2, 0, 0)

    def begin_v(self):
        self.send(4, 0, 0)
        self.send(8, 0, 0)
        self.done(0, 0)

    def near(self):
        for n, du in ((0, 3), (1, 1)):
            self.arrive(n, du, 0)
            if not self.ring.direct:
                self.send(2 + n, du, 0, n)
            self.send(4 + du, du, 0)
            self.send(8 + du, du, 0)
            self.done(du, 0)

    def far(self):
        if self.ring.direct:
            self.arrive(2, 2, 0)
        else:
            self.arrive(2, 2, 0, 0)
            self.arrive(3, 2, 0, 1)
        self.send(6, 2, 0)
        self.send(10, 2, 0)
        self.done(2, 0)

    def line(self, w):
        self.arrive(4 + w, w, 3)
        self.send(12 + w, w, 3, 0)
        self.done(w, 3)
        self.arrive(8 + w, w, 1)
        self.send(16 + w, w, 1, 1)
        self.done(w, 1)

    def last(self, w):
        self.arrive(12 + w, w, 2, 0)
        self.arrive(16 + w, w, 2, 1)
        self.done(w, 2)

    def finish(self):
        for item in self.later:
            self.copy(*item).wait_send()
        if self.swap is not None:
            for du in range(4):
                for dv in range(4):
                    self.swap(du, dv).wait()


class Reduce:
    def __init__(self, plane, view, add, bufs, sems, direct=False):
        self.ring = Ring(plane.dev, sems.at[0], sems.at[1], direct)
        self.view, self.add = view, add
        va, vb, vp, vm, ua, ub, up, um = bufs
        self.pieces = {
            2: (2, 0, 0, ua), 3: (2, 0, 1, ub), 0: (1, 0, None, up), 1: (3, 0, None, um),
        }
        if direct:
            self.pieces[2] = (2, 0, None, ua)
            del self.pieces[3]
        for w in range(4):
            self.pieces[12 + w] = (w, 2, 0, va.at[w])
            self.pieces[16 + w] = (w, 2, 1, vb.at[w])
            self.pieces[4 + w] = (w, 1, None, vp.at[w])
            self.pieces[8 + w] = (w, 3, None, vm.at[w])

    def copy(self, n):
        du, dv, part, dst = self.pieces[n]
        return self.ring.copy(n, self.view(du, dv, part), dst)

    def take(self, n, du, dv, part=None):
        self.copy(n).wait_recv()
        self.add(du, dv, part, self.pieces[n][3])

    def event(self, du, dv):
        if dv == 2:
            self.copy(12 + du).start()
            self.copy(16 + du).start()
        elif dv == 1:
            self.take(12 + du, du, 1, 0)
            self.copy(4 + du).start()
        elif dv == 3:
            self.take(16 + du, du, 3, 1)
            self.copy(8 + du).start()
        else:
            self.take(4 + du, du, 0)
            self.take(8 + du, du, 0)
            if self.ring.direct:
                if du:
                    self.copy({1: 0, 2: 2, 3: 1}[du]).start()
            elif du == 2:
                self.copy(2).start()
                self.copy(3).start()
            elif du == 1:
                self.take(2, 1, 0, 0)
                self.copy(0).start()
            elif du == 3:
                self.take(3, 3, 0, 1)
                self.copy(1).start()

    def end(self):
        self.take(0, 0, 0)
        self.take(1, 0, 0)
        if self.ring.direct:
            self.take(2, 0, 0)

    def finish(self):
        for n in self.pieces:
            self.copy(n).wait_send()


class SumZ:
    def __init__(self, b, s, items, sems):
        self.b, self.s, self.items, self.sems = b, s, items, sems

    def copies(self, n):
        at = hop(self.b, 2 if n > 1 else 1 + 2 * n)
        dev = (hop(self.b, 1 if n in (0, 2) else 3), self.s)
        found = []
        for k, (ref, bufs) in enumerate(self.items):
            size = ref.shape[1] // 2
            src = ref.at[at] if n < 2 else ref.at[at, pl.ds(size * (n - 2), size)]
            found.append(rcopy(src, bufs[n], self.sems.at[0, k, n], self.sems.at[1, k, n], dev))
        return found

    def start(self, n):
        for cp in self.copies(n):
            cp.start()

    def begin(self):
        self.start(2)
        self.start(3)

    def middle(self):
        for n in (2, 3):
            for cp in self.copies(n):
                cp.wait_recv()
            at = hop(self.b, 1 if n == 2 else 3)
            for ref, bufs in self.items:
                size = ref.shape[1] // 2
                part = (at, pl.ds(size * (n - 2), size))
                ref[part] = ref[part] + bufs[n][...]
            self.start(n - 2)

    def result(self):
        for n in (0, 1):
            for cp in self.copies(n):
                cp.wait_recv()
        found = []
        for ref, bufs in self.items:
            found.append(ref[self.b].astype(F32) + bufs[0][...].astype(F32) + bufs[1][...].astype(F32))
        return found

    def finish(self):
        for n in range(4):
            for cp in self.copies(n):
                cp.wait_send()


SCRATCH = {
    "spread": ((960, 1024), BF16), "sprt": ((1024, 960), BF16), "fold": ((D, D), BF16),
    "raw_f": ((160, 144), F32), "dwn_f": ((32, 384), F32),
    "za": ((4, 160, 144), BF16), "zd": ((4, 32, 384), BF16),
    "blk1": ((32, D), BF16), "blk2": ((ROWS, D), BF16),
    "g1": ((32, 32, D), BF16), "g2": ((32, ROWS, D), BF16),
    "tok": ((2, D, PIECE), BF16), "cot": ((2, D, PIECE), BF16),
    "qpos": ((1, LANES), jnp.int32), "qstart": ((1, LANES), jnp.int32), "gain_s": ((4, 8, D), F32), "x_s": ((T, D), F32), "h1": ((T, D), BF16),
    "kv": ((KV, T, 128), BF16), "qt": ((KV, 128, LANES), BF16), "dot": ((KV, 128, LANES), BF16),
    "kva": ((16, KV, T, 128), BF16),
    "m_s": ((KV, 1, LANES), F32), "l_s": ((KV, 1, LANES), F32), "delta": ((KV, 1, LANES), F32),
    "acc": ((KV, HD, LANES), F32), "dq": ((KV, HD, LANES), F32), "dkv": ((KV, T, 128), F32),
    "wd_s": ((D, FF), BF16), "act_s": ((T, FF), BF16), "wo_s": ((D, D), BF16),
    "h2_s": ((T, D), BF16), "dh2_s": ((T, D), F32), "mix_s": ((T, D), F32),
    "mixed": ((2, D, PIECE), BF16), "tgrad": ((2, D, PIECE), BF16),
    "sent": ((16, KV, T, 128), BF16),
    "kva_": ((4, KV, PIECE, 128), BF16), "kvb_": ((4, KV, PIECE, 128), BF16),
    "kvp_": ((4, KV, T, 128), BF16), "kvm_": ((4, KV, T, 128), BF16),
    "kua_": ((KV, PIECE, 128), BF16), "kub_": ((KV, PIECE, 128), BF16),
    "kup_": ((KV, T, 128), BF16), "kum_": ((KV, T, 128), BF16),
    "r2": ((16, ROWS, D), BF16),
    "wva": ((4, ROWS // 2, D), BF16), "wvb": ((4, ROWS // 2, D), BF16),
    "wvp": ((4, ROWS, D), BF16), "wvm": ((4, ROWS, D), BF16),
    "wua": ((ROWS // 2, D), BF16), "wub": ((ROWS // 2, D), BF16),
    "wup": ((ROWS, D), BF16), "wum": ((ROWS, D), BF16),
    "r1": ((16, 32, D), BF16),
    "ava": ((4, 16, D), BF16), "avb": ((4, 16, D), BF16),
    "avp": ((4, 32, D), BF16), "avm": ((4, 32, D), BF16),
    "aua": ((32, D), BF16), "aub": ((16, D), BF16),
    "aup": ((32, D), BF16), "aum": ((32, D), BF16),
    "zs2": ((4, 128, 144), BF16), "zd2": ((4, 32, 384), BF16), "zs1": ((4, 32, 144), BF16),
    "zs2p": ((128, 144), BF16), "zs2m": ((128, 144), BF16), "zs2a": ((64, 144), BF16), "zs2b": ((64, 144), BF16),
    "zd2p": ((32, 384), BF16), "zd2m": ((32, 384), BF16), "zd2a": ((16, 384), BF16), "zd2b": ((16, 384), BF16),
    "zs1l": ((3, 32, 144), BF16),
}
SEMS = {
    "lsem": (4,), "zsem": (2, 2, 4), "zz": (4, 2, 2), "zl": (4,),
    "g1sem": (2, 20), "g1swap": (2, 16), "g2sem": (2, 20), "g2swap": (2, 16), "kvsem": (2, 20),
    "dksem": (2, 20), "d2fold": (2, 16), "d2sem": (2, 20), "d1fold": (2, 16), "d1sem": (2, 20),
    "z2sem": (2, 2, 4), "z1sem": (2, 4), "zasem": (2, 4),
}
INPUTS = (
    "wq", "wk", "wv", "wo", "wg", "wu", "wd", "gains", "tokens", "cotin", "cos", "sin", "begins",
    "owner", "spread_in", "sprt_in", "fold_in",
)
OUTPUTS = ("mixed_o", "tgrad_o", "raw_o", "down_o")


class Refs:
    def __init__(self, refs):
        for name, ref in zip((*INPUTS, *OUTPUTS, *SCRATCH, *SEMS), refs, strict=True):
            setattr(self, name, ref)


def layer_kernel(*refs):
    r = Refs(refs)
    plane = Plane()
    b, s, c, p, y, x = plane.b, plane.s, plane.c, plane.p, plane.y, plane.x
    target = 2 * chip_of(s)
    slot = lax.div(s, 16)
    e = early_piece(p)
    bar = hail(neighbours(b, s, c, y, x))
    around = [target, target + 1, e, 31 - e]
    for peer in around:
        @pl.when(peer != s)
        def _():
            pl.semaphore_signal(bar, inc=1, device_id=(b, peer), device_id_type=MESH)
    constants = [
        pltpu.make_async_copy(src, dst, r.lsem.at[k])
        for k, (src, dst) in enumerate(((r.spread_in, r.spread), (r.sprt_in, r.sprt), (r.fold_in, r.fold)))
    ]
    for cp in constants:
        cp.start()
    for lane in range(0, LANES, PIECE):
        q = lane // 384
        at = (31 - e if q else e) * PIECE
        r.qpos[:, lane : lane + PIECE] = at + lax.broadcasted_iota(jnp.int32, (1, PIECE), 1)
        r.qstart[:, lane : lane + PIECE] = r.begins[q : q + 1, :]
    r.raw_f[...] = jnp.zeros_like(r.raw_f)
    r.dwn_f[...] = jnp.zeros_like(r.dwn_f)
    for at, ref in ((0, r.wq), (18, r.wk), (24, r.wv), (32, r.wo), (64, r.wg), (112, r.wu)):
        r.raw_f[at : at + ref.shape[0], :] = ref[...].astype(F32)
    r.raw_f[30:32, 0:18] = r.gains[...].astype(F32)
    r.dwn_f[0:18, :] = r.wd[...].astype(F32)
    r.za[pl.ds(b, 1)] = r.raw_f[...].astype(BF16)[None]
    r.zd[pl.ds(b, 1)] = r.dwn_f[...].astype(BF16)[None]
    peers = 10
    for peer in around:
        peers = peers + jnp.where(peer != s, 1, 0)
    pl.semaphore_wait(bar, peers)

    def zcopies(n, at, part):
        dev = (hop(b, 1 if n in (0, 2) else 3), s)
        found = []
        for k, (ref, low, rows) in enumerate(((r.za, 32, 64), (r.zd, 0, 16))):
            view = ref.at[at, pl.ds(low, 2 * rows) if part is None else pl.ds(low + rows * part, rows)]
            found.append(rcopy(view, view, r.zsem.at[0, k, n], r.zsem.at[1, k, n], dev))
        return found

    def start(copies):
        for cp in copies:
            cp.start()

    def acopy(d, at):
        view = r.za.at[at, pl.ds(0, 32)]
        return rcopy(view, view, r.zasem.at[0, d], r.zasem.at[1, d], (hop(b, d), s))

    start([acopy(d, b) for d in (1, 2, 3)])
    zsent = [zcopies(0, b, None), zcopies(1, b, None)]
    start(zsent[0] + zsent[1])

    def outward(k, src_ref, dst_ref, act_remote, act_local):
        for m in (0, 1):
            dst = target + m

            @pl.when(dst != s)
            def _():
                act_remote(rcopy(src_ref.at[m], dst_ref.at[slot], r.zz.at[k, 0, m], r.zz.at[k, 1, slot], (b, dst)))

            @pl.when(dst == s)
            def _():
                act_local(pltpu.make_async_copy(src_ref.at[m], dst_ref.at[slot], r.zl.at[k]))

    def outward_wait(k, src_ref, dst_ref):
        for q, src in enumerate((e, 31 - e)):
            @pl.when(src != s)
            def _():
                rcopy(src_ref.at[0], dst_ref.at[q], r.zz.at[k, 0, 0], r.zz.at[k, 1, q], (b, src)).wait_recv()

    def homeward(k, src_ref, dst_ref, act_remote, act_local):
        for q, dst in enumerate((e, 31 - e)):
            @pl.when(dst != s)
            def _():
                act_remote(rcopy(src_ref.at[q], dst_ref.at[c], r.zz.at[k, 0, q], r.zz.at[k, 1, c], (b, dst)))

            @pl.when(dst == s)
            def _():
                act_local(pltpu.make_async_copy(src_ref.at[q], dst_ref.at[c], r.zl.at[k]))

    def homeward_wait(k, src_ref, dst_ref):
        for m in (0, 1):
            src = target + m

            @pl.when(src != s)
            def _():
                rcopy(src_ref.at[0], dst_ref.at[m], r.zz.at[k, 0, 0], r.zz.at[k, 1, m], (b, src)).wait_recv()

    begin = (lambda cp: cp.start(), lambda cp: cp.start())
    ended = (lambda cp: cp.wait_send(), lambda cp: cp.wait())
    outward(0, r.tokens, r.tok, *begin)

    for d in (1, 2, 3):
        acopy(d, hop(b, 4 - d)).wait_recv()
    r.blk1[...] = jnp.concatenate([r.za[i, 0:32, :].astype(F32) for i in range(4)], axis=1).astype(BF16)

    def weights(ref, own, sems, swap_sems, half, direct=False):
        def view(du, dv, part=None):
            at = 2 * plane.index(du, dv) + c
            return ref.at[at] if part is None else ref.at[at, pl.ds(half * part, half)]

        def swap(du, dv):
            n = plane.common(du, dv)
            dst = view(du, dv)
            src = own if (du, dv) == (0, 0) else dst
            return rcopy(src, dst, swap_sems.at[0, n], swap_sems.at[1, n], plane.other)

        return Gather(plane, view, own, sems, swap, direct)

    first = weights(r.g1, r.blk1, r.g1sem, r.g1swap, 16, True)
    second = weights(r.g2, r.blk2, r.g2sem, r.g2swap, ROWS // 2)
    first.begin_u()
    first.begin_v()
    r.g1[pl.ds(s, 1)] = r.blk1[...][None]
    for n, way in ((0, 3), (1, 1)):
        for cp in zcopies(n, hop(b, way), None):
            cp.wait_recv()
        zsent.append(zcopies(2 + n, hop(b, way), n))
        start(zsent[-1])
    first.near()
    first.line(0)
    first.far()
    for n in (2, 3):
        for cp in zcopies(n, hop(b, 2), n - 2):
            cp.wait_recv()
    down = jnp.concatenate([r.zd[i] for i in range(4)], axis=1)
    r.blk2[0:128, :] = jnp.concatenate([r.za[i, 32:160, :].astype(F32) for i in range(4)], axis=1).astype(BF16)
    r.blk2[128:224, 512:576] = jnp.zeros((96, 64), BF16)
    for k in range(3):
        r.blk2[128 + 32 * k : 160 + 32 * k, 0:512] = down[:, 512 * k : 512 * (k + 1)]
    second.begin_u()
    r.g2[pl.ds(s, 1)] = r.blk2[...][None]
    outward_wait(0, r.tokens, r.tok)
    outward(0, r.tokens, r.tok, *ended)
    r.x_s[...] = token_rows(r.tok)
    for w in (3, 1, 2):
        first.line(w)
    second.begin_v()
    for w in (0, 3, 1, 2):
        first.last(w)
    second.near()
    first.finish()
    for cp in constants:
        cp.wait()

    owner_rows = r.owner[...]
    fold = r.fold[...]
    wa = r.g1[...].reshape(1024, D)
    gain1 = gain_row(wa, 30, fold, owner_rows)
    r.gain_s[0] = jnp.broadcast_to(gain1, (8, D))
    r.gain_s[1] = jnp.broadcast_to(gain_row(wa, 31, fold, owner_rows), (8, D))
    xin = r.x_s[...]
    inv1 = lax.rsqrt(jnp.sum(xin * xin, axis=-1, keepdims=True) * (1.0 / D) + EPS)
    r.h1[...] = (xin * inv1 * gain1).astype(BF16)
    w_all = nn(r.spread[...], wa).astype(BF16)
    z = nt(w_all, r.h1[...])
    co, si = r.cos[...], r.sin[...]

    def rot(a):
        a1, a2 = a[0:32], a[32:64]
        return jnp.concatenate([a1 * co - a2 * si, a2 * co + a1 * si], axis=0)

    def unrot(a):
        a1, a2 = a[0:32], a[32:64]
        return jnp.concatenate([a1 * co + a2 * si, a2 * co - a1 * si], axis=0)

    for h in range(KV):
        kh = rot(z[576 + 64 * h : 640 + 64 * h])
        vh = z[768 + 64 * h : 832 + 64 * h]
        r.kv[h] = jnp.concatenate([kh, vh], axis=0).T.astype(BF16)

    def kview(ref):
        def view(du, dv, part=None):
            at = plane.index(du, dv)
            return ref.at[at] if part is None else ref.at[at, :, HALVES[part]]
        return view

    keys = Gather(plane, kview(r.kva), r.kv, r.kvsem)
    keys.begin_u()
    keys.begin_v()
    outward(1, r.cotin, r.cot, *begin)
    r.kva[pl.ds(p, 1)] = r.kv[...][None]
    for h in range(HEADS):
        q = (rot(z[64 * h : 64 * h + 64]).astype(BF16).astype(F32) * 0.125).astype(BF16)
        kvh, gi = h // 3, h % 3
        for piece in range(2):
            lane = piece * 384 + gi * 128
            r.qt[kvh, 0:64, lane : lane + 128] = q[:, piece * 128 : piece * 128 + 128]
    for h in range(KV):
        r.qt[h, 64:128, :] = jnp.zeros((64, LANES), BF16)
        r.dot[h, 0:64, :] = jnp.zeros((64, LANES), BF16)

    r.m_s[...] = jnp.full_like(r.m_s, MASKED)
    r.l_s[...] = jnp.zeros_like(r.l_s)
    r.acc[...] = jnp.zeros_like(r.acc)
    every = pl.ds(0, LANES)
    late = pl.ds(384, 384)

    def step(block, h, lanes, mask, drop):
        st = nn(block, r.qt[h, :, lanes])
        if mask is not None:
            st = jnp.where(mask, st, MASKED)
        m_old = r.m_s[h, :, lanes]
        top = jnp.max(st, axis=0, keepdims=True)
        if drop is None:
            m_new = jnp.maximum(m_old, top)
            m_sub = m_new
        else:
            m_new = jnp.maximum(m_old, jnp.where(drop, MASKED, top))
            m_sub = jnp.where(drop, -MASKED, m_new)
        pt = jnp.exp(st - m_sub)
        a = jnp.exp(m_old - m_new)
        r.m_s[h, :, lanes] = m_new
        r.l_s[h, :, lanes] = r.l_s[h, :, lanes] * a + jnp.sum(pt, axis=0, keepdims=True)
        r.acc[h, :, lanes] = r.acc[h, :, lanes] * a + tn(block, pt.astype(BF16))[64:128]

    def allowed():
        return diagonal_mask(e, r.qpos[...], r.qstart[...])

    mask = allowed()
    for h in range(KV):
        step(r.kv[h], h, every, mask, None)

    events = {
        1: [keys.near, lambda: second.line(0)], 2: [lambda: keys.line(0)], 3: [keys.far, second.far],
        4: [lambda: keys.line(3)], 5: [lambda: keys.line(1)], 6: [lambda: second.line(3)], 7: [lambda: keys.line(2)],
        8: [lambda: second.line(1)], 10: [lambda: second.line(2)], 12: [lambda: keys.last(0)], 13: [lambda: keys.last(3)],
        14: [lambda: keys.last(1), lambda: second.last(0)], 15: [lambda: keys.last(2)],
    }

    def visit(i, carry):
        for k, todo in events.items():
            @pl.when(i == k)
            def _():
                for event in todo:
                    event()

        j = plane.index(pick(i, [o[0] for o in FORWARD]), pick(i, [o[1] for o in FORWARD]))
        ej = early_piece(j)

        @pl.when((ej < e) & (j > 0))
        def _():
            for h in range(KV):
                step(r.kva[j, h, 0:PIECE, :], h, every, None, None)

        @pl.when((ej < e) & (j == 0))
        def _():
            keep = first_mask(r.qstart[...])
            for h in range(KV):
                step(r.kva[0, h, 0:PIECE, :], h, every, keep, None)

        @pl.when(ej > e)
        def _():
            drop = r.qstart[:, late] >= PIECE
            for h in range(KV):
                step(r.kva[j, h], h, late, None, drop)

        return carry

    lax.fori_loop(1, 16, visit, 0)
    for h in range(KV):
        total = r.l_s[h]
        r.acc[h] = r.acc[h] / total
        r.m_s[h] = r.m_s[h] + jnp.log(total)
    rows = []
    for h in range(HEADS):
        kvh, gi = h // 3, h % 3
        rows.append(
            jnp.concatenate(
                [r.acc[kvh, :, q * 384 + gi * 128 : q * 384 + gi * 128 + 128] for q in range(2)], axis=1
            )
        )
    att_t = jnp.concatenate(rows, axis=0).T.astype(BF16)
    outward_wait(1, r.cotin, r.cot)
    outward(1, r.cotin, r.cot, *ended)
    dy = token_rows(r.cot).astype(BF16)
    dyt_rows = jnp.concatenate([r.cot[0], r.cot[1]], axis=1)
    for w in (3, 1, 2):
        second.last(w)
    keys.finish()
    second.finish()
    for group in zsent + [[acopy(d, b) for d in (1, 2, 3)]]:
        for cp in group:
            cp.wait_send()

    p2 = r.spread[0:576, :]
    p2t = r.sprt[:, 0:576]
    r.wo_s[...] = nn(p2, r.g2[:, 0:32, :].reshape(1024, D)).astype(BF16)
    for k in range(3):
        third = r.g2[:, 128 + 32 * k : 160 + 32 * k, 0:512].reshape(1024, 512)
        r.wd_s[:, 512 * k : 512 * k + 512] = nn(p2, third).astype(BF16)
    middle = r.x_s[...] + nt(att_t, r.wo_s[...])
    inv2 = lax.rsqrt(jnp.sum(middle * middle, axis=-1, keepdims=True) * (1.0 / D) + EPS)
    n2 = middle * inv2
    r.h2_s[...] = (n2 * r.gain_s[1, 0:1, :]).astype(BF16)
    r.mix_s[...] = middle
    r.dh2_s[...] = jnp.zeros_like(r.dh2_s)

    def chunk(f, carry):
        at = pl.ds(8 * f, 8)
        lanes = pl.ds(pl.multiple_of(384 * f, 128), 384)
        wg = r.g2[at, 32:80, :].reshape(384, D)
        wu = r.g2[at, 80:128, :].reshape(384, D)
        h2 = r.h2_s[...]
        gate = nt(h2, wg)
        up = nt(h2, wu)
        sig = 1.0 / (1.0 + jnp.exp(-gate))
        silu = gate * sig
        act = (silu * up).astype(BF16)
        r.act_s[:, lanes] = act
        wdf = r.wd_s[:, lanes]
        r.mix_s[...] += nt(act, wdf)
        da = nn(dy, wdf)
        dup = (da * silu).astype(BF16)
        dgate = (da * up * sig * (1.0 + gate * (1.0 - sig))).astype(BF16)
        r.dh2_s[...] += nn(dgate, wg) + nn(dup, wu)
        r.g2[at, 32:80, :] = tn(dgate, h2).astype(BF16).reshape(8, 48, D)
        r.g2[at, 80:128, :] = tn(dup, h2).astype(BF16).reshape(8, 48, D)
        return carry

    lax.fori_loop(0, 4, chunk, 0)
    for q in range(2):
        r.mixed[q] = r.mix_s[PIECE * q : PIECE * (q + 1), :].T.astype(BF16)
    homeward(2, r.mixed, r.mixed_o, *begin)
    dyt = nn(p2t, dyt_rows).astype(BF16)
    r.g2[:, 128:224, 512:576] = jnp.zeros((32, 96, 64), BF16)
    for k in range(3):
        part = nn(dyt, r.act_s[:, 512 * k : 512 * k + 512]).astype(BF16)
        r.g2[:, 128 + 32 * k : 160 + 32 * k, 0:512] = part.reshape(32, 32, 512)
    dh2 = r.dh2_s[...]
    gsum = jnp.sum(dh2 * n2, axis=0, keepdims=True)
    r.gain_s[2] = jnp.broadcast_to(gsum, (8, D))
    gain = nn((jnp.concatenate([r.gain_s[2]] * 4, axis=0) * r.owner[...]).astype(BF16), r.fold[...])
    g2v = dh2 * r.gain_s[1, 0:1, :]
    dmid = dy.astype(F32) + inv2 * (g2v - n2 * (jnp.sum(g2v * n2, axis=-1, keepdims=True) * (1.0 / D)))
    r.mix_s[...] = dmid
    dbt = nn(p2t, dmid.T.astype(BF16)).astype(BF16)
    r.g2[:, 0:32, :] = (nn(dbt, att_t) + place_row(18, gain)).astype(BF16).reshape(32, 32, D)

    def folder(ref, land, sems):
        def copy(du, dv):
            at = plane.index(du, dv)
            n = plane.common(du, dv)
            return rcopy(ref.at[2 * at + 1 - c], land.at[at], sems.at[0, n], sems.at[1, n], plane.other)

        def fold_in(du, dv):
            copy(du, dv).wait_recv()
            at = plane.index(du, dv)
            ref[2 * at + c] = ref[2 * at + c] + land[at]

        return copy, fold_in

    def reducer(ref, bufs, sems, half, direct=False):
        def view(du, dv, part=None):
            at = 2 * plane.index(du, dv) + c
            return ref.at[at] if part is None else ref.at[at, pl.ds(half * part, half)]

        def add(du, dv, part, buf):
            at = 2 * plane.index(du, dv) + c
            where = (at,) if part is None else (at, pl.ds(half * part, half))
            ref[where] = ref[where] + buf[...]

        return Reduce(plane, view, add, bufs, sems, direct)

    copy2, fold2 = folder(r.g2, r.r2, r.d2fold)
    sum2 = reducer(r.g2, (r.wva, r.wvb, r.wvp, r.wvm, r.wua, r.wub, r.wup, r.wum), r.d2sem, ROWS // 2)
    order = BACKWARD[1:] + BACKWARD[:1]
    for du, dv in order:
        copy2(dv, du).start()
    datt = nn(dmid.astype(BF16), r.wo_s[...]).astype(BF16).astype(F32).T
    for h in range(HEADS):
        kvh, gi = h // 3, h % 3
        for q in range(2):
            lane = q * 384 + gi * 128
            part = datt[64 * h : 64 * h + 64, 128 * q : 128 * q + 128]
            r.dot[kvh, 64:128, lane : lane + 128] = part.astype(BF16)
            r.delta[kvh, :, lane : lane + 128] = jnp.sum(
                part * r.acc[kvh, :, lane : lane + 128], axis=0, keepdims=True
            )

    def add_keys(du, dv, part, buf):
        at = plane.index(du, dv)
        if part is None:
            r.sent[at] = r.sent[at] + buf[...]
        else:
            rows = slice(PIECE * part, PIECE * (part + 1))
            r.sent[at, :, rows, :] = r.sent[at, :, rows, :] + buf[...]

    sumk = Reduce(
        plane, kview(r.sent), add_keys,
        (r.kva_, r.kvb_, r.kvp_, r.kvm_, r.kua_, r.kub_, r.kup_, r.kum_), r.dksem,
    )
    r.dq[...] = jnp.zeros_like(r.dq)

    def back(block, h, lanes, mask, drop):
        q = r.qt[h, :, lanes]
        do = r.dot[h, :, lanes]
        st = nn(block, q)
        if mask is not None:
            st = jnp.where(mask, st, MASKED)
        base = r.m_s[h, :, lanes]
        if drop is not None:
            base = jnp.where(drop, -MASKED, base)
        pt = jnp.exp(st - base)
        dp = nn(block, do)
        ds = (pt * (dp - r.delta[h, :, lanes])).astype(BF16)
        r.dq[h, :, lanes] += tn(block, ds)[0:64]
        return nt(ds, q) + nt(pt.astype(BF16), do)

    def visit_back(i, carry):
        j = plane.index(pick(i, [o[0] for o in BACKWARD]), pick(i, [o[1] for o in BACKWARD]))
        ej = early_piece(j)

        @pl.when(ej < e)
        def _():
            r.sent[j, :, PIECE:T, :] = jnp.zeros((KV, PIECE, 128), BF16)

        @pl.when((ej < e) & (j > 0))
        def _():
            for h in range(KV):
                r.sent[j, h, 0:PIECE, :] = back(r.kva[j, h, 0:PIECE, :], h, every, None, None).astype(BF16)

        @pl.when((ej < e) & (j == 0))
        def _():
            keep = first_mask(r.qstart[...])
            for h in range(KV):
                r.sent[0, h, 0:PIECE, :] = back(r.kva[0, h, 0:PIECE, :], h, every, keep, None).astype(BF16)

        @pl.when(ej > e)
        def _():
            drop = r.qstart[:, late] >= PIECE
            for h in range(KV):
                r.sent[j, h] = back(r.kva[j, h], h, late, None, drop).astype(BF16)

        for k, offset in enumerate(BACKWARD):
            if k:
                @pl.when(i == k)
                def _():
                    sumk.event(*offset)
                    fold2(*offset)
                    sum2.event(*offset)

        return carry

    lax.fori_loop(1, 16, visit_back, 0)
    mask = allowed()
    for h in range(KV):
        r.dkv[h] = back(r.kva[p, h], h, every, mask, None)
    for n, buf in ((4, r.kvp_.at[0]), (8, r.kvm_.at[0]), (0, r.kup_), (1, r.kum_)):
        sumk.copy(n).wait_recv()
        r.dkv[...] += buf[...].astype(F32)

    fold2(0, 0)
    sum2.event(0, 0)
    parts, vals = [], []
    for h in range(HEADS):
        kvh, gi = h // 3, h % 3
        part = jnp.concatenate(
            [r.dq[kvh, :, q * 384 + gi * 128 : q * 384 + gi * 128 + 128] for q in range(2)], axis=1
        )
        parts.append(unrot(part * 0.125))
    for h in range(KV):
        both = r.dkv[h].T
        parts.append(unrot(both[0:64]))
        vals.append(both[64:128])
    dz = jnp.concatenate(parts + vals, axis=0).astype(BF16)
    dzp = nn(r.sprt[...], dz).astype(BF16)
    dh1 = tn(dzp, r.g1[...].reshape(1024, D))
    n1 = r.x_s[...] * inv1
    gsum1 = jnp.sum(dh1 * n1, axis=0, keepdims=True)
    r.gain_s[3] = jnp.broadcast_to(gsum1, (8, D))
    gain_sum = nn((jnp.concatenate([r.gain_s[3]] * 4, axis=0) * r.owner[...]).astype(BF16), r.fold[...])
    r.g1[...] = (nn(dzp, r.h1[...]) + place_row(30, gain_sum)).astype(BF16).reshape(32, 32, D)
    copy1, fold1 = folder(r.g1, r.r1, r.d1fold)
    sum1 = reducer(r.g1, (r.ava, r.avb, r.avp, r.avm, r.aua, r.aub, r.aup, r.aum), r.d1sem, 16, True)
    for du, dv in order:
        copy1(dv, du).start()
    sum2.end()
    total2 = r.g2[s].astype(F32)
    down2 = jnp.concatenate([total2[128 + 32 * k : 160 + 32 * k, 0:512] for k in range(3)], axis=1)
    for k in range(4):
        r.zs2[k] = total2[0:128, 144 * k : 144 * k + 144].astype(BF16)
        r.zd2[k] = down2[:, 384 * k : 384 * k + 384].astype(BF16)
    z2 = SumZ(b, s, [
        (r.zs2, (r.zs2p, r.zs2m, r.zs2a, r.zs2b)), (r.zd2, (r.zd2p, r.zd2m, r.zd2a, r.zd2b)),
    ], r.z2sem)
    z2.begin()
    g1v = dh1 * r.gain_s[0, 0:1, :]
    tg = r.mix_s[...] + inv1 * (g1v - n1 * (jnp.sum(g1v * n1, axis=-1, keepdims=True) * (1.0 / D)))
    for q in range(2):
        r.tgrad[q] = tg[PIECE * q : PIECE * (q + 1), :].T.astype(BF16)
    homeward(3, r.tgrad, r.tgrad_o, *begin)
    for offset in order:
        fold1(*offset)
        sum1.event(*offset)
        if offset == (0, 3):
            z2.middle()
    sum1.end()
    total1 = r.g1[s].astype(F32)
    for k in range(4):
        r.zs1[k] = total1[:, 144 * k : 144 * k + 144].astype(BF16)
    z1 = [
        rcopy(r.zs1.at[hop(b, d)], r.zs1l.at[d - 1], r.z1sem.at[0, d], r.z1sem.at[1, d], (hop(b, d), s))
        for d in (1, 2, 3)
    ]
    start(z1)
    raw2, down_sum = z2.result()
    r.raw_o[32:160, :] = raw2
    r.down_o[...] = down_sum
    total = r.zs1[b].astype(F32)
    for d, cp in enumerate(z1):
        cp.wait_recv()
        total += r.zs1l[d].astype(F32)
    r.raw_o[0:32, :] = total
    for offset in order:
        copy2(*offset).wait_send()
        copy1(*offset).wait_send()
    for part in (sumk, sum2, sum1, z2):
        part.finish()
    for cp in z1:
        cp.wait_send()
    for k, src, dst in ((2, r.mixed, r.mixed_o), (3, r.tgrad, r.tgrad_o)):
        homeward(k, src, dst, *ended)
        homeward_wait(k, src, dst)


def layer_call(shards, tokens, cot, tables, constants):
    any_ = pl.BlockSpec(memory_space=pl.ANY)
    vm = pl.BlockSpec(memory_space=pltpu.VMEM)
    return pl.pallas_call(
        layer_kernel,
        out_shape=(
            jax.ShapeDtypeStruct((2, D, PIECE), BF16),
            jax.ShapeDtypeStruct((2, D, PIECE), BF16),
            jax.ShapeDtypeStruct((160, 144), F32),
            jax.ShapeDtypeStruct((32, 384), F32),
        ),
        in_specs=[vm] * 8 + [any_] * 2 + [vm] * 4 + [any_] * 3,
        out_specs=(any_, any_, vm, vm),
        scratch_shapes=[pltpu.VMEM(shape, kind) for shape, kind in SCRATCH.values()]
        + [pltpu.SemaphoreType.DMA(shape) for shape in SEMS.values()],
        compiler_params=pltpu.CompilerParams(
            collective_id=0, has_side_effects=True, vmem_limit_bytes=VLIMIT
        ),
        name="decoder_layer",
    )(*shards, tokens, cot, *tables, *constants)


def finish_kernel(mixed, tgrad, raw, down, mixed_o, tgrad_o, g1, wq, wk, wv, wo, g2, wg, wu, wd):
    mixed_o[...] = mixed[...]
    tgrad_o[...] = tgrad[...]
    g1[...] = raw[30:31, 0:18]
    g2[...] = raw[50:51, 0:18]
    for at, ref in ((0, wq), (18, wk), (24, wv), (32, wo), (64, wg), (112, wu)):
        ref[...] = raw[at : at + ref.shape[0], :]
    wd[...] = down[0:18, :]


def finish_call(mixed, tgrad, raw, down):
    vm = pl.BlockSpec(memory_space=pltpu.VMEM)
    shapes = [(1, 18), (18, 144), (6, 144), (6, 144), (18, 144), (1, 18), (48, 144), (48, 144), (18, 384)]
    return pl.pallas_call(
        finish_kernel,
        out_shape=tuple([jax.ShapeDtypeStruct((2, D, PIECE), BF16)] * 2 + [jax.ShapeDtypeStruct(n, F32) for n in shapes]),
        in_specs=[vm] * 4,
        out_specs=(vm,) * 11,
        name="write_outputs",
    )(mixed, tgrad, raw, down)


def body(
    tokens, doc_lengths, first_gain, query_weight, key_matrix, value_matrix,
    output_weight, second_gain, gate_weight, up_weight, down_weight, cotangent,
):
    s = lax.axis_index("seq")
    c, p = s % 2, s // 2
    gains = jnp.stack([first_gain, second_gain])
    spread = jnp.asarray(spread_matrix())
    sprt = jnp.asarray(spread_matrix().T.copy())
    fold, owner = (jnp.asarray(m) for m in gain_matrix())

    lens = lax.dynamic_index_in_dim(doc_lengths[:, 0, :], c, 0, False)
    starts = [jnp.zeros((), jnp.int32), lens[0], lens[0] + lens[1]]
    at = jnp.arange(PIECE, dtype=jnp.int32)
    e = early_piece(p)
    spots = jnp.stack([e * PIECE + at, (31 - e) * PIECE + at])
    begins = jnp.where(spots >= starts[2], starts[2], jnp.where(spots >= starts[1], starts[1], 0))
    rates = THETA ** (-2.0 * jnp.arange(HD // 2, dtype=F32) / HD)
    angles = (spots - begins).reshape(T).astype(F32)[None, :] * rates[:, None]
    cos, sin = jnp.cos(angles), jnp.sin(angles)
    shards = [
        query_weight.T, key_matrix.T, value_matrix.T, output_weight.T,
        gate_weight.T, up_weight.T, down_weight.T, gains,
    ]
    turn = lambda a: jnp.swapaxes(a[:, 0], 1, 2)
    mixed, tgrad, raw, down = layer_call(
        shards, turn(tokens), turn(cotangent), (cos, sin, begins, owner), (spread, sprt, fold)
    )
    mixed, tgrad, g1, wq, wk, wv, wo, g2, wg, wu, wd = finish_call(mixed, tgrad, raw, down)
    back = lambda a: jnp.swapaxes(a, 1, 2)[:, None]
    return (
        back(mixed), back(tgrad), g1.reshape(18), wq.T, wk.T, wv.T, wo.T, g2.reshape(18), wg.T, wu.T, wd.T,
    )


def solution(mesh):
    weight = P("batch", "seq")
    rows = P(None, "batch", "seq", None)
    return jax.shard_map(
        body,
        mesh=mesh,
        in_specs=(
            rows, P(None, "batch", None), P("seq"), weight, weight, weight, weight,
            P("seq"), weight, weight, weight, rows,
        ),
        out_specs=(
            rows, rows, P("seq"), weight, weight, weight, weight,
            P("seq"), weight, weight, weight,
        ),
        check_vma=False,
    )
```

```python
import numpy as np
import ml_dtypes
import jax
import jax.numpy as jnp
from jax import lax
from jax.experimental import pallas as pl
from jax.experimental.pallas import tpu as pltpu
from jax.sharding import PartitionSpec as P

D = 576
HEADS = 9
KV = 3
HD = 64
FF = 1536
PIECE = 128
T = 2 * PIECE
LANES = 3 * T
EPS = 1e-05
THETA = 100000.0
MASKED = -1e30
MESH = pl.DeviceIdType.MESH
F32 = jnp.float32
BF16 = jnp.bfloat16
VLIMIT = 58 * 1024 * 1024


def spread_matrix():
    m = np.zeros((960, 1024), np.float32)
    n = np.arange(576)
    m[n, 32 * (n // 18) + n % 18] = 1
    n = np.arange(192)
    m[576 + n, 32 * (n // 6) + 18 + n % 6] = 1
    m[768 + n, 32 * (n // 6) + 24 + n % 6] = 1
    return m.astype(ml_dtypes.bfloat16)


def gain_matrix():
    n = np.arange(576)
    fold = np.zeros((576, 576), np.float32)
    for b in range(4):
        fold[n, 144 * b + n % 18] = 1
    owner = (n[None, :] // 18 == np.arange(32)[:, None]).astype(np.float32)
    return fold.astype(ml_dtypes.bfloat16), owner


def nn(a, b):
    return lax.dot_general(a, b, (((1,), (0,)), ((), ())), preferred_element_type=F32)


def nt(a, b):
    return lax.dot_general(a, b, (((1,), (1,)), ((), ())), preferred_element_type=F32)


def tn(a, b):
    return lax.dot_general(a, b, (((0,), (0,)), ((), ())), preferred_element_type=F32)


def rcopy(src, dst, ss, rs, dev):
    return pltpu.make_async_remote_copy(
        src_ref=src, dst_ref=dst, send_sem=ss, recv_sem=rs, device_id=dev, device_id_type=MESH
    )


def place():
    b = lax.axis_index("batch")
    s = lax.axis_index("seq")
    c = lax.rem(s, 2)
    p = lax.div(s, 2)
    return b, s, c, p, lax.div(p, 4), lax.rem(p, 4)


def chip_of(piece):
    i = jnp.minimum(piece, 31 - piece)
    half = lax.div(i, 2)
    return jnp.where(lax.rem(i, 2) == 0, half, 15 - half)


def early_piece(chip):
    return jnp.where(chip < 8, 2 * chip, 31 - 2 * chip)


def seq_of(y, x, c):
    return (y * 4 + x) * 2 + c


def hop(i, d):
    return lax.rem(i + d, 4)


def hail(devices):
    bar = pltpu.get_barrier_semaphore()
    for dev in devices:
        pl.semaphore_signal(bar, inc=1, device_id=dev, device_id_type=MESH)
    return bar


def neighbours(b, s, c, y, x):
    found = [(b, seq_of(y, x, 1 - c))]
    for d in (1, 2, 3):
        found += [
            (hop(b, d), s),
            (b, seq_of(y, hop(x, d), c)),
            (b, seq_of(hop(y, d), x, c)),
        ]
    return found


class Ring:
    def __init__(self, dev, ss, rs, direct=False):
        self.dev, self.ss, self.rs, self.direct = dev, ss, rs, direct

    def copy(self, n, src, dst):
        if n == 2 and self.direct:
            return rcopy(src, dst, self.ss.at[n], self.rs.at[n], self.dev(2, 0))
        du, dv = {0: (1, 0), 1: (3, 0), 2: (1, 0), 3: (3, 0)}.get(n, (0, 1 if n // 4 in (1, 3) else 3))
        return rcopy(src, dst, self.ss.at[n], self.rs.at[n], self.dev(du, dv))


def token_rows(ref):
    return jnp.concatenate([ref[0].astype(F32).T, ref[1].astype(F32).T], axis=0)


def gain_row(blocks, row, fold, owner):
    at = lax.broadcasted_iota(jnp.int32, (32, 1024), 0) * 32 + row
    one = (lax.broadcasted_iota(jnp.int32, (32, 1024), 1) == at).astype(F32).astype(BF16)
    spread = nt(nn(one, blocks[:, 0:128]).astype(BF16), fold[:, 0:128])
    return jnp.sum(spread * owner, axis=0, keepdims=True)


def place_row(row, values):
    at = lax.broadcasted_iota(jnp.int32, (1024, 32), 1) * 32 + row
    one = (lax.broadcasted_iota(jnp.int32, (1024, 32), 0) == at).astype(F32).astype(BF16)
    return nn(one, values.astype(BF16))


def diagonal_mask(p, qpos, qstart):
    row = lax.broadcasted_iota(jnp.int32, (T, 1), 0)
    kpos = jnp.where(row < PIECE, p * PIECE + row, (31 - p) * PIECE + row - PIECE)
    return (kpos <= qpos) & (kpos >= qstart)


def first_mask(qstart):
    row = lax.broadcasted_iota(jnp.int32, (PIECE, 1), 0)
    return row >= qstart


def pick(i, values):
    found = values[0]
    for k, value in enumerate(values[1:]):
        found = jnp.where(i == k + 1, value, found)
    return found


FORWARD = ((0, 0), (3, 0), (1, 0), (0, 3), (0, 1), (2, 0), (3, 3), (3, 1), (1, 3), (1, 1), (2, 3), (2, 1), (0, 2), (3, 2), (1, 2), (2, 2))
BACKWARD = ((0, 0), (2, 2), (1, 2), (3, 2), (0, 2), (2, 1), (2, 3), (1, 1), (1, 3), (3, 1), (3, 3), (0, 1), (0, 3), (2, 0), (1, 0), (3, 0))
HALVES = (pl.ds(0, PIECE), pl.ds(PIECE, PIECE))


ROWS = 224


class Plane:
    def __init__(self):
        self.b, self.s, self.c, self.p, self.y, self.x = place()
        c, y, x = self.c, self.y, self.x
        self.u, self.v = jnp.where(c == 0, x, y), jnp.where(c == 0, y, x)
        self.su, self.sv = 1 + 3 * c, 4 - 3 * c
        self.other = (self.b, seq_of(y, x, 1 - c))

    def index(self, du, dv):
        return lax.rem(self.u + du, 4) * self.su + lax.rem(self.v + dv, 4) * self.sv

    def dev(self, du, dv):
        return (self.b, 2 * self.index(du, dv) + self.c)

    def common(self, du, dv):
        return du * self.su + dv * self.sv


class Gather:
    def __init__(self, plane, view, own, sems, swap=None, direct=False):
        self.ring = Ring(plane.dev, sems.at[0], sems.at[1], direct)
        self.view, self.own, self.swap = view, own, swap
        self.later = []

    def copy(self, n, du, dv, part=None):
        ref = self.view(du, dv, part)
        return self.ring.copy(n, self.own if (du, dv) == (0, 0) else ref, ref)

    def send(self, *item):
        self.copy(*item).start()
        self.later.append(item)

    def arrive(self, n, du, dv, part=None):
        ref = self.view(du, dv, part)
        self.ring.copy(n, ref, ref).wait_recv()

    def done(self, du, dv):
        if self.swap is not None:
            self.swap(du, dv).start()

    def begin_u(self):
        self.send(0, 0, 0)
        self.send(1, 0, 0)
        if self.ring.direct:
            self.send(2, 0, 0)

    def begin_v(self):
        self.send(4, 0, 0)
        self.send(8, 0, 0)
        self.done(0, 0)

    def near(self):
        for n, du in ((0, 3), (1, 1)):
            self.arrive(n, du, 0)
            if not self.ring.direct:
                self.send(2 + n, du, 0, n)
            self.send(4 + du, du, 0)
            self.send(8 + du, du, 0)
            self.done(du, 0)

    def far(self):
        if self.ring.direct:
            self.arrive(2, 2, 0)
        else:
            self.arrive(2, 2, 0, 0)
            self.arrive(3, 2, 0, 1)
        self.send(6, 2, 0)
        self.send(10, 2, 0)
        self.done(2, 0)

    def line(self, w):
        self.arrive(4 + w, w, 3)
        self.send(12 + w, w, 3, 0)
        self.done(w, 3)
        self.arrive(8 + w, w, 1)
        self.send(16 + w, w, 1, 1)
        self.done(w, 1)

    def last(self, w):
        self.arrive(12 + w, w, 2, 0)
        self.arrive(16 + w, w, 2, 1)
        self.done(w, 2)

    def finish(self):
        for item in self.later:
            self.copy(*item).wait_send()
        if self.swap is not None:
            for du in range(4):
                for dv in range(4):
                    self.swap(du, dv).wait()


class Reduce:
    def __init__(self, plane, view, add, bufs, sems, direct=False):
        self.ring = Ring(plane.dev, sems.at[0], sems.at[1], direct)
        self.view, self.add = view, add
        va, vb, vp, vm, ua, ub, up, um = bufs
        self.pieces = {
            2: (2, 0, 0, ua), 3: (2, 0, 1, ub), 0: (1, 0, None, up), 1: (3, 0, None, um),
        }
        if direct:
            self.pieces[2] = (2, 0, None, ua)
            del self.pieces[3]
        for w in range(4):
            self.pieces[12 + w] = (w, 2, 0, va.at[w])
            self.pieces[16 + w] = (w, 2, 1, vb.at[w])
            self.pieces[4 + w] = (w, 1, None, vp.at[w])
            self.pieces[8 + w] = (w, 3, None, vm.at[w])

    def copy(self, n):
        du, dv, part, dst = self.pieces[n]
        return self.ring.copy(n, self.view(du, dv, part), dst)

    def take(self, n, du, dv, part=None):
        self.copy(n).wait_recv()
        self.add(du, dv, part, self.pieces[n][3])

    def event(self, du, dv):
        if dv == 2:
            self.copy(12 + du).start()
            self.copy(16 + du).start()
        elif dv == 1:
            self.take(12 + du, du, 1, 0)
            self.copy(4 + du).start()
        elif dv == 3:
            self.take(16 + du, du, 3, 1)
            self.copy(8 + du).start()
        else:
            self.take(4 + du, du, 0)
            self.take(8 + du, du, 0)
            if self.ring.direct:
                if du:
                    self.copy({1: 0, 2: 2, 3: 1}[du]).start()
            elif du == 2:
                self.copy(2).start()
                self.copy(3).start()
            elif du == 1:
                self.take(2, 1, 0, 0)
                self.copy(0).start()
            elif du == 3:
                self.take(3, 3, 0, 1)
                self.copy(1).start()

    def end(self):
        self.take(0, 0, 0)
        self.take(1, 0, 0)
        if self.ring.direct:
            self.take(2, 0, 0)

    def finish(self):
        for n in self.pieces:
            self.copy(n).wait_send()


class SumZ:
    def __init__(self, b, s, items, sems):
        self.b, self.s, self.items, self.sems = b, s, items, sems

    def copies(self, n):
        at = hop(self.b, 2 if n > 1 else 1 + 2 * n)
        dev = (hop(self.b, 1 if n in (0, 2) else 3), self.s)
        found = []
        for k, (ref, bufs) in enumerate(self.items):
            size = ref.shape[1] // 2
            src = ref.at[at] if n < 2 else ref.at[at, pl.ds(size * (n - 2), size)]
            found.append(rcopy(src, bufs[n], self.sems.at[0, k, n], self.sems.at[1, k, n], dev))
        return found

    def start(self, n):
        for cp in self.copies(n):
            cp.start()

    def begin(self):
        self.start(2)
        self.start(3)

    def middle(self):
        for n in (2, 3):
            for cp in self.copies(n):
                cp.wait_recv()
            at = hop(self.b, 1 if n == 2 else 3)
            for ref, bufs in self.items:
                size = ref.shape[1] // 2
                part = (at, pl.ds(size * (n - 2), size))
                ref[part] = ref[part] + bufs[n][...]
            self.start(n - 2)

    def result(self):
        for n in (0, 1):
            for cp in self.copies(n):
                cp.wait_recv()
        found = []
        for ref, bufs in self.items:
            found.append(ref[self.b].astype(F32) + bufs[0][...].astype(F32) + bufs[1][...].astype(F32))
        return found

    def finish(self):
        for n in range(4):
            for cp in self.copies(n):
                cp.wait_send()


SCRATCH = {
    "spread": ((960, 1024), BF16), "sprt": ((1024, 960), BF16), "fold": ((D, D), BF16),
    "raw_f": ((160, 144), F32), "dwn_f": ((32, 384), F32),
    "za": ((4, 160, 144), BF16), "zd": ((4, 32, 384), BF16),
    "blk1": ((32, D), BF16), "blk2": ((ROWS, D), BF16),
    "g1": ((32, 32, D), BF16), "g2": ((32, ROWS, D), BF16),
    "tok": ((2, D, PIECE), BF16), "cot": ((2, D, PIECE), BF16),
    "qpos": ((1, LANES), jnp.int32), "qstart": ((1, LANES), jnp.int32), "gain_s": ((4, 8, D), F32), "x_s": ((T, D), F32), "h1": ((T, D), BF16),
    "kv": ((KV, T, 128), BF16), "qt": ((KV, 128, LANES), BF16), "dot": ((KV, 128, LANES), BF16),
    "kva": ((16, KV, T, 128), BF16),
    "m_s": ((KV, 1, LANES), F32), "l_s": ((KV, 1, LANES), F32), "delta": ((KV, 1, LANES), F32),
    "acc": ((KV, HD, LANES), F32), "dq": ((KV, HD, LANES), F32), "dkv": ((KV, T, 128), F32),
    "wd_s": ((D, FF), BF16), "act_s": ((T, FF), BF16), "wo_s": ((D, D), BF16),
    "h2_s": ((T, D), BF16), "dh2_s": ((T, D), F32), "mix_s": ((T, D), F32),
    "mixed": ((2, D, PIECE), BF16), "tgrad": ((2, D, PIECE), BF16),
    "sent": ((16, KV, T, 128), BF16),
    "kva_": ((4, KV, PIECE, 128), BF16), "kvb_": ((4, KV, PIECE, 128), BF16),
    "kvp_": ((4, KV, T, 128), BF16), "kvm_": ((4, KV, T, 128), BF16),
    "kua_": ((KV, PIECE, 128), BF16), "kub_": ((KV, PIECE, 128), BF16),
    "kup_": ((KV, T, 128), BF16), "kum_": ((KV, T, 128), BF16),
    "r2": ((16, ROWS, D), BF16),
    "wva": ((4, ROWS // 2, D), BF16), "wvb": ((4, ROWS // 2, D), BF16),
    "wvp": ((4, ROWS, D), BF16), "wvm": ((4, ROWS, D), BF16),
    "wua": ((ROWS // 2, D), BF16), "wub": ((ROWS // 2, D), BF16),
    "wup": ((ROWS, D), BF16), "wum": ((ROWS, D), BF16),
    "r1": ((16, 32, D), BF16),
    "ava": ((4, 16, D), BF16), "avb": ((4, 16, D), BF16),
    "avp": ((4, 32, D), BF16), "avm": ((4, 32, D), BF16),
    "aua": ((32, D), BF16), "aub": ((16, D), BF16),
    "aup": ((32, D), BF16), "aum": ((32, D), BF16),
    "zs2": ((4, 128, 144), BF16), "zd2": ((4, 32, 384), BF16), "zs1": ((4, 32, 144), BF16),
    "zs2p": ((128, 144), BF16), "zs2m": ((128, 144), BF16), "zs2a": ((64, 144), BF16), "zs2b": ((64, 144), BF16),
    "zd2p": ((32, 384), BF16), "zd2m": ((32, 384), BF16), "zd2a": ((16, 384), BF16), "zd2b": ((16, 384), BF16),
    "zs1l": ((3, 32, 144), BF16),
}
SEMS = {
    "lsem": (4,), "zsem": (2, 2, 4), "zz": (4, 2, 2), "zl": (4,),
    "g1sem": (2, 20), "g1swap": (2, 16), "g2sem": (2, 20), "g2swap": (2, 16), "kvsem": (2, 20),
    "dksem": (2, 20), "d2fold": (2, 16), "d2sem": (2, 20), "d1fold": (2, 16), "d1sem": (2, 20),
    "z2sem": (2, 2, 4), "z1sem": (2, 4), "zasem": (2, 4),
}
INPUTS = (
    "wq", "wk", "wv", "wo", "wg", "wu", "wd", "gains", "tokens", "cotin", "cos", "sin", "begins",
    "owner", "spread_in", "sprt_in", "fold_in",
)
OUTPUTS = ("mixed_o", "tgrad_o", "raw_o", "down_o")


class Refs:
    def __init__(self, refs):
        for name, ref in zip((*INPUTS, *OUTPUTS, *SCRATCH, *SEMS), refs, strict=True):
            setattr(self, name, ref)


def layer_kernel(*refs):
    r = Refs(refs)
    plane = Plane()
    b, s, c, p, y, x = plane.b, plane.s, plane.c, plane.p, plane.y, plane.x
    target = 2 * chip_of(s)
    slot = lax.div(s, 16)
    e = early_piece(p)
    bar = hail(neighbours(b, s, c, y, x))
    around = [target, target + 1, e, 31 - e]
    for peer in around:
        @pl.when(peer != s)
        def _():
            pl.semaphore_signal(bar, inc=1, device_id=(b, peer), device_id_type=MESH)
    constants = [
        pltpu.make_async_copy(src, dst, r.lsem.at[k])
        for k, (src, dst) in enumerate(((r.spread_in, r.spread), (r.sprt_in, r.sprt), (r.fold_in, r.fold)))
    ]
    for cp in constants:
        cp.start()
    for lane in range(0, LANES, PIECE):
        q = lane // 384
        at = (31 - e if q else e) * PIECE
        r.qpos[:, lane : lane + PIECE] = at + lax.broadcasted_iota(jnp.int32, (1, PIECE), 1)
        r.qstart[:, lane : lane + PIECE] = r.begins[q : q + 1, :]
    r.raw_f[...] = jnp.zeros_like(r.raw_f)
    r.dwn_f[...] = jnp.zeros_like(r.dwn_f)
    for at, ref in ((0, r.wq), (18, r.wk), (24, r.wv), (32, r.wo), (64, r.wg), (112, r.wu)):
        r.raw_f[at : at + ref.shape[0], :] = ref[...].astype(F32)
    r.raw_f[30:32, 0:18] = r.gains[...].astype(F32)
    r.dwn_f[0:18, :] = r.wd[...].astype(F32)
    r.za[pl.ds(b, 1)] = r.raw_f[...].astype(BF16)[None]
    r.zd[pl.ds(b, 1)] = r.dwn_f[...].astype(BF16)[None]
    peers = 10
    for peer in around:
        peers = peers + jnp.where(peer != s, 1, 0)
    pl.semaphore_wait(bar, peers)

    def zcopies(n, at, part):
        dev = (hop(b, 1 if n in (0, 2) else 3), s)
        found = []
        for k, (ref, low, rows) in enumerate(((r.za, 32, 64), (r.zd, 0, 16))):
            view = ref.at[at, pl.ds(low, 2 * rows) if part is None else pl.ds(low + rows * part, rows)]
            found.append(rcopy(view, view, r.zsem.at[0, k, n], r.zsem.at[1, k, n], dev))
        return found

    def start(copies):
        for cp in copies:
            cp.start()

    def acopy(d, at):
        view = r.za.at[at, pl.ds(0, 32)]
        return rcopy(view, view, r.zasem.at[0, d], r.zasem.at[1, d], (hop(b, d), s))

    start([acopy(d, b) for d in (1, 2, 3)])
    zsent = [zcopies(0, b, None), zcopies(1, b, None)]
    start(zsent[0] + zsent[1])

    def outward(k, src_ref, dst_ref, act_remote, act_local):
        for m in (0, 1):
            dst = target + m

            @pl.when(dst != s)
            def _():
                act_remote(rcopy(src_ref.at[m], dst_ref.at[slot], r.zz.at[k, 0, m], r.zz.at[k, 1, slot], (b, dst)))

            @pl.when(dst == s)
            def _():
                act_local(pltpu.make_async_copy(src_ref.at[m], dst_ref.at[slot], r.zl.at[k]))

    def outward_wait(k, src_ref, dst_ref):
        for q, src in enumerate((e, 31 - e)):
            @pl.when(src != s)
            def _():
                rcopy(src_ref.at[0], dst_ref.at[q], r.zz.at[k, 0, 0], r.zz.at[k, 1, q], (b, src)).wait_recv()

    def homeward(k, src_ref, dst_ref, act_remote, act_local):
        for q, dst in enumerate((e, 31 - e)):
            @pl.when(dst != s)
            def _():
                act_remote(rcopy(src_ref.at[q], dst_ref.at[c], r.zz.at[k, 0, q], r.zz.at[k, 1, c], (b, dst)))

            @pl.when(dst == s)
            def _():
                act_local(pltpu.make_async_copy(src_ref.at[q], dst_ref.at[c], r.zl.at[k]))

    def homeward_wait(k, src_ref, dst_ref):
        for m in (0, 1):
            src = target + m

            @pl.when(src != s)
            def _():
                rcopy(src_ref.at[0], dst_ref.at[m], r.zz.at[k, 0, 0], r.zz.at[k, 1, m], (b, src)).wait_recv()

    begin = (lambda cp: cp.start(), lambda cp: cp.start())
    ended = (lambda cp: cp.wait_send(), lambda cp: cp.wait())
    outward(0, r.tokens, r.tok, *begin)

    for d in (1, 2, 3):
        acopy(d, hop(b, 4 - d)).wait_recv()
    r.blk1[...] = jnp.concatenate([r.za[i, 0:32, :].astype(F32) for i in range(4)], axis=1).astype(BF16)

    def weights(ref, own, sems, swap_sems, half, direct=False):
        def view(du, dv, part=None):
            at = 2 * plane.index(du, dv) + c
            return ref.at[at] if part is None else ref.at[at, pl.ds(half * part, half)]

        def swap(du, dv):
            n = plane.common(du, dv)
            dst = view(du, dv)
            src = own if (du, dv) == (0, 0) else dst
            return rcopy(src, dst, swap_sems.at[0, n], swap_sems.at[1, n], plane.other)

        return Gather(plane, view, own, sems, swap, direct)

    first = weights(r.g1, r.blk1, r.g1sem, r.g1swap, 16, True)
    second = weights(r.g2, r.blk2, r.g2sem, r.g2swap, ROWS // 2)
    first.begin_u()
    first.begin_v()
    r.g1[pl.ds(s, 1)] = r.blk1[...][None]
    for n, way in ((0, 3), (1, 1)):
        for cp in zcopies(n, hop(b, way), None):
            cp.wait_recv()
        zsent.append(zcopies(2 + n, hop(b, way), n))
        start(zsent[-1])
    first.near()
    first.line(0)
    first.far()
    for n in (2, 3):
        for cp in zcopies(n, hop(b, 2), n - 2):
            cp.wait_recv()
    down = jnp.concatenate([r.zd[i] for i in range(4)], axis=1)
    r.blk2[0:128, :] = jnp.concatenate([r.za[i, 32:160, :].astype(F32) for i in range(4)], axis=1).astype(BF16)
    r.blk2[128:224, 512:576] = jnp.zeros((96, 64), BF16)
    for k in range(3):
        r.blk2[128 + 32 * k : 160 + 32 * k, 0:512] = down[:, 512 * k : 512 * (k + 1)]
    second.begin_u()
    r.g2[pl.ds(s, 1)] = r.blk2[...][None]
    outward_wait(0, r.tokens, r.tok)
    outward(0, r.tokens, r.tok, *ended)
    r.x_s[...] = token_rows(r.tok)
    for w in (3, 1, 2):
        first.line(w)
    second.begin_v()
    for w in (0, 3, 1, 2):
        first.last(w)
    second.near()
    first.finish()
    for cp in constants:
        cp.wait()

    owner_rows = r.owner[...]
    fold = r.fold[...]
    wa = r.g1[...].reshape(1024, D)
    gain1 = gain_row(wa, 30, fold, owner_rows)
    r.gain_s[0] = jnp.broadcast_to(gain1, (8, D))
    r.gain_s[1] = jnp.broadcast_to(gain_row(wa, 31, fold, owner_rows), (8, D))
    xin = r.x_s[...]
    inv1 = lax.rsqrt(jnp.sum(xin * xin, axis=-1, keepdims=True) * (1.0 / D) + EPS)
    r.h1[...] = (xin * inv1 * gain1).astype(BF16)
    w_all = nn(r.spread[...], wa).astype(BF16)
    z = nt(w_all, r.h1[...])
    co, si = r.cos[...], r.sin[...]

    def rot(a):
        a1, a2 = a[0:32], a[32:64]
        return jnp.concatenate([a1 * co - a2 * si, a2 * co + a1 * si], axis=0)

    def unrot(a):
        a1, a2 = a[0:32], a[32:64]
        return jnp.concatenate([a1 * co + a2 * si, a2 * co - a1 * si], axis=0)

    for h in range(KV):
        kh = rot(z[576 + 64 * h : 640 + 64 * h])
        vh = z[768 + 64 * h : 832 + 64 * h]
        r.kv[h] = jnp.concatenate([kh, vh], axis=0).T.astype(BF16)

    def kview(ref):
        def view(du, dv, part=None):
            at = plane.index(du, dv)
            return ref.at[at] if part is None else ref.at[at, :, HALVES[part]]
        return view

    keys = Gather(plane, kview(r.kva), r.kv, r.kvsem)
    keys.begin_u()
    keys.begin_v()
    outward(1, r.cotin, r.cot, *begin)
    r.kva[pl.ds(p, 1)] = r.kv[...][None]
    for h in range(HEADS):
        q = (rot(z[64 * h : 64 * h + 64]).astype(BF16).astype(F32) * 0.125).astype(BF16)
        kvh, gi = h // 3, h % 3
        for piece in range(2):
            lane = piece * 384 + gi * 128
            r.qt[kvh, 0:64, lane : lane + 128] = q[:, piece * 128 : piece * 128 + 128]
    for h in range(KV):
        r.qt[h, 64:128, :] = jnp.zeros((64, LANES), BF16)
        r.dot[h, 0:64, :] = jnp.zeros((64, LANES), BF16)

    r.m_s[...] = jnp.full_like(r.m_s, MASKED)
    r.l_s[...] = jnp.zeros_like(r.l_s)
    r.acc[...] = jnp.zeros_like(r.acc)
    every = pl.ds(0, LANES)
    late = pl.ds(384, 384)

    def step(block, h, lanes, mask, drop):
        st = nn(block, r.qt[h, :, lanes])
        if mask is not None:
            st = jnp.where(mask, st, MASKED)
        m_old = r.m_s[h, :, lanes]
        top = jnp.max(st, axis=0, keepdims=True)
        if drop is None:
            m_new = jnp.maximum(m_old, top)
            m_sub = m_new
        else:
            m_new = jnp.maximum(m_old, jnp.where(drop, MASKED, top))
            m_sub = jnp.where(drop, -MASKED, m_new)
        pt = jnp.exp(st - m_sub)
        a = jnp.exp(m_old - m_new)
        r.m_s[h, :, lanes] = m_new
        r.l_s[h, :, lanes] = r.l_s[h, :, lanes] * a + jnp.sum(pt, axis=0, keepdims=True)
        r.acc[h, :, lanes] = r.acc[h, :, lanes] * a + tn(block, pt.astype(BF16))[64:128]

    def allowed():
        return diagonal_mask(e, r.qpos[...], r.qstart[...])

    mask = allowed()
    for h in range(KV):
        step(r.kv[h], h, every, mask, None)

    events = {
        1: [keys.near, lambda: second.line(0)], 2: [lambda: keys.line(0)], 3: [keys.far, second.far],
        4: [lambda: keys.line(3)], 5: [lambda: keys.line(1)], 6: [lambda: second.line(3)], 7: [lambda: keys.line(2)],
        8: [lambda: second.line(1)], 10: [lambda: second.line(2)], 12: [lambda: keys.last(0)], 13: [lambda: keys.last(3)],
        14: [lambda: keys.last(1), lambda: second.last(0)], 15: [lambda: keys.last(2)],
    }

    def visit(i, carry):
        for k, todo in events.items():
            @pl.when(i == k)
            def _():
                for event in todo:
                    event()

        j = plane.index(pick(i, [o[0] for o in FORWARD]), pick(i, [o[1] for o in FORWARD]))
        ej = early_piece(j)

        @pl.when((ej < e) & (j > 0))
        def _():
            for h in range(KV):
                step(r.kva[j, h, 0:PIECE, :], h, every, None, None)

        @pl.when((ej < e) & (j == 0))
        def _():
            keep = first_mask(r.qstart[...])
            for h in range(KV):
                step(r.kva[0, h, 0:PIECE, :], h, every, keep, None)

        @pl.when(ej > e)
        def _():
            drop = r.qstart[:, late] >= PIECE
            for h in range(KV):
                step(r.kva[j, h], h, late, None, drop)

        return carry

    lax.fori_loop(1, 16, visit, 0)
    for h in range(KV):
        total = r.l_s[h]
        r.acc[h] = r.acc[h] / total
        r.m_s[h] = r.m_s[h] + jnp.log(total)
    rows = []
    for h in range(HEADS):
        kvh, gi = h // 3, h % 3
        rows.append(
            jnp.concatenate(
                [r.acc[kvh, :, q * 384 + gi * 128 : q * 384 + gi * 128 + 128] for q in range(2)], axis=1
            )
        )
    att_t = jnp.concatenate(rows, axis=0).T.astype(BF16)
    outward_wait(1, r.cotin, r.cot)
    outward(1, r.cotin, r.cot, *ended)
    dy = token_rows(r.cot).astype(BF16)
    dyt_rows = jnp.concatenate([r.cot[0], r.cot[1]], axis=1)
    for w in (3, 1, 2):
        second.last(w)
    keys.finish()
    second.finish()
    for group in zsent + [[acopy(d, b) for d in (1, 2, 3)]]:
        for cp in group:
            cp.wait_send()

    p2 = r.spread[0:576, :]
    p2t = r.sprt[:, 0:576]
    r.wo_s[...] = nn(p2, r.g2[:, 0:32, :].reshape(1024, D)).astype(BF16)
    for k in range(3):
        third = r.g2[:, 128 + 32 * k : 160 + 32 * k, 0:512].reshape(1024, 512)
        r.wd_s[:, 512 * k : 512 * k + 512] = nn(p2, third).astype(BF16)
    middle = r.x_s[...] + nt(att_t, r.wo_s[...])
    inv2 = lax.rsqrt(jnp.sum(middle * middle, axis=-1, keepdims=True) * (1.0 / D) + EPS)
    n2 = middle * inv2
    r.h2_s[...] = (n2 * r.gain_s[1, 0:1, :]).astype(BF16)
    r.mix_s[...] = middle
    r.dh2_s[...] = jnp.zeros_like(r.dh2_s)

    def chunk(f, carry):
        at = pl.ds(8 * f, 8)
        lanes = pl.ds(pl.multiple_of(384 * f, 128), 384)
        wg = r.g2[at, 32:80, :].reshape(384, D)
        wu = r.g2[at, 80:128, :].reshape(384, D)
        h2 = r.h2_s[...]
        gate = nt(h2, wg)
        up = nt(h2, wu)
        sig = 1.0 / (1.0 + jnp.exp(-gate))
        silu = gate * sig
        act = (silu * up).astype(BF16)
        r.act_s[:, lanes] = act
        wdf = r.wd_s[:, lanes]
        r.mix_s[...] += nt(act, wdf)
        da = nn(dy, wdf)
        dup = (da * silu).astype(BF16)
        dgate = (da * up * sig * (1.0 + gate * (1.0 - sig))).astype(BF16)
        r.dh2_s[...] += nn(dgate, wg) + nn(dup, wu)
        r.g2[at, 32:80, :] = tn(dgate, h2).astype(BF16).reshape(8, 48, D)
        r.g2[at, 80:128, :] = tn(dup, h2).astype(BF16).reshape(8, 48, D)
        return carry

    lax.fori_loop(0, 4, chunk, 0)
    for q in range(2):
        r.mixed[q] = r.mix_s[PIECE * q : PIECE * (q + 1), :].T.astype(BF16)
    homeward(2, r.mixed, r.mixed_o, *begin)
    dyt = nn(p2t, dyt_rows).astype(BF16)
    r.g2[:, 128:224, 512:576] = jnp.zeros((32, 96, 64), BF16)
    for k in range(3):
        part = nn(dyt, r.act_s[:, 512 * k : 512 * k + 512]).astype(BF16)
        r.g2[:, 128 + 32 * k : 160 + 32 * k, 0:512] = part.reshape(32, 32, 512)
    dh2 = r.dh2_s[...]
    gsum = jnp.sum(dh2 * n2, axis=0, keepdims=True)
    r.gain_s[2] = jnp.broadcast_to(gsum, (8, D))
    gain = nn((jnp.concatenate([r.gain_s[2]] * 4, axis=0) * r.owner[...]).astype(BF16), r.fold[...])
    g2v = dh2 * r.gain_s[1, 0:1, :]
    dmid = dy.astype(F32) + inv2 * (g2v - n2 * (jnp.sum(g2v * n2, axis=-1, keepdims=True) * (1.0 / D)))
    r.mix_s[...] = dmid
    dbt = nn(p2t, dmid.T.astype(BF16)).astype(BF16)
    r.g2[:, 0:32, :] = (nn(dbt, att_t) + place_row(18, gain)).astype(BF16).reshape(32, 32, D)

    def folder(ref, land, sems):
        def copy(du, dv):
            at = plane.index(du, dv)
            n = plane.common(du, dv)
            return rcopy(ref.at[2 * at + 1 - c], land.at[at], sems.at[0, n], sems.at[1, n], plane.other)

        def fold_in(du, dv):
            copy(du, dv).wait_recv()
            at = plane.index(du, dv)
            ref[2 * at + c] = ref[2 * at + c] + land[at]

        return copy, fold_in

    def reducer(ref, bufs, sems, half, direct=False):
        def view(du, dv, part=None):
            at = 2 * plane.index(du, dv) + c
            return ref.at[at] if part is None else ref.at[at, pl.ds(half * part, half)]

        def add(du, dv, part, buf):
            at = 2 * plane.index(du, dv) + c
            where = (at,) if part is None else (at, pl.ds(half * part, half))
            ref[where] = ref[where] + buf[...]

        return Reduce(plane, view, add, bufs, sems, direct)

    copy2, fold2 = folder(r.g2, r.r2, r.d2fold)
    sum2 = reducer(r.g2, (r.wva, r.wvb, r.wvp, r.wvm, r.wua, r.wub, r.wup, r.wum), r.d2sem, ROWS // 2)
    order = BACKWARD[1:] + BACKWARD[:1]
    for du, dv in order:
        copy2(dv, du).start()
    datt = nn(dmid.astype(BF16), r.wo_s[...]).astype(BF16).astype(F32).T
    for h in range(HEADS):
        kvh, gi = h // 3, h % 3
        for q in range(2):
            lane = q * 384 + gi * 128
            part = datt[64 * h : 64 * h + 64, 128 * q : 128 * q + 128]
            r.dot[kvh, 64:128, lane : lane + 128] = part.astype(BF16)
            r.delta[kvh, :, lane : lane + 128] = jnp.sum(
                part * r.acc[kvh, :, lane : lane + 128], axis=0, keepdims=True
            )

    def add_keys(du, dv, part, buf):
        at = plane.index(du, dv)
        if part is None:
            r.sent[at] = r.sent[at] + buf[...]
        else:
            rows = slice(PIECE * part, PIECE * (part + 1))
            r.sent[at, :, rows, :] = r.sent[at, :, rows, :] + buf[...]

    sumk = Reduce(
        plane, kview(r.sent), add_keys,
        (r.kva_, r.kvb_, r.kvp_, r.kvm_, r.kua_, r.kub_, r.kup_, r.kum_), r.dksem,
    )
    r.dq[...] = jnp.zeros_like(r.dq)

    def back(block, h, lanes, mask, drop):
        q = r.qt[h, :, lanes]
        do = r.dot[h, :, lanes]
        st = nn(block, q)
        if mask is not None:
            st = jnp.where(mask, st, MASKED)
        base = r.m_s[h, :, lanes]
        if drop is not None:
            base = jnp.where(drop, -MASKED, base)
        pt = jnp.exp(st - base)
        dp = nn(block, do)
        ds = (pt * (dp - r.delta[h, :, lanes])).astype(BF16)
        r.dq[h, :, lanes] += tn(block, ds)[0:64]
        return nt(ds, q) + nt(pt.astype(BF16), do)

    def visit_back(i, carry):
        j = plane.index(pick(i, [o[0] for o in BACKWARD]), pick(i, [o[1] for o in BACKWARD]))
        ej = early_piece(j)

        @pl.when(ej < e)
        def _():
            r.sent[j, :, PIECE:T, :] = jnp.zeros((KV, PIECE, 128), BF16)

        @pl.when((ej < e) & (j > 0))
        def _():
            for h in range(KV):
                r.sent[j, h, 0:PIECE, :] = back(r.kva[j, h, 0:PIECE, :], h, every, None, None).astype(BF16)

        @pl.when((ej < e) & (j == 0))
        def _():
            keep = first_mask(r.qstart[...])
            for h in range(KV):
                r.sent[0, h, 0:PIECE, :] = back(r.kva[0, h, 0:PIECE, :], h, every, keep, None).astype(BF16)

        @pl.when(ej > e)
        def _():
            drop = r.qstart[:, late] >= PIECE
            for h in range(KV):
                r.sent[j, h] = back(r.kva[j, h], h, late, None, drop).astype(BF16)

        for k, offset in enumerate(BACKWARD):
            if k:
                @pl.when(i == k)
                def _():
                    sumk.event(*offset)
                    if offset[1] != 2:
                        fold2(*offset)
                        sum2.event(*offset)

        return carry

    for offset in BACKWARD:
        if offset[1] == 2:
            fold2(*offset)
            sum2.event(*offset)
    lax.fori_loop(1, 16, visit_back, 0)
    mask = allowed()
    for h in range(KV):
        r.dkv[h] = back(r.kva[p, h], h, every, mask, None)
    for n, buf in ((4, r.kvp_.at[0]), (8, r.kvm_.at[0]), (0, r.kup_), (1, r.kum_)):
        sumk.copy(n).wait_recv()
        r.dkv[...] += buf[...].astype(F32)

    fold2(0, 0)
    sum2.event(0, 0)
    parts, vals = [], []
    for h in range(HEADS):
        kvh, gi = h // 3, h % 3
        part = jnp.concatenate(
            [r.dq[kvh, :, q * 384 + gi * 128 : q * 384 + gi * 128 + 128] for q in range(2)], axis=1
        )
        parts.append(unrot(part * 0.125))
    for h in range(KV):
        both = r.dkv[h].T
        parts.append(unrot(both[0:64]))
        vals.append(both[64:128])
    dz = jnp.concatenate(parts + vals, axis=0).astype(BF16)
    dzp = nn(r.sprt[...], dz).astype(BF16)
    dh1 = tn(dzp, r.g1[...].reshape(1024, D))
    n1 = r.x_s[...] * inv1
    gsum1 = jnp.sum(dh1 * n1, axis=0, keepdims=True)
    r.gain_s[3] = jnp.broadcast_to(gsum1, (8, D))
    gain_sum = nn((jnp.concatenate([r.gain_s[3]] * 4, axis=0) * r.owner[...]).astype(BF16), r.fold[...])
    r.g1[...] = (nn(dzp, r.h1[...]) + place_row(30, gain_sum)).astype(BF16).reshape(32, 32, D)
    copy1, fold1 = folder(r.g1, r.r1, r.d1fold)
    sum1 = reducer(r.g1, (r.ava, r.avb, r.avp, r.avm, r.aua, r.aub, r.aup, r.aum), r.d1sem, 16, True)
    for du, dv in order:
        copy1(dv, du).start()
    sum2.end()
    total2 = r.g2[s].astype(F32)
    down2 = jnp.concatenate([total2[128 + 32 * k : 160 + 32 * k, 0:512] for k in range(3)], axis=1)
    for k in range(4):
        r.zs2[k] = total2[0:128, 144 * k : 144 * k + 144].astype(BF16)
        r.zd2[k] = down2[:, 384 * k : 384 * k + 384].astype(BF16)
    z2 = SumZ(b, s, [
        (r.zs2, (r.zs2p, r.zs2m, r.zs2a, r.zs2b)), (r.zd2, (r.zd2p, r.zd2m, r.zd2a, r.zd2b)),
    ], r.z2sem)
    z2.begin()
    g1v = dh1 * r.gain_s[0, 0:1, :]
    tg = r.mix_s[...] + inv1 * (g1v - n1 * (jnp.sum(g1v * n1, axis=-1, keepdims=True) * (1.0 / D)))
    for q in range(2):
        r.tgrad[q] = tg[PIECE * q : PIECE * (q + 1), :].T.astype(BF16)
    homeward(3, r.tgrad, r.tgrad_o, *begin)
    for offset in order:
        fold1(*offset)
        sum1.event(*offset)
        if offset == (0, 3):
            z2.middle()
    sum1.end()
    total1 = r.g1[s].astype(F32)
    for k in range(4):
        r.zs1[k] = total1[:, 144 * k : 144 * k + 144].astype(BF16)
    z1 = [
        rcopy(r.zs1.at[hop(b, d)], r.zs1l.at[d - 1], r.z1sem.at[0, d], r.z1sem.at[1, d], (hop(b, d), s))
        for d in (1, 2, 3)
    ]
    start(z1)
    raw2, down_sum = z2.result()
    r.raw_o[32:160, :] = raw2
    r.down_o[...] = down_sum
    total = r.zs1[b].astype(F32)
    for d, cp in enumerate(z1):
        cp.wait_recv()
        total += r.zs1l[d].astype(F32)
    r.raw_o[0:32, :] = total
    for offset in order:
        copy2(*offset).wait_send()
        copy1(*offset).wait_send()
    for part in (sumk, sum2, sum1, z2):
        part.finish()
    for cp in z1:
        cp.wait_send()
    for k, src, dst in ((2, r.mixed, r.mixed_o), (3, r.tgrad, r.tgrad_o)):
        homeward(k, src, dst, *ended)
        homeward_wait(k, src, dst)


def layer_call(shards, tokens, cot, tables, constants):
    any_ = pl.BlockSpec(memory_space=pl.ANY)
    vm = pl.BlockSpec(memory_space=pltpu.VMEM)
    return pl.pallas_call(
        layer_kernel,
        out_shape=(
            jax.ShapeDtypeStruct((2, D, PIECE), BF16),
            jax.ShapeDtypeStruct((2, D, PIECE), BF16),
            jax.ShapeDtypeStruct((160, 144), F32),
            jax.ShapeDtypeStruct((32, 384), F32),
        ),
        in_specs=[vm] * 8 + [any_] * 2 + [vm] * 4 + [any_] * 3,
        out_specs=(any_, any_, vm, vm),
        scratch_shapes=[pltpu.VMEM(shape, kind) for shape, kind in SCRATCH.values()]
        + [pltpu.SemaphoreType.DMA(shape) for shape in SEMS.values()],
        compiler_params=pltpu.CompilerParams(
            collective_id=0, has_side_effects=True, vmem_limit_bytes=VLIMIT
        ),
        name="decoder_layer",
    )(*shards, tokens, cot, *tables, *constants)


def finish_kernel(mixed, tgrad, raw, down, mixed_o, tgrad_o, g1, wq, wk, wv, wo, g2, wg, wu, wd):
    mixed_o[...] = mixed[...]
    tgrad_o[...] = tgrad[...]
    g1[...] = raw[30:31, 0:18]
    g2[...] = raw[50:51, 0:18]
    for at, ref in ((0, wq), (18, wk), (24, wv), (32, wo), (64, wg), (112, wu)):
        ref[...] = raw[at : at + ref.shape[0], :]
    wd[...] = down[0:18, :]


def finish_call(mixed, tgrad, raw, down):
    vm = pl.BlockSpec(memory_space=pltpu.VMEM)
    shapes = [(1, 18), (18, 144), (6, 144), (6, 144), (18, 144), (1, 18), (48, 144), (48, 144), (18, 384)]
    return pl.pallas_call(
        finish_kernel,
        out_shape=tuple([jax.ShapeDtypeStruct((2, D, PIECE), BF16)] * 2 + [jax.ShapeDtypeStruct(n, F32) for n in shapes]),
        in_specs=[vm] * 4,
        out_specs=(vm,) * 11,
        name="write_outputs",
    )(mixed, tgrad, raw, down)


def body(
    tokens, doc_lengths, first_gain, query_weight, key_matrix, value_matrix,
    output_weight, second_gain, gate_weight, up_weight, down_weight, cotangent,
):
    s = lax.axis_index("seq")
    c, p = s % 2, s // 2
    gains = jnp.stack([first_gain, second_gain])
    spread = jnp.asarray(spread_matrix())
    sprt = jnp.asarray(spread_matrix().T.copy())
    fold, owner = (jnp.asarray(m) for m in gain_matrix())

    lens = lax.dynamic_index_in_dim(doc_lengths[:, 0, :], c, 0, False)
    starts = [jnp.zeros((), jnp.int32), lens[0], lens[0] + lens[1]]
    at = jnp.arange(PIECE, dtype=jnp.int32)
    e = early_piece(p)
    spots = jnp.stack([e * PIECE + at, (31 - e) * PIECE + at])
    begins = jnp.where(spots >= starts[2], starts[2], jnp.where(spots >= starts[1], starts[1], 0))
    rates = THETA ** (-2.0 * jnp.arange(HD // 2, dtype=F32) / HD)
    angles = (spots - begins).reshape(T).astype(F32)[None, :] * rates[:, None]
    cos, sin = jnp.cos(angles), jnp.sin(angles)
    shards = [
        query_weight.T, key_matrix.T, value_matrix.T, output_weight.T,
        gate_weight.T, up_weight.T, down_weight.T, gains,
    ]
    turn = lambda a: jnp.swapaxes(a[:, 0], 1, 2)
    mixed, tgrad, raw, down = layer_call(
        shards, turn(tokens), turn(cotangent), (cos, sin, begins, owner), (spread, sprt, fold)
    )
    mixed, tgrad, g1, wq, wk, wv, wo, g2, wg, wu, wd = finish_call(mixed, tgrad, raw, down)
    back = lambda a: jnp.swapaxes(a, 1, 2)[:, None]
    return (
        back(mixed), back(tgrad), g1.reshape(18), wq.T, wk.T, wv.T, wo.T, g2.reshape(18), wg.T, wu.T, wd.T,
    )


def solution(mesh):
    weight = P("batch", "seq")
    rows = P(None, "batch", "seq", None)
    return jax.shard_map(
        body,
        mesh=mesh,
        in_specs=(
            rows, P(None, "batch", None), P("seq"), weight, weight, weight, weight,
            P("seq"), weight, weight, weight, rows,
        ),
        out_specs=(
            rows, rows, P("seq"), weight, weight, weight, weight,
            P("seq"), weight, weight, weight,
        ),
        check_vma=False,
    )
```
